128 devices in a mesh: lat: 8 (over z, y_lo), lon: 16 (over y_hi, x, core).
Axes of the slice: x: 4, y: 4 (y_hi: 2, y_lo: 2; y = y_hi * 2 + y_lo), z: 4, core: 2. Of those that a mesh axis runs over, the one named last changes fastest.
Arguments:
- tokens: float32 [2, 96, 576, 512], P(None, 'lat', 'lon'), may hold values from -6 to 6
- cotangent: float32 [2, 96, 576, 512], P(None, 'lat', 'lon'), may hold values from -6 to 6
- region_ids: int32 [2, 96, 576], P(None, 'lat', 'lon'), may hold values from 0 to 11, as said below
- w_qkv: bfloat16 [512, 1536], replicated, may hold values from -2 to 2
- w_proj: bfloat16 [512, 512], replicated, may hold values from -0.25 to 0.25
- w_in: bfloat16 [512, 2048], replicated, may hold values from -0.25 to 0.25
- w_out: bfloat16 [2048, 512], replicated, may hold values from -0.125 to 0.125
Outputs:
- grad_tokens: float32 [2, 96, 576, 512], P(None, 'lat', 'lon')
- grad_qkv: float32 [512, 1536], replicated
- grad_proj: float32 [512, 512], replicated
- grad_in: float32 [512, 2048], replicated
- grad_out: float32 [2048, 512], replicated
The draws below stay inside these ranges and needn't reach their ends.
Inputs may be any that keep to these rules, and one draw needn't show every extreme that they name: `region_ids`: a cell attends only to cells of its window with the same region id; ids are constant on contiguous strips of the shifted grid, changing where the roll wrapped over the band's latitude ends or over the levels, and at one column inside each block of 12 columns.
All inputs are finite; a program needn't handle non-finite values.
Results may differ from the reference program's by a relative error of at most 0.0152.
Values may be sent and summed in bfloat16 or wider, within the bound.
A program may use at most 192 MiB of HBM per device.

```python
import jax
import jax.numpy as jnp
from jax import lax

D = 512
HEADS = 16
FFN = 2048
LEVELS = 2
WLEV = 2
WLAT = 6
WLON = 12
NLAT = 96
NLON = 576


def draw_region_ids(key, part):
    key = jax.random.fold_in(key, 7)
    blocks_lon = NLON // WLON
    cuts = jax.random.randint(key, (blocks_lon,), 1, WLON)
    rows = jnp.arange(NLAT, dtype=jnp.int32)
    lat_part = jnp.where(rows >= NLAT - WLAT // 2, 2, jnp.where(rows >= NLAT - WLAT, 1, 0)).astype(jnp.int32)
    levels = jnp.arange(LEVELS, dtype=jnp.int32)
    lev_part = jnp.where(levels >= LEVELS - WLEV // 2, 1, 0).astype(jnp.int32)
    cols = jnp.arange(NLON, dtype=jnp.int32)
    offset = cols % WLON
    limit = jnp.repeat(cuts, WLON)
    cut_part = jnp.where(offset >= limit, 1, 0).astype(jnp.int32)
    result = 4 * lat_part[None, :, None] + 2 * lev_part[:, None, None] + cut_part[None, None, :]
    return result.astype(jnp.int32)


def draw_w_qkv(key, part):
    key = jax.random.fold_in(key, 11)
    key_one = jax.random.fold_in(key, 0)
    scale = D ** (-0.5)
    result = jax.random.truncated_normal(key_one, -4.0, 4.0, (D, 3 * D), jnp.float32) * scale
    result = jnp.clip(result, -1.95, 1.95)
    return result.astype(jnp.bfloat16)


def steps_of(rng, extent, cuts, low, largest):
    def one(axis_at, shards_of):
        steps = jax.random.uniform(jax.random.fold_in(jax.random.fold_in(rng, 6), axis_at), (shards_of,), jnp.float32, low / len(cuts), largest / len(cuts))
        return jnp.repeat(jnp.exp(steps), extent[axis_at] // shards_of).reshape((-1,) + (1,) * (len(extent) - axis_at - 1))

    gain = one(*cuts[0])
    for cut in cuts[1:]:
        gain = gain * one(*cut)
    return gain


def bell_draw(stream_key, shape, width, most, pieces=(), held_as=jnp.bfloat16):
    values = jax.random.normal(stream_key, shape, jnp.float32) * width
    if len(pieces) > 0:
        values = steps_of(stream_key, shape, pieces, -0.22, 0.18) * values
    return jnp.clip(values, min=-most, max=most).astype(held_as)


def setup_inputs(seed: int = 0) -> dict:
    streams_of = jax.random.split(jax.random.key(seed), 8)
    return {
        "tokens": bell_draw(streams_of[0], (LEVELS, NLAT, NLON, D), 1.0, 6.0, ((1, 8), (2, 16)), jnp.float32),
        "cotangent": bell_draw(streams_of[1], (LEVELS, NLAT, NLON, D), 1.0, 6.0, ((1, 8), (2, 16)), jnp.float32),
        "region_ids": draw_region_ids(jax.random.fold_in(streams_of[7], 71), 0),
        "w_qkv": draw_w_qkv(jax.random.fold_in(streams_of[7], 71), 0),
        "w_proj": bell_draw(streams_of[4], (D, D), D ** -0.5, 0.25),
        "w_in": bell_draw(streams_of[5], (D, FFN), D ** -0.5, 0.25),
        "w_out": bell_draw(streams_of[6], (FFN, D), FFN ** -0.5, 0.125),
    }


EPS = 1e-05
MASKED = -1000000000.0

def norm_rows(values):
    centred = values - lax.optimization_barrier(jnp.mean(values, axis=-1, keepdims=True))
    spread = lax.optimization_barrier(jnp.mean(centred * centred, axis=-1, keepdims=True))
    return centred * lax.rsqrt(spread + EPS)

def outer_sum(left_m, right_m):
    return lax.dot_general(left_m, right_m, (((0,), (0,)), ((), ())), preferred_element_type=jnp.float32)

def times_transposed(left_m, right_m):
    return lax.dot_general(left_m, right_m, (((1,), (1,)), ((), ())), preferred_element_type=jnp.float32)

def split_windows(lattice):
    levels, rows_lat, cols_lon, channels = lattice.shape
    blocks = lattice.reshape(levels, rows_lat // WLAT, WLAT, cols_lon // WLON, WLON, channels)
    blocks = blocks.transpose(1, 3, 0, 2, 4, 5)
    return blocks.reshape(-1, levels * WLAT * WLON, channels)

def merge_windows(blocks, rows_lat, cols_lon):
    channels = blocks.shape[-1]
    lattice = blocks.reshape(rows_lat // WLAT, cols_lon // WLON, WLEV, WLAT, WLON, channels)
    return lattice.transpose(2, 0, 3, 1, 4, 5).reshape(WLEV, rows_lat, cols_lon, channels)

def core_forward(packed, region):
    win_count, win_size, triple = packed.shape
    features = triple // 3
    head_dim = features // HEADS
    heads_all = packed.reshape(win_count, win_size, 3, HEADS, head_dim)
    queries = heads_all[:, :, 0]
    keys_all = heads_all[:, :, 1]
    values_all = heads_all[:, :, 2]
    scores = jnp.einsum('wqhd,wkhd->whqk', queries.astype(jnp.float32), keys_all.astype(jnp.float32)) * head_dim ** (-0.5)
    allowed = region[:, None, :, None] == region[:, None, None, :]
    scores = jnp.where(allowed, scores, MASKED)
    soft = jax.nn.softmax(scores, axis=-1)
    attn_probs = soft.astype(jnp.bfloat16)
    mixed_heads = jnp.einsum('whqk,wkhd->wqhd', attn_probs.astype(jnp.float32), values_all.astype(jnp.float32))
    mixed_heads = mixed_heads.reshape(win_count, win_size, features).astype(jnp.bfloat16)
    return (mixed_heads, (queries, keys_all, values_all, soft, attn_probs, allowed))

def core_backward(saved, d_mixed):
    queries, keys_all, values_all, soft, attn_probs, allowed = saved
    win_count, win_size, heads_n, head_dim = queries.shape
    d_heads = d_mixed.reshape(win_count, win_size, heads_n, head_dim).astype(jnp.float32)
    d_probs = jnp.einsum('wqhd,wkhd->whqk', d_heads, values_all.astype(jnp.float32)).astype(jnp.bfloat16)
    d_probs = lax.optimization_barrier(d_probs).astype(jnp.float32)
    d_values = jnp.einsum('whqk,wqhd->wkhd', attn_probs.astype(jnp.float32), d_heads)
    total = lax.optimization_barrier(jnp.sum(d_probs * soft, axis=-1, keepdims=True))
    d_scores = jnp.where(allowed, soft * (d_probs - total), 0.0) * head_dim ** (-0.5)
    d_scores = d_scores.astype(jnp.bfloat16).astype(jnp.float32)
    d_queries = jnp.einsum('whqk,wkhd->wqhd', d_scores, keys_all.astype(jnp.float32))
    d_keys = jnp.einsum('whqk,wqhd->wkhd', d_scores, queries.astype(jnp.float32))
    d_packed = jnp.stack([d_queries, d_keys, d_values], axis=2)
    return d_packed.reshape(win_count, win_size, -1).astype(jnp.bfloat16)

def attention_forward(normed, region_grid, w_qkv, w_proj):
    rows_lat, cols_lon = (normed.shape[1], normed.shape[2])
    win_in = split_windows(normed)
    region = split_windows(region_grid[..., None])[..., 0]
    flat_in = win_in.reshape(-1, win_in.shape[-1])
    packed = jnp.dot(flat_in, w_qkv, preferred_element_type=jnp.float32).astype(jnp.bfloat16)
    packed = packed.reshape(win_in.shape[0], win_in.shape[1], -1)
    mixed_heads, saved = core_forward(packed, region)
    flat_mixed = mixed_heads.reshape(-1, mixed_heads.shape[-1])
    attended = jnp.dot(flat_mixed, w_proj, preferred_element_type=jnp.float32).astype(jnp.bfloat16)
    attended = merge_windows(attended.reshape(mixed_heads.shape), rows_lat, cols_lon)
    return (attended, (flat_in, packed.shape, flat_mixed, saved))

def attention_backward(kept_attn, d_attended, w_qkv, w_proj):
    flat_in, packed_shape, flat_mixed, saved = kept_attn
    rows_lat, cols_lon = (d_attended.shape[1], d_attended.shape[2])
    d_flat = split_windows(d_attended).reshape(flat_mixed.shape)
    grad_proj = outer_sum(flat_mixed, d_flat)
    d_mixed = times_transposed(d_flat, w_proj).astype(jnp.bfloat16)
    d_packed = core_backward(saved, d_mixed)
    flat_packed = d_packed.reshape(-1, d_packed.shape[-1])
    grad_qkv = outer_sum(flat_in, flat_packed)
    d_normed = times_transposed(flat_packed, w_qkv)
    d_normed = merge_windows(d_normed.reshape(packed_shape[0], packed_shape[1], -1), rows_lat, cols_lon)
    return (d_normed, grad_qkv, grad_proj)

def mlp_backward(middle, cot_rows, w_in, w_out):
    normed_mid, norm_back = jax.vjp(norm_rows, middle)
    normed_half = normed_mid.astype(jnp.bfloat16)
    pre_act = jnp.dot(normed_half, w_in, preferred_element_type=jnp.float32)
    activated, gelu_back = jax.vjp(jax.nn.gelu, pre_act)
    activated = activated.astype(jnp.bfloat16)
    cot_half = cot_rows.astype(jnp.bfloat16)
    grad_out = outer_sum(activated, cot_half)
    d_act = times_transposed(cot_half, w_out)
    d_pre = gelu_back(d_act)[0].astype(jnp.bfloat16)
    grad_in = outer_sum(normed_half, d_pre)
    d_normed = times_transposed(d_pre, w_in)
    d_mid = cot_rows + norm_back(d_normed)[0]
    return (d_mid, grad_in, grad_out)

def reference(tokens, cotangent, region_ids, w_qkv, w_proj, w_in, w_out):
    offsets = (-(WLEV // 2), -(WLAT // 2), -(WLON // 2))
    shifted = jnp.roll(tokens, offsets, axis=(0, 1, 2))
    shifted_cot = jnp.roll(cotangent, offsets, axis=(0, 1, 2))
    normed_full, norm_back = jax.vjp(norm_rows, shifted)
    attended, kept_attn = attention_forward(normed_full.astype(jnp.bfloat16), region_ids, w_qkv, w_proj)
    middle = shifted + attended.astype(jnp.float32)
    features = tokens.shape[-1]
    d_mid, grad_in, grad_out = mlp_backward(middle.reshape(-1, features), shifted_cot.reshape(-1, features), w_in, w_out)
    d_mid = d_mid.reshape(middle.shape)
    d_normed, grad_qkv, grad_proj = attention_backward(kept_attn, d_mid.astype(jnp.bfloat16), w_qkv, w_proj)
    d_shifted = d_mid + norm_back(d_normed)[0]
    grad_tokens = jnp.roll(d_shifted, (WLEV // 2, WLAT // 2, WLON // 2), axis=(0, 1, 2))
    return (grad_tokens, grad_qkv, grad_proj, grad_in, grad_out)
```

```python
import functools

import jax
import jax.numpy as jnp
from jax import lax
from jax.experimental import pallas as pl
from jax.experimental.pallas import tpu as pltpu
from jax.sharding import PartitionSpec as P

D = 512
HEADS = 16
HEAD_DIM = D // HEADS
FFN = 2048
WLEV = 2
WLAT = 6
WLON = 12
WIN = WLEV * WLAT * WLON
GROUP = 8
LANES = GROUP * HEAD_DIM
GROUPS = HEADS // GROUP
SPREAD = GROUP * WIN
HALF_LAT = WLAT // 2
HALF_LON = WLON // 2
EPS = 1e-05
MASKED = -1e10
SCALE = HEAD_DIM ** -0.5
LOG2E = 1.4426950408889634
GELU_A = 0.7978845608028654
GELU_B = 0.044715
F32 = jnp.float32
BF16 = jnp.bfloat16


def nn(a, b):
    return lax.dot_general(a, b, (((1,), (0,)), ((), ())), preferred_element_type=F32)


def nt(a, b):
    return lax.dot_general(a, b, (((1,), (1,)), ((), ())), preferred_element_type=F32)


def norm_parts(v):
    centred = v - jnp.mean(v, axis=-1, keepdims=True)
    r = lax.rsqrt(jnp.mean(centred * centred, axis=-1, keepdims=True) + EPS)
    return centred * r, r


def norm_back(unit, r, g):
    return r * (g - jnp.mean(g, axis=-1, keepdims=True) - unit * jnp.mean(g * unit, axis=-1, keepdims=True))


def spread_heads(v):
    lane_head = lax.broadcasted_iota(jnp.int32, v.shape, 1) // HEAD_DIM
    zero = jnp.zeros_like(v)
    return jnp.concatenate([jnp.where(lane_head == h, v, zero) for h in range(GROUP)], axis=0)


def own_blocks(full):
    return jnp.concatenate(
        [full[HEAD_DIM * h : HEAD_DIM * (h + 1), WIN * h : WIN * (h + 1)] for h in range(GROUP)], axis=0
    )


BLOCKS = 12
OUT_BLOCKS = (0, 2, 4, 6)
IN_BLOCKS = (1, 3, 5, 7)
PROJ_BLOCK = 8
QKV_BLOCKS = (9, 10, 11)
ROUTES = (
    ("xyz", 1), ("yzx", 1), ("zxy", 1), ("xyz", 3), ("yzx", 3), ("zxy", 3),
    ("xyz", 1), ("yzx", 1), ("zxy", 1),
    ("xyz", 0), ("yzx", 0), ("zxy", 0),
)
SLOTS = 17


class Place:
    def __init__(self):
        lat, lon = lax.axis_index("lat"), lax.axis_index("lon")
        self.core = lon % 2
        self.at = {"x": (lon // 2) % 4, "y": (lon // 8) * 2 + lat % 2, "z": lat // 2}

    def mesh_id(self, at, core):
        return (at["z"] * 2 + at["y"] % 2, (at["y"] // 2) * 8 + at["x"] * 2 + core)

    def sibling(self):
        return self.mesh_id(self.at, 1 - self.core)

    def along(self, axis, step):
        at = dict(self.at)
        at[axis] = (at[axis] + step) % 4
        return self.mesh_id(at, self.core), at[axis]

    def across(self, axis, kind):
        at, c = dict(self.at), self.at[axis]
        at[axis] = c + 1 - 2 * (c % 2) if kind == 1 else 3 - c
        bit = ((c + 1) // 2) % 2 if kind == 1 else c // 2
        return self.mesh_id(at, self.core), bit


def greet(place, others=()):
    barrier = pltpu.get_barrier_semaphore()
    partners = [place.sibling()] + [place.along(a, s)[0] for a in "xyz" for s in (1, 2, 3)] + list(others)
    for partner in partners:
        pl.semaphore_signal(barrier, inc=1, device_id=partner, device_id_type=pl.DeviceIdType.MESH)
    pl.semaphore_wait(barrier, len(partners))


class Sum:
    def __init__(self, place, u, g, done, got, send, recv):
        self.u, self.g, self.done, self.got, self.send, self.recv = u, g, done, got, send, recv
        self.stage, self.slots, self.copies = 0, 0, []
        order, first = ROUTES[u]
        self.steps, base, rows = [], 0, D

        def halve(name, target, bit, base, rows):
            rows //= 2
            self.steps.append((name, [(target, base + (1 - bit) * rows)], base + bit * rows, rows))
            return base + bit * rows, rows

        def quarter(name, axis, base, rows):
            rows //= 4
            peers = [place.along(axis, step) for step in (1, 2, 3)]
            self.steps.append((name, [(t, base + c * rows) for t, c in peers], base + place.at[axis] * rows, rows))
            return base + place.at[axis] * rows, rows

        base, rows = halve("core", place.sibling(), place.core, base, rows)
        if first:
            base, rows = halve("near", *place.across(order[0], first), base, rows)
            base, rows = halve("far", *place.across(order[0], 4 - first), base, rows)
        else:
            base, rows = quarter("axis", order[0], base, rows)
        base, rows = quarter("second", order[1], base, rows)
        peers = [place.along(order[2], step)[0] for step in (1, 2, 3)]
        self.swap = (peers, place.at[order[2]], base, rows)
        self.last = 2 * len(self.steps) + 1

    def part(self, ref, base, rows):
        return ref.at[self.u, pl.ds(pl.multiple_of(base, rows), rows), :]

    def copy(self, src, dst, target):
        slot = self.slots
        self.slots += 1
        one = pltpu.make_async_remote_copy(
            src_ref=src, dst_ref=dst, send_sem=self.send.at[self.u, slot], recv_sem=self.recv.at[self.u, slot],
            device_id=target, device_id_type=pl.DeviceIdType.MESH,
        )
        one.start()
        self.copies.append(one)

    def landing(self, name, i):
        if name == "axis":
            return self.got[name].at[i, self.u - QKV_BLOCKS[0]]
        return self.got[name].at[i, self.u]

    def advance(self):
        n, stage = len(self.steps), self.stage
        self.stage += 1
        for one in self.copies:
            one.wait()
        self.copies = []
        if 1 <= stage <= n:
            name, targets, base, rows = self.steps[stage - 1]
            mine = self.part(self.g, base, rows)
            total = mine[...].astype(F32)
            for i in range(len(targets)):
                total = total + self.landing(name, i)[...].astype(F32)
            mine[...] = total.astype(BF16)
        if stage == n + 1:
            _, _, base, rows = self.swap
            four = [self.got["swap"][c, self.u].astype(F32) for c in range(4)]
            self.part(self.done, base, rows)[...] = ((four[0] + four[1]) + (four[2] + four[3])).astype(BF16)
        if stage < n:
            name, targets, _, rows = self.steps[stage]
            for i, (target, base) in enumerate(targets):
                self.copy(self.part(self.g, base, rows), self.landing(name, i), target)
        elif stage == n:
            targets, at, base, rows = self.swap
            mine = self.part(self.g, base, rows)
            self.got["swap"][at, self.u] = mine[...]
            for target in targets:
                self.copy(mine, self.got["swap"].at[at, self.u], target)
        elif stage <= 2 * n:
            _, targets, base, rows = self.steps[2 * n - stage]
            mine = self.part(self.done, base, rows)
            for target, _ in targets:
                self.copy(mine, mine, target)


LANDINGS = (
    ("core", (1, BLOCKS, D // 2, D)),
    ("near", (1, BLOCKS - 3, D // 4, D)),
    ("far", (1, BLOCKS - 3, D // 8, D)),
    ("axis", (3, 3, D // 8, D)),
    ("second", (3, BLOCKS, D // 32, D)),
    ("swap", (4, BLOCKS, D // 32, D)),
)


def sum_scratch():
    return [pltpu.VMEM(shape, BF16) for _, shape in LANDINGS] + [pltpu.SemaphoreType.DMA((BLOCKS, SLOTS))] * 2


def unpack_kernel(g_ref, tok_ref, out_ref, in_ref, qkv_ref, proj_ref, tok_out, half, full, got, put, whole):
    def target(u):
        if u == PROJ_BLOCK:
            return proj_ref
        if u in OUT_BLOCKS:
            return out_ref.at[pl.ds(D * OUT_BLOCKS.index(u), D), :]
        if u in IN_BLOCKS:
            return in_ref.at[:, pl.ds(D * IN_BLOCKS.index(u), D)]
        return qkv_ref.at[:, pl.ds(D * QKV_BLOCKS.index(u), D)]

    ins = [pltpu.make_async_copy(g_ref.at[u], half.at[u], got.at[u]) for u in range(BLOCKS)]
    outs = [pltpu.make_async_copy(full.at[u], target(u), put.at[u]) for u in range(BLOCKS)]
    through = pltpu.make_async_copy(tok_ref, tok_out, whole)
    for one in ins:
        one.start()
    through.start()
    for u in range(BLOCKS):
        ins[u].wait()
        full[u] = half[u].astype(F32)
        outs[u].start()
    for one in outs:
        one.wait()
    through.wait()


def unpack_call(grads, grad_tokens):
    anywhere = pl.BlockSpec(memory_space=pl.ANY)
    return pl.pallas_call(
        unpack_kernel,
        out_shape=tuple(jax.ShapeDtypeStruct(s, F32) for s in ((FFN, D), (D, FFN), (D, 3 * D), (D, D), grad_tokens.shape)),
        in_specs=[anywhere] * 2,
        out_specs=(anywhere,) * 5,
        scratch_shapes=[
            pltpu.VMEM((BLOCKS, D, D), BF16),
            pltpu.VMEM((BLOCKS, D, D), F32),
            pltpu.SemaphoreType.DMA((BLOCKS,)),
            pltpu.SemaphoreType.DMA((BLOCKS,)),
            pltpu.SemaphoreType.DMA,
        ],
        compiler_params=pltpu.CompilerParams(vmem_limit_bytes=40 * 1024 * 1024),
        name="unpack",
    )(grads, grad_tokens)


LAT_ROWS, LON_ROWS = 32, 16
LAT_AT, LON_AT, DIAG_AT, HALO_ROWS = 0, 192, 336, 384
WINDOWS = 6
WIDE = 3
OWN_ROWS = 9
OWN_COLS = 30
HALO_PARTS = ((LAT_AT, LON_AT), (LON_AT, DIAG_AT), (DIAG_AT, HALO_ROWS))


def cell(level, row, wide, col=0):
    return ((row // WLAT) * WIDE + wide) * WIN + level * (WLAT * WLON) + (row % WLAT) * WLON + col


def padded(pieces, rows):
    have = sum(p.shape[0] for p in pieces)
    return jnp.concatenate(pieces + [jnp.zeros((rows - have, D), F32)], axis=0).astype(BF16)


def pack_ahead(src, dst):
    for level in range(WLEV):
        for row in range(HALF_LAT):
            at = LAT_AT + (level * HALF_LAT + row) * LAT_ROWS
            dst[at : at + LAT_ROWS, :] = padded([src[level, row, HALF_LON : HALF_LON + OWN_COLS, :]], LAT_ROWS)
    for row in range(HALF_LAT + OWN_ROWS):
        at = DIAG_AT + row * LON_ROWS if row < HALF_LAT else LON_AT + (row - HALF_LAT) * LON_ROWS
        dst[at : at + LON_ROWS, :] = padded([src[level, row, :HALF_LON, :] for level in range(WLEV)], LON_ROWS)


def place_strip(flat, level, row, strip):
    flat[cell(level, row, 0) : cell(level, row, 0) + WLON, :] = strip[:WLON]
    flat[cell(level, row, 1) : cell(level, row, 1) + WLON, :] = strip[WLON : 2 * WLON]
    flat[cell(level, row, 2) : cell(level, row, 2) + HALF_LON, :] = strip[2 * WLON : OWN_COLS]


def take_strip(flat, level, row):
    return [
        flat[cell(level, row, 0) : cell(level, row, 0) + WLON, :],
        flat[cell(level, row, 1) : cell(level, row, 1) + WLON, :],
        flat[cell(level, row, 2) : cell(level, row, 2) + HALF_LON, :],
    ]


def place_own(src, flat):
    for level in range(WLEV):
        for row in range(OWN_ROWS):
            place_strip(flat, level, row, src[level, row + HALF_LAT, HALF_LON : HALF_LON + OWN_COLS, :])


def place_halo(got, flat):
    for level in range(WLEV):
        for row in range(HALF_LAT):
            at = LAT_AT + (level * HALF_LAT + row) * LAT_ROWS
            place_strip(flat, level, OWN_ROWS + row, got[at : at + LAT_ROWS, :].astype(F32))
    for row in range(OWN_ROWS + HALF_LAT):
        at = LON_AT + row * LON_ROWS if row < OWN_ROWS else DIAG_AT + (row - OWN_ROWS) * LON_ROWS
        both = got[at : at + LON_ROWS, :].astype(F32)
        for level in range(WLEV):
            to = cell(level, row, 2, HALF_LON)
            flat[to : to + HALF_LON, :] = both[HALF_LON * level : HALF_LON * (level + 1)]


def pack_back(flat, dst):
    for level in range(WLEV):
        for row in range(HALF_LAT):
            at = LAT_AT + (level * HALF_LAT + row) * LAT_ROWS
            dst[at : at + LAT_ROWS, :] = padded(take_strip(flat, level, OWN_ROWS + row), LAT_ROWS)
    for row in range(OWN_ROWS + HALF_LAT):
        at = LON_AT + row * LON_ROWS if row < OWN_ROWS else DIAG_AT + (row - OWN_ROWS) * LON_ROWS
        ends = [cell(level, row, 2, HALF_LON) for level in range(WLEV)]
        dst[at : at + LON_ROWS, :] = padded([flat[e : e + HALF_LON, :] for e in ends], LON_ROWS)


def return_own(flat, out):
    for level in range(WLEV):
        for row in range(OWN_ROWS):
            out[level, row + HALF_LAT, HALF_LON : HALF_LON + OWN_COLS, :] = jnp.concatenate(
                take_strip(flat, level, row), axis=0
            )


def return_halo(got, out):
    for row in range(HALF_LAT + OWN_ROWS):
        at = DIAG_AT + row * LON_ROWS if row < HALF_LAT else LON_AT + (row - HALF_LAT) * LON_ROWS
        both = got[at : at + LON_ROWS, :].astype(F32)
        for level in range(WLEV):
            out[level, row, :HALF_LON, :] = both[HALF_LON * level : HALF_LON * (level + 1)]
    for level in range(WLEV):
        for row in range(HALF_LAT):
            at = LAT_AT + (level * HALF_LAT + row) * LAT_ROWS
            out[level, row, HALF_LON : HALF_LON + OWN_COLS, :] = got[at : at + LAT_ROWS, :].astype(F32)[:OWN_COLS]


AFTER_CHUNK = ((0, 1), (2, 3), (0, 1, 4, 5), (2, 3, 6, 7))
AFTER_PROJ = (8, 0, 1, 4, 5)
AFTER_WINDOW = ((2, 3, 6, 7), (8,), (0, 1, 4, 5), (2, 3, 6, 7), (8,), (0, 1, 4, 5))
AFTER_QKV = (2, 3, 6, 7, 8)
AFTER_INPUT = (0, 1, 4, 5)
AFTER_NORM = (9, 10, 11, 2, 3, 6, 7, 8)


def block_kernel(
    tokens, cotangent, region, wqkv, wproj, win, wout,
    out_ref, done_ref,
    cot_ref, x_ref, c_ref, wqkv_ref, wproj_ref, win_ref, wout_ref,
    normed, packed, probs, mixed, mid, nmid, dnm, g_ref,
    halo_out, halo_in, back_out, back_in, load_sem, halo_sem, *landings_and_sems,
):
    place = Place()
    *landings, send, recv = landings_and_sems
    got = {name: ref for (name, _), ref in zip(LANDINGS, landings)}
    sums = [Sum(place, u, g_ref, done_ref, got, send, recv) for u in range(BLOCKS)]

    def tick(*blocks):
        for u in blocks:
            sums[u].advance()

    loads = [
        pltpu.make_async_copy(src, dst, load_sem.at[i])
        for i, (src, dst) in enumerate(
            ((tokens, out_ref), (cotangent, cot_ref), (wqkv, wqkv_ref), (wproj, wproj_ref), (win, win_ref), (wout, wout_ref))
        )
    ]
    for one in loads:
        one.start()

    lat, lon = lax.axis_index("lat"), lax.axis_index("lon")
    lats, lons = lax.axis_size("lat"), lax.axis_size("lon")
    up, down = lax.rem(lat + lats - 1, lats), lax.rem(lat + 1, lats)
    left, right = lax.rem(lon + lons - 1, lons), lax.rem(lon + 1, lons)
    ahead = ((up, lon), (lat, left), (up, left))
    back = ((down, lon), (lat, right), (down, right))
    greet(place, ahead + back)

    def exchange(src, dst, targets, at):
        copies = []
        for i, (lo, hi) in enumerate(HALO_PARTS):
            one = pltpu.make_async_remote_copy(
                src_ref=src.at[lo:hi], dst_ref=dst.at[lo:hi],
                send_sem=halo_sem.at[0, at + i], recv_sem=halo_sem.at[1, at + i],
                device_id=targets[i], device_id_type=pl.DeviceIdType.MESH,
            )
            one.start()
            copies.append(one)
        return copies

    loads[0].wait()
    pack_ahead(out_ref, halo_out.at[0])
    token_halo = exchange(halo_out.at[0], halo_in.at[0], ahead, 0)
    loads[1].wait()
    pack_ahead(cot_ref, halo_out.at[1])
    cot_halo = exchange(halo_out.at[1], halo_in.at[1], ahead, 3)
    place_own(out_ref, x_ref)

    rows_of = lambda w: pl.ds(pl.multiple_of(w * WIN, WIN), WIN)

    def attention_forward(first, last):
        @pl.loop(first, last)
        def _(w):
            unit, _ = norm_parts(x_ref[rows_of(w), :])
            normed[rows_of(w), :] = unit.astype(BF16)

        if first == 0:
            loads[2].wait()
        rows = slice(first * WIN, last * WIN)
        for j in range(3):
            cols = slice(D * j, D * (j + 1))
            packed[rows, cols] = nn(normed[rows, :], wqkv_ref[:, cols]).astype(BF16)

        @pl.loop(first, last)
        def _(w):
            rows = rows_of(w)
            line = region[w]
            allowed = jnp.broadcast_to(line, (WIN, WIN)).T[:, :1] == jnp.concatenate([line] * GROUP, axis=1)
            for g in range(GROUPS):
                lo = LANES * g
                q = packed[rows, lo : lo + LANES]
                k = packed[rows, D + lo : D + lo + LANES]
                v = packed[rows, 2 * D + lo : 2 * D + lo + LANES]
                s = jnp.where(allowed, nt(k, spread_heads(q)), MASKED)
                e = jnp.exp2((s - jnp.max(s, axis=0, keepdims=True)) * (SCALE * LOG2E))
                p = (e * (1.0 / jnp.sum(e, axis=0, keepdims=True))).astype(BF16)
                probs[w * GROUPS + g] = p
                mixed[rows, lo : lo + LANES] = own_blocks(nn(v.T, p)).T.astype(BF16)

    attention_forward(0, 2)
    for one in token_halo:
        one.wait()
    place_halo(halo_in.at[0], x_ref)
    attention_forward(2, WINDOWS)

    loads[3].wait()
    mid[...] = nn(mixed[...], wproj_ref[...]).astype(BF16).astype(F32)

    @pl.loop(0, WINDOWS)
    def _(w):
        rows = rows_of(w)
        middle = x_ref[rows, :] + mid[rows, :]
        mid[rows, :] = middle
        nmid[rows, :] = norm_parts(middle)[0].astype(BF16)

    place_own(cot_ref, c_ref)
    for one in cot_halo:
        one.wait()
    place_halo(halo_in.at[1], c_ref)
    loads[4].wait()
    loads[5].wait()

    nmid_t = nmid[...].T
    for j in range(FFN // D):
        cols = slice(D * j, D * (j + 1))
        cot = c_ref[...].astype(BF16)
        u = nn(nmid[...], win_ref[:, cols])
        da = nt(cot, wout_ref[cols, :])
        square = u * u
        t = jnp.tanh(u * (GELU_A + (GELU_A * GELU_B) * square))
        half = 0.5 + 0.5 * t
        act = (u * half).astype(BF16)
        slope = half + u * (0.5 - 0.5 * t * t) * (GELU_A + (3 * GELU_A * GELU_B) * square)
        dpre = (slope * da).astype(BF16)
        g_ref[OUT_BLOCKS[j]] = nn(act.T, cot).astype(BF16)
        g_ref[IN_BLOCKS[j]] = nn(nmid_t, dpre).astype(BF16)
        part = nt(dpre, win_ref[:, cols])
        if j == 0:
            dnm[...] = part
        else:
            dnm[...] += part
        tick(*AFTER_CHUNK[j])

    @pl.loop(0, WINDOWS)
    def _(w):
        rows = rows_of(w)
        unit, r = norm_parts(mid[rows, :])
        d_mid = c_ref[rows, :] + norm_back(unit, r, dnm[rows, :])
        c_ref[rows, :] = d_mid
        nmid[rows, :] = d_mid.astype(BF16)

    g_ref[PROJ_BLOCK] = nn(mixed[...].T, nmid[...]).astype(BF16)
    tick(*AFTER_PROJ)
    mixed[...] = nt(nmid[...], wproj_ref[...]).astype(BF16)

    for w in range(WINDOWS):

        @pl.loop(w, w + 1)
        def _(w):
            rows = rows_of(w)
            for g in range(GROUPS):
                lo = LANES * g
                q = spread_heads(packed[rows, lo : lo + LANES])
                k = packed[rows, D + lo : D + lo + LANES]
                v = packed[rows, 2 * D + lo : 2 * D + lo + LANES]
                do = spread_heads(mixed[rows, lo : lo + LANES])
                p = probs[w * GROUPS + g]
                dp = nt(v, do)
                pf = p.astype(F32)
                total = jnp.sum(dp * pf, axis=0, keepdims=True)
                ds = (pf * (dp - total) * SCALE).astype(BF16)
                packed[rows, lo : lo + LANES] = own_blocks(nn(k.T, ds)).T.astype(BF16)
                packed[rows, D + lo : D + lo + LANES] = nn(ds, q).astype(BF16)
                packed[rows, 2 * D + lo : 2 * D + lo + LANES] = nn(p, do).astype(BF16)

        tick(*AFTER_WINDOW[w])

    normed_t = normed[...].T
    for j in range(3):
        g_ref[QKV_BLOCKS[j]] = nn(normed_t, packed[:, D * j : D * (j + 1)]).astype(BF16)
        tick(QKV_BLOCKS[j])
    tick(*AFTER_QKV)
    for j in range(3):
        cols = slice(D * j, D * (j + 1))
        part = nt(packed[:, cols], wqkv_ref[:, cols])
        if j == 0:
            dnm[...] = part
        else:
            dnm[...] += part
    tick(*AFTER_INPUT)

    @pl.loop(0, WINDOWS)
    def _(w):
        rows = rows_of(w)
        unit, r = norm_parts(x_ref[rows, :])
        c_ref[rows, :] = c_ref[rows, :] + norm_back(unit, r, dnm[rows, :])

    tick(*AFTER_NORM)
    pack_back(c_ref, back_out)
    grad_halo = exchange(back_out, back_in, back, 6)
    return_own(c_ref, out_ref)

    rounds = 0
    while any(one.stage <= one.last for one in sums):
        tick(*(u for u in (9, 10, 11, 0, 1, 2, 3, 4, 5, 6, 7, 8) if sums[u].stage <= sums[u].last))
        rounds += 1
        if rounds == 2:
            for one in grad_halo:
                one.wait()
            return_halo(back_in, out_ref)


def block_call(tokens, cotangent, region, w_qkv, w_proj, w_in, w_out):
    anywhere, vmem = pl.BlockSpec(memory_space=pl.ANY), pl.BlockSpec(memory_space=pltpu.VMEM)
    cells = WINDOWS * WIN
    return pl.pallas_call(
        block_kernel,
        out_shape=(jax.ShapeDtypeStruct(tokens.shape, F32), jax.ShapeDtypeStruct((BLOCKS, D, D), BF16)),
        in_specs=[anywhere, anywhere, vmem] + [anywhere] * 4,
        out_specs=(vmem, vmem),
        scratch_shapes=[
            pltpu.VMEM(tokens.shape, F32),
            pltpu.VMEM((cells, D), F32),
            pltpu.VMEM((cells, D), F32),
            pltpu.VMEM(w_qkv.shape, BF16),
            pltpu.VMEM(w_proj.shape, BF16),
            pltpu.VMEM(w_in.shape, BF16),
            pltpu.VMEM(w_out.shape, BF16),
            pltpu.VMEM((cells, D), BF16),
            pltpu.VMEM((cells, 3 * D), BF16),
            pltpu.VMEM((WINDOWS * GROUPS, WIN, SPREAD), BF16),
            pltpu.VMEM((cells, D), BF16),
            pltpu.VMEM((cells, D), F32),
            pltpu.VMEM((cells, D), BF16),
            pltpu.VMEM((cells, D), F32),
            pltpu.VMEM((BLOCKS, D, D), BF16),
            pltpu.VMEM((2, HALO_ROWS, D), BF16),
            pltpu.VMEM((2, HALO_ROWS, D), BF16),
            pltpu.VMEM((HALO_ROWS, D), BF16),
            pltpu.VMEM((HALO_ROWS, D), BF16),
            pltpu.SemaphoreType.DMA((6,)),
            pltpu.SemaphoreType.DMA((2, 9)),
        ]
        + sum_scratch(),
        compiler_params=pltpu.CompilerParams(
            collective_id=0, has_side_effects=True, vmem_limit_bytes=63 * 1024 * 1024
        ),
        cost_estimate=pl.CostEstimate(flops=16 * 10**9, bytes_accessed=24 * 10**6, transcendentals=4 * 10**6),
        name="block",
    )(tokens, cotangent, region, w_qkv, w_proj, w_in, w_out)


def local(tokens, cotangent, region_ids, w_qkv, w_proj, w_in, w_out):
    levels, rows_lat, cols_lon = region_ids.shape
    region = region_ids[::-1].reshape(levels, rows_lat // WLAT, WLAT, cols_lon // WLON, WLON)
    region = region.transpose(1, 3, 0, 2, 4).reshape(-1, 1, WIN).astype(F32)
    grad_tokens, grads = block_call(tokens, cotangent, region, w_qkv, w_proj, w_in, w_out)
    grad_out, grad_in, grad_qkv, grad_proj, grad_tokens = unpack_call(grads, grad_tokens)
    return grad_tokens, grad_qkv, grad_proj, grad_in, grad_out


def solution(mesh):
    grid = P(None, "lat", "lon", None)
    in_specs = (grid, grid, P(None, "lat", "lon"), P(), P(), P(), P())
    out_specs = (grid, P(), P(), P(), P())
    return jax.shard_map(local, mesh=mesh, in_specs=in_specs, out_specs=out_specs, check_vma=False)
```

```python
import functools

import jax
import jax.numpy as jnp
from jax import lax
from jax.experimental import pallas as pl
from jax.experimental.pallas import tpu as pltpu
from jax.sharding import PartitionSpec as P

D = 512
HEADS = 16
HEAD_DIM = D // HEADS
FFN = 2048
WLEV = 2
WLAT = 6
WLON = 12
WIN = WLEV * WLAT * WLON
GROUP = 8
LANES = GROUP * HEAD_DIM
GROUPS = HEADS // GROUP
SPREAD = GROUP * WIN
HALF_LAT = WLAT // 2
HALF_LON = WLON // 2
EPS = 1e-05
MASKED = -1e10
SCALE = HEAD_DIM ** -0.5
LOG2E = 1.4426950408889634
GELU_A = 0.7978845608028654
GELU_B = 0.044715
F32 = jnp.float32
BF16 = jnp.bfloat16


def nn(a, b):
    return lax.dot_general(a, b, (((1,), (0,)), ((), ())), preferred_element_type=F32)


def nt(a, b):
    return lax.dot_general(a, b, (((1,), (1,)), ((), ())), preferred_element_type=F32)


def norm_parts(v):
    centred = v - jnp.mean(v, axis=-1, keepdims=True)
    r = lax.rsqrt(jnp.mean(centred * centred, axis=-1, keepdims=True) + EPS)
    return centred * r, r


def norm_back(unit, r, g):
    return r * (g - jnp.mean(g, axis=-1, keepdims=True) - unit * jnp.mean(g * unit, axis=-1, keepdims=True))


def spread_heads(v):
    lane_head = lax.broadcasted_iota(jnp.int32, v.shape, 1) // HEAD_DIM
    zero = jnp.zeros_like(v)
    return jnp.concatenate([jnp.where(lane_head == h, v, zero) for h in range(GROUP)], axis=0)


def own_blocks(full):
    return jnp.concatenate(
        [full[HEAD_DIM * h : HEAD_DIM * (h + 1), WIN * h : WIN * (h + 1)] for h in range(GROUP)], axis=0
    )


BLOCKS = 12
OUT_BLOCKS = (0, 2, 4, 6)
IN_BLOCKS = (1, 3, 5, 7)
PROJ_BLOCK = 8
QKV_BLOCKS = (9, 10, 11)
ROUTES = (
    ("xyz", 1), ("yzx", 1), ("zxy", 1), ("xyz", 3), ("yzx", 3), ("zxy", 3),
    ("xyz", 1), ("yzx", 1), ("zxy", 1),
    ("xyz", 0), ("yzx", 0), ("zxy", 0),
)
SLOTS = 17


class Place:
    def __init__(self):
        lat, lon = lax.axis_index("lat"), lax.axis_index("lon")
        self.core = lon % 2
        self.at = {"x": (lon // 2) % 4, "y": (lon // 8) * 2 + lat % 2, "z": lat // 2}

    def mesh_id(self, at, core):
        return (at["z"] * 2 + at["y"] % 2, (at["y"] // 2) * 8 + at["x"] * 2 + core)

    def sibling(self):
        return self.mesh_id(self.at, 1 - self.core)

    def along(self, axis, step):
        at = dict(self.at)
        at[axis] = (at[axis] + step) % 4
        return self.mesh_id(at, self.core), at[axis]

    def across(self, axis, kind):
        at, c = dict(self.at), self.at[axis]
        at[axis] = c + 1 - 2 * (c % 2) if kind == 1 else 3 - c
        bit = ((c + 1) // 2) % 2 if kind == 1 else c // 2
        return self.mesh_id(at, self.core), bit


def greet(place, others=()):
    barrier = pltpu.get_barrier_semaphore()
    partners = [place.sibling()] + [place.along(a, s)[0] for a in "xyz" for s in (1, 2, 3)] + list(others)
    for partner in partners:
        pl.semaphore_signal(barrier, inc=1, device_id=partner, device_id_type=pl.DeviceIdType.MESH)
    pl.semaphore_wait(barrier, len(partners))


class Sum:
    def __init__(self, place, u, g, done, got, send, recv):
        self.u, self.g, self.done, self.got, self.send, self.recv = u, g, done, got, send, recv
        self.stage, self.slots, self.copies = 0, 0, []
        order, first = ROUTES[u]
        self.steps, base, rows = [], 0, D

        def halve(name, target, bit, base, rows):
            rows //= 2
            self.steps.append((name, [(target, base + (1 - bit) * rows)], base + bit * rows, rows))
            return base + bit * rows, rows

        def quarter(name, axis, base, rows):
            rows //= 4
            peers = [place.along(axis, step) for step in (1, 2, 3)]
            self.steps.append((name, [(t, base + c * rows) for t, c in peers], base + place.at[axis] * rows, rows))
            return base + place.at[axis] * rows, rows

        base, rows = halve("core", place.sibling(), place.core, base, rows)
        if first:
            base, rows = halve("near", *place.across(order[0], first), base, rows)
            base, rows = halve("far", *place.across(order[0], 4 - first), base, rows)
        else:
            base, rows = quarter("axis", order[0], base, rows)
        base, rows = quarter("second", order[1], base, rows)
        peers = [place.along(order[2], step)[0] for step in (1, 2, 3)]
        self.swap = (peers, place.at[order[2]], base, rows)
        self.last = 2 * len(self.steps) + 1

    def part(self, ref, base, rows):
        return ref.at[self.u, pl.ds(pl.multiple_of(base, rows), rows), :]

    def copy(self, src, dst, target):
        slot = self.slots
        self.slots += 1
        one = pltpu.make_async_remote_copy(
            src_ref=src, dst_ref=dst, send_sem=self.send.at[self.u, slot], recv_sem=self.recv.at[self.u, slot],
            device_id=target, device_id_type=pl.DeviceIdType.MESH,
        )
        one.start()
        self.copies.append(one)

    def landing(self, name, i):
        if name == "axis":
            return self.got[name].at[i, self.u - QKV_BLOCKS[0]]
        return self.got[name].at[i, self.u]

    def advance(self):
        n, stage = len(self.steps), self.stage
        self.stage += 1
        for one in self.copies:
            one.wait()
        self.copies = []
        if 1 <= stage <= n:
            name, targets, base, rows = self.steps[stage - 1]
            mine = self.part(self.g, base, rows)
            total = mine[...].astype(F32)
            for i in range(len(targets)):
                total = total + self.landing(name, i)[...].astype(F32)
            mine[...] = total.astype(BF16)
        if stage == n + 1:
            _, _, base, rows = self.swap
            four = [self.got["swap"][c, self.u].astype(F32) for c in range(4)]
            self.part(self.done, base, rows)[...] = ((four[0] + four[1]) + (four[2] + four[3])).astype(BF16)
        if stage < n:
            name, targets, _, rows = self.steps[stage]
            for i, (target, base) in enumerate(targets):
                self.copy(self.part(self.g, base, rows), self.landing(name, i), target)
        elif stage == n:
            targets, at, base, rows = self.swap
            mine = self.part(self.g, base, rows)
            self.got["swap"][at, self.u] = mine[...]
            for target in targets:
                self.copy(mine, self.got["swap"].at[at, self.u], target)
        elif stage <= 2 * n:
            _, targets, base, rows = self.steps[2 * n - stage]
            mine = self.part(self.done, base, rows)
            for target, _ in targets:
                self.copy(mine, mine, target)


LANDINGS = (
    ("core", (1, BLOCKS, D // 2, D)),
    ("near", (1, BLOCKS - 3, D // 4, D)),
    ("far", (1, BLOCKS - 3, D // 8, D)),
    ("axis", (3, 3, D // 8, D)),
    ("second", (3, BLOCKS, D // 32, D)),
    ("swap", (4, BLOCKS, D // 32, D)),
)


def sum_scratch():
    return [pltpu.VMEM(shape, BF16) for _, shape in LANDINGS] + [pltpu.SemaphoreType.DMA((BLOCKS, SLOTS))] * 2


def unpack_kernel(g_ref, tok_ref, out_ref, in_ref, qkv_ref, proj_ref, tok_out, half, full, lines_in, got, put, whole):
    def target(u):
        if u == PROJ_BLOCK:
            return proj_ref
        if u in OUT_BLOCKS:
            return out_ref.at[pl.ds(D * OUT_BLOCKS.index(u), D), :]
        if u in IN_BLOCKS:
            return in_ref.at[:, pl.ds(D * IN_BLOCKS.index(u), D)]
        return qkv_ref.at[:, pl.ds(D * QKV_BLOCKS.index(u), D)]

    ins = [pltpu.make_async_copy(g_ref.at[u], half.at[u], got.at[u]) for u in range(BLOCKS)]
    outs = [pltpu.make_async_copy(full.at[u], target(u), put.at[u]) for u in range(BLOCKS)]
    arrive = pltpu.make_async_copy(tok_ref, lines_in, whole.at[0])
    leave = pltpu.make_async_copy(lines_in, tok_out, whole.at[1])
    arrive.start()
    for one in ins:
        one.start()
    arrive.wait()
    leave.start()
    for u in range(BLOCKS):
        ins[u].wait()
        full[u] = half[u].astype(F32)
        outs[u].start()
    for one in outs:
        one.wait()
    leave.wait()


def unpack_call(grads, grad_tokens):
    anywhere = pl.BlockSpec(memory_space=pl.ANY)
    return pl.pallas_call(
        unpack_kernel,
        out_shape=tuple(jax.ShapeDtypeStruct(s, F32) for s in ((FFN, D), (D, FFN), (D, 3 * D), (D, D), grad_tokens.shape)),
        in_specs=[anywhere] * 2,
        out_specs=(anywhere,) * 5,
        scratch_shapes=[
            pltpu.VMEM((BLOCKS, D, D), BF16),
            pltpu.VMEM((BLOCKS, D, D), F32),
            pltpu.VMEM(grad_tokens.shape, F32),
            pltpu.SemaphoreType.DMA((BLOCKS,)),
            pltpu.SemaphoreType.DMA((BLOCKS,)),
            pltpu.SemaphoreType.DMA((2,)),
        ],
        compiler_params=pltpu.CompilerParams(vmem_limit_bytes=60 * 1024 * 1024),
        name="unpack",
    )(grads, grad_tokens)


LAT_ROWS, LON_ROWS = 64, 16
LAT_AT, LON_AT, DIAG_AT, HALO_ROWS = 0, 192, 336, 384
WINDOWS = 6
FEW = 48
TINY = 16
PIECE = 256
WIDE = 3
OWN_ROWS = 9
OWN_COLS = 30
STRIP = OWN_COLS * WLEV
EDGE = HALF_LON * WLEV
LINE = WLON * WLEV
HALO_PARTS = ((LAT_AT, LON_AT), (LON_AT, DIAG_AT), (DIAG_AT, HALO_ROWS))


def cell(row, wide):
    return ((row // WLAT) * WIDE + wide) * WIN + (row % WLAT) * LINE


def lines(v):
    return v.reshape(v.shape[0] * WLEV, D)


def cells(v):
    return v.reshape(v.shape[0] // WLEV, WLEV, D)


def padded(pieces, rows):
    have = sum(p.shape[0] for p in pieces)
    return jnp.concatenate(pieces + [jnp.zeros((rows - have, D), F32)], axis=0).astype(BF16)


def ahead_at(row):
    return DIAG_AT + row * LON_ROWS if row < HALF_LAT else LON_AT + (row - HALF_LAT) * LON_ROWS


def behind_at(row):
    return LON_AT + row * LON_ROWS if row < OWN_ROWS else DIAG_AT + (row - OWN_ROWS) * LON_ROWS


def pack_ahead(src, dst):
    for row in range(HALF_LAT):
        at = LAT_AT + row * LAT_ROWS
        dst[at : at + LAT_ROWS, :] = padded([lines(src[row, HALF_LON : HALF_LON + OWN_COLS])], LAT_ROWS)
    for row in range(HALF_LAT + OWN_ROWS):
        at = ahead_at(row)
        dst[at : at + LON_ROWS, :] = padded([lines(src[row, :HALF_LON])], LON_ROWS)


def place_strip(flat, row, strip):
    flat[cell(row, 0) : cell(row, 0) + LINE, :] = strip[:LINE]
    flat[cell(row, 1) : cell(row, 1) + LINE, :] = strip[LINE : 2 * LINE]
    flat[cell(row, 2) : cell(row, 2) + EDGE, :] = strip[2 * LINE : STRIP]


def take_strip(flat, row):
    return [
        flat[cell(row, 0) : cell(row, 0) + LINE, :],
        flat[cell(row, 1) : cell(row, 1) + LINE, :],
        flat[cell(row, 2) : cell(row, 2) + EDGE, :],
    ]


def place_own(src, flat):
    for row in range(OWN_ROWS):
        place_strip(flat, row, lines(src[row + HALF_LAT, HALF_LON : HALF_LON + OWN_COLS]))


def place_halo(got, flat):
    for row in range(HALF_LAT):
        at = LAT_AT + row * LAT_ROWS
        place_strip(flat, OWN_ROWS + row, got[at : at + LAT_ROWS, :].astype(F32))
    for row in range(OWN_ROWS + HALF_LAT):
        at, to = behind_at(row), cell(row, 2) + EDGE
        flat[to : to + EDGE, :] = got[at : at + LON_ROWS, :].astype(F32)[:EDGE]


def pack_back(flat, dst):
    for row in range(HALF_LAT):
        at = LAT_AT + row * LAT_ROWS
        dst[at : at + LAT_ROWS, :] = padded(take_strip(flat, OWN_ROWS + row), LAT_ROWS)
    for row in range(OWN_ROWS + HALF_LAT):
        at, end = behind_at(row), cell(row, 2) + EDGE
        dst[at : at + LON_ROWS, :] = padded([flat[end : end + EDGE, :]], LON_ROWS)


def return_own(flat, out):
    for row in range(OWN_ROWS):
        strip = jnp.concatenate(take_strip(flat, row), axis=0)
        out[row + HALF_LAT, HALF_LON : HALF_LON + OWN_COLS] = cells(strip)


def return_halo(got, out):
    for row in range(HALF_LAT + OWN_ROWS):
        at = ahead_at(row)
        out[row, :HALF_LON] = cells(got[at : at + LON_ROWS, :].astype(F32)[:EDGE])
    for row in range(HALF_LAT):
        at = LAT_AT + row * LAT_ROWS
        out[row, HALF_LON : HALF_LON + OWN_COLS] = cells(got[at : at + LAT_ROWS, :].astype(F32)[:STRIP])


def place_regions(region, flat):
    for row in range(HALF_LAT + OWN_ROWS):
        ids = region[row].astype(F32)
        levels = [jnp.broadcast_to(ids[l : l + 1], (128, ids.shape[1])).T for l in range(WLEV)]
        both = jnp.stack(levels[::-1], axis=1).reshape(ids.shape[1] * WLEV, 128)
        for wide in range(WIDE):
            flat[cell(row, wide) : cell(row, wide) + LINE, :] = both[LINE * wide : LINE * (wide + 1)]


AFTER_CHUNK = ((0, 1), (0, 1, 2, 3), (2, 3, 4, 5), (0, 1, 4, 5, 6, 7))
AFTER_PROJ = (8, 2, 3, 6, 7)
AFTER_WINDOW = ((0, 1, 8), (4, 5), (2, 3), (0, 1, 6, 7), (4, 5, 8), (2, 3))
AFTER_QKV = (0, 1, 6, 7, 8)
AFTER_INPUT = (9, 10, 11, 4, 5)
AFTER_NORM = (0, 1, 2, 3, 6, 7, 8)


def block_kernel(
    tokens, cotangent, region, wqkv, wproj, win, wout,
    out_ref, done_hbm,
    done_ref, cot_ref, region_ref, x_ref, c_ref, wqkv_ref, wproj_ref, win_ref, wout_ref,
    normed, packed, probs, mixed, mid, nmid, dnm, g_ref,
    pre, dact, act, dpre, cot_half, dscores,
    halo_out, halo_in, back_out, back_in, load_sem, halo_sem, done_sem, *landings_and_sems,
):
    place = Place()
    *landings, send, recv = landings_and_sems
    got = {name: ref for (name, _), ref in zip(LANDINGS, landings)}
    sums = [Sum(place, u, g_ref, done_ref, got, send, recv) for u in range(BLOCKS)]

    leaving = {u: pltpu.make_async_copy(done_ref.at[u], done_hbm.at[u], done_sem.at[u]) for u in range(BLOCKS)}

    def tick(*blocks):
        for u in blocks:
            sums[u].advance()
            if sums[u].stage == sums[u].last + 1:
                leaving[u].start()

    loads = [
        pltpu.make_async_copy(src, dst, load_sem.at[i])
        for i, (src, dst) in enumerate(
            ((tokens, out_ref), (cotangent, cot_ref), (wqkv, wqkv_ref), (wproj, wproj_ref), (win, win_ref), (wout, wout_ref))
        )
    ]
    for one in loads:
        one.start()

    lat, lon = lax.axis_index("lat"), lax.axis_index("lon")
    lats, lons = lax.axis_size("lat"), lax.axis_size("lon")
    up, down = lax.rem(lat + lats - 1, lats), lax.rem(lat + 1, lats)
    left, right = lax.rem(lon + lons - 1, lons), lax.rem(lon + 1, lons)
    ahead = ((up, lon), (lat, left), (up, left))
    back = ((down, lon), (lat, right), (down, right))
    greet(place, ahead + back)

    def exchange(src, dst, targets, at):
        copies = []
        for i, (lo, hi) in enumerate(HALO_PARTS):
            one = pltpu.make_async_remote_copy(
                src_ref=src.at[lo:hi], dst_ref=dst.at[lo:hi],
                send_sem=halo_sem.at[0, at + i], recv_sem=halo_sem.at[1, at + i],
                device_id=targets[i], device_id_type=pl.DeviceIdType.MESH,
            )
            one.start()
            copies.append(one)
        return copies

    loads[0].wait()
    pack_ahead(out_ref, halo_out.at[0])
    token_halo = exchange(halo_out.at[0], halo_in.at[0], ahead, 0)
    loads[1].wait()
    pack_ahead(cot_ref, halo_out.at[1])
    cot_halo = exchange(halo_out.at[1], halo_in.at[1], ahead, 3)
    place_own(out_ref, x_ref)
    place_regions(region, region_ref)

    rows_of = lambda w: pl.ds(pl.multiple_of(w * WIN, WIN), WIN)
    few_of = lambda i: pl.ds(pl.multiple_of(i * FEW, FEW), FEW)
    fews = WIN // FEW
    pieces = [(c, min(c + PIECE, SPREAD)) for c in range(0, SPREAD, PIECE)]

    def attention_forward(first, last):
        @pl.loop(first * fews, last * fews)
        def _(i):
            unit, _ = norm_parts(x_ref[few_of(i), :])
            normed[few_of(i), :] = unit.astype(BF16)

        if first == 0:
            loads[2].wait()
        rows = slice(first * WIN, last * WIN)
        for j in range(3):
            cols = slice(D * j, D * (j + 1))
            packed[rows, cols] = nn(normed[rows, :], wqkv_ref[:, cols]).astype(BF16)

        @pl.loop(first, last)
        def _(w):
            rows = rows_of(w)
            ids = region_ref[rows, :]
            of_key, of_query = ids[:, :1], jnp.concatenate([ids.T[:1]] * GROUP, axis=1)
            for g in range(GROUPS):
                lo = LANES * g
                q = packed[rows, lo : lo + LANES]
                k = packed[rows, D + lo : D + lo + LANES]
                v = packed[rows, 2 * D + lo : 2 * D + lo + LANES]
                q = spread_heads(q)
                for c0, c1 in pieces:
                    s = jnp.where(of_key == of_query[:, c0:c1], nt(k, q[c0:c1]), MASKED)
                    e = jnp.exp2((s - jnp.max(s, axis=0, keepdims=True)) * (SCALE * LOG2E))
                    p = e * (1.0 / jnp.sum(e, axis=0, keepdims=True))
                    probs[w * GROUPS + g, :, c0:c1] = p.astype(BF16)
                mixed[rows, lo : lo + LANES] = own_blocks(nn(v.T, probs[w * GROUPS + g])).T.astype(BF16)

    attention_forward(0, 2)
    for one in token_halo:
        one.wait()
    place_halo(halo_in.at[0], x_ref)
    attention_forward(2, WINDOWS)

    loads[3].wait()
    mid[...] = nn(mixed[...], wproj_ref[...]).astype(BF16).astype(F32)

    @pl.loop(0, WINDOWS * fews)
    def _(i):
        rows = few_of(i)
        middle = x_ref[rows, :] + mid[rows, :]
        mid[rows, :] = middle
        nmid[rows, :] = norm_parts(middle)[0].astype(BF16)

    place_own(cot_ref, c_ref)
    for one in cot_halo:
        one.wait()
    place_halo(halo_in.at[1], c_ref)
    loads[4].wait()
    loads[5].wait()

    nmid_t = nmid[...].T
    cot_half[...] = c_ref[...].astype(BF16)
    for j in range(FFN // D):
        cols = slice(D * j, D * (j + 1))
        pre[...] = nn(nmid[...], win_ref[:, cols])
        dact[...] = nt(cot_half[...], wout_ref[cols, :])

        @pl.loop(0, WINDOWS * WIN // TINY, unroll=2)
        def _(i):
            rows = pl.ds(pl.multiple_of(i * TINY, TINY), TINY)
            u = pre[rows, :]
            square = u * u
            t = jnp.tanh(u * (GELU_A + (GELU_A * GELU_B) * square))
            half = 0.5 + 0.5 * t
            act[rows, :] = (u * half).astype(BF16)
            slope = half + u * (0.5 - 0.5 * t * t) * (GELU_A + (3 * GELU_A * GELU_B) * square)
            dpre[rows, :] = (slope * dact[rows, :]).astype(BF16)

        g_ref[OUT_BLOCKS[j]] = nn(act[...].T, cot_half[...]).astype(BF16)
        g_ref[IN_BLOCKS[j]] = nn(nmid_t, dpre[...]).astype(BF16)
        part = nt(dpre[...], win_ref[:, cols])
        if j == 0:
            dnm[...] = part
        else:
            dnm[...] += part
        tick(*AFTER_CHUNK[j])

    @pl.loop(0, WINDOWS * fews)
    def _(i):
        rows = few_of(i)
        unit, r = norm_parts(mid[rows, :])
        d_mid = c_ref[rows, :] + norm_back(unit, r, dnm[rows, :])
        c_ref[rows, :] = d_mid
        nmid[rows, :] = d_mid.astype(BF16)

    g_ref[PROJ_BLOCK] = nn(mixed[...].T, nmid[...]).astype(BF16)
    tick(*AFTER_PROJ)
    mixed[...] = nt(nmid[...], wproj_ref[...]).astype(BF16)

    for w in range(WINDOWS):

        @pl.loop(w, w + 1)
        def _(w):
            rows = rows_of(w)
            for g in range(GROUPS):
                lo = LANES * g
                q = spread_heads(packed[rows, lo : lo + LANES])
                k = packed[rows, D + lo : D + lo + LANES]
                v = packed[rows, 2 * D + lo : 2 * D + lo + LANES]
                do = spread_heads(mixed[rows, lo : lo + LANES])
                p = probs[w * GROUPS + g]
                for c0, c1 in pieces:
                    dp = nt(v, do[c0:c1])
                    pf = probs[w * GROUPS + g, :, c0:c1].astype(F32)
                    total = jnp.sum(dp * pf, axis=0, keepdims=True)
                    dscores[:, c0:c1] = (pf * (dp - total) * SCALE).astype(BF16)
                ds = dscores[...]
                packed[rows, lo : lo + LANES] = own_blocks(nn(k.T, ds)).T.astype(BF16)
                packed[rows, D + lo : D + lo + LANES] = nn(ds, q).astype(BF16)
                packed[rows, 2 * D + lo : 2 * D + lo + LANES] = nn(p, do).astype(BF16)

        tick(*AFTER_WINDOW[w])

    normed_t = normed[...].T
    for j in range(3):
        g_ref[QKV_BLOCKS[j]] = nn(normed_t, packed[:, D * j : D * (j + 1)]).astype(BF16)
        tick(QKV_BLOCKS[j])
    tick(*AFTER_QKV)
    for j in range(3):
        cols = slice(D * j, D * (j + 1))
        part = nt(packed[:, cols], wqkv_ref[:, cols])
        if j == 0:
            dnm[...] = part
        else:
            dnm[...] += part
    tick(*AFTER_INPUT)

    @pl.loop(0, WINDOWS * fews)
    def _(i):
        rows = few_of(i)
        unit, r = norm_parts(x_ref[rows, :])
        c_ref[rows, :] = c_ref[rows, :] + norm_back(unit, r, dnm[rows, :])

    tick(*AFTER_NORM)
    pack_back(c_ref, back_out)
    grad_halo = exchange(back_out, back_in, back, 6)
    return_own(c_ref, out_ref)

    rounds = 0
    while any(one.stage <= one.last for one in sums):
        tick(*(u for u in (9, 10, 11, 0, 1, 2, 3, 4, 5, 6, 7, 8) if sums[u].stage <= sums[u].last))
        rounds += 1
        if rounds == 2:
            for one in grad_halo:
                one.wait()
            return_halo(back_in, out_ref)
    for one in leaving.values():
        one.wait()


def block_call(tokens, cotangent, region, w_qkv, w_proj, w_in, w_out):
    anywhere, vmem = pl.BlockSpec(memory_space=pl.ANY), pl.BlockSpec(memory_space=pltpu.VMEM)
    count = WINDOWS * WIN
    return pl.pallas_call(
        block_kernel,
        out_shape=(jax.ShapeDtypeStruct(tokens.shape, F32), jax.ShapeDtypeStruct((BLOCKS, D, D), BF16)),
        in_specs=[anywhere, anywhere, vmem] + [anywhere] * 4,
        out_specs=(vmem, anywhere),
        scratch_shapes=[
            pltpu.VMEM((BLOCKS, D, D), BF16),
            pltpu.VMEM(tokens.shape, F32),
            pltpu.VMEM((count, 128), F32),
            pltpu.VMEM((count, D), F32),
            pltpu.VMEM((count, D), F32),
            pltpu.VMEM(w_qkv.shape, BF16),
            pltpu.VMEM(w_proj.shape, BF16),
            pltpu.VMEM(w_in.shape, BF16),
            pltpu.VMEM(w_out.shape, BF16),
            pltpu.VMEM((count, D), BF16),
            pltpu.VMEM((count, 3 * D), BF16),
            pltpu.VMEM((WINDOWS * GROUPS, WIN, SPREAD), BF16),
            pltpu.VMEM((count, D), BF16),
            pltpu.VMEM((count, D), F32),
            pltpu.VMEM((count, D), BF16),
            pltpu.VMEM((count, D), F32),
            pltpu.VMEM((BLOCKS, D, D), BF16),
            pltpu.VMEM((count, D), F32),
            pltpu.VMEM((count, D), F32),
            pltpu.VMEM((count, D), BF16),
            pltpu.VMEM((count, D), BF16),
            pltpu.VMEM((count, D), BF16),
            pltpu.VMEM((WIN, SPREAD), BF16),
            pltpu.VMEM((2, HALO_ROWS, D), BF16),
            pltpu.VMEM((2, HALO_ROWS, D), BF16),
            pltpu.VMEM((HALO_ROWS, D), BF16),
            pltpu.VMEM((HALO_ROWS, D), BF16),
            pltpu.SemaphoreType.DMA((6,)),
            pltpu.SemaphoreType.DMA((2, 9)),
            pltpu.SemaphoreType.DMA((BLOCKS,)),
        ]
        + sum_scratch(),
        compiler_params=pltpu.CompilerParams(
            collective_id=0, has_side_effects=True, vmem_limit_bytes=63 * 1024 * 1024
        ),
        cost_estimate=pl.CostEstimate(flops=16 * 10**9, bytes_accessed=24 * 10**6, transcendentals=4 * 10**6),
        name="block",
    )(tokens, cotangent, region, w_qkv, w_proj, w_in, w_out)


def local(tokens, cotangent, region_ids, w_qkv, w_proj, w_in, w_out):
    grad_tokens, grads = block_call(
        tokens.transpose(1, 2, 0, 3), cotangent.transpose(1, 2, 0, 3), region_ids.transpose(1, 0, 2),
        w_qkv, w_proj, w_in, w_out,
    )
    grad_out, grad_in, grad_qkv, grad_proj, grad_tokens = unpack_call(grads, grad_tokens)
    return grad_tokens.transpose(2, 0, 1, 3), grad_qkv, grad_proj, grad_in, grad_out


def solution(mesh):
    grid = P(None, "lat", "lon", None)
    in_specs = (grid, grid, P(None, "lat", "lon"), P(), P(), P(), P())
    out_specs = (grid, P(), P(), P(), P())
    return jax.shard_map(local, mesh=mesh, in_specs=in_specs, out_specs=out_specs, check_vma=False)
```

```python
import functools

import jax
import jax.numpy as jnp
from jax import lax
from jax.experimental import pallas as pl
from jax.experimental.pallas import tpu as pltpu
from jax.sharding import PartitionSpec as P

D = 512
HEADS = 16
HEAD_DIM = D // HEADS
FFN = 2048
WLEV = 2
WLAT = 6
WLON = 12
WIN = WLEV * WLAT * WLON
GROUP = 8
LANES = GROUP * HEAD_DIM
GROUPS = HEADS // GROUP
SPREAD = GROUP * WIN
HALF_LAT = WLAT // 2
HALF_LON = WLON // 2
EPS = 1e-05
MASKED = -1e10
SCALE = HEAD_DIM ** -0.5
LOG2E = 1.4426950408889634
GELU_A = 0.7978845608028654
GELU_B = 0.044715
F32 = jnp.float32
BF16 = jnp.bfloat16


def nn(a, b):
    return lax.dot_general(a, b, (((1,), (0,)), ((), ())), preferred_element_type=F32)


def nt(a, b):
    return lax.dot_general(a, b, (((1,), (1,)), ((), ())), preferred_element_type=F32)


def norm_parts(v):
    centred = v - jnp.mean(v, axis=-1, keepdims=True)
    r = lax.rsqrt(jnp.mean(centred * centred, axis=-1, keepdims=True) + EPS)
    return centred * r, r


def norm_back(unit, r, g):
    return r * (g - jnp.mean(g, axis=-1, keepdims=True) - unit * jnp.mean(g * unit, axis=-1, keepdims=True))


def spread_heads(v):
    lane_head = lax.broadcasted_iota(jnp.int32, v.shape, 1) // HEAD_DIM
    zero = jnp.zeros_like(v)
    return jnp.concatenate([jnp.where(lane_head == h, v, zero) for h in range(GROUP)], axis=0)


def own_blocks(full):
    return jnp.concatenate(
        [full[HEAD_DIM * h : HEAD_DIM * (h + 1), WIN * h : WIN * (h + 1)] for h in range(GROUP)], axis=0
    )


BLOCKS = 12
OUT_BLOCKS = (0, 2, 4, 6)
IN_BLOCKS = (1, 3, 5, 7)
PROJ_BLOCK = 8
QKV_BLOCKS = (9, 10, 11)
ROUTES = (
    ("xyz", 1), ("yzx", 1), ("zxy", 1), ("xyz", 3), ("yzx", 3), ("zxy", 3),
    ("xyz", 1), ("yzx", 1), ("zxy", 1),
    ("xyz", 0), ("yzx", 0), ("zxy", 0),
)
SLOTS = 17


class Place:
    def __init__(self):
        lat, lon = lax.axis_index("lat"), lax.axis_index("lon")
        self.core = lon % 2
        self.at = {"x": (lon // 2) % 4, "y": (lon // 8) * 2 + lat % 2, "z": lat // 2}

    def mesh_id(self, at, core):
        return (at["z"] * 2 + at["y"] % 2, (at["y"] // 2) * 8 + at["x"] * 2 + core)

    def sibling(self):
        return self.mesh_id(self.at, 1 - self.core)

    def along(self, axis, step):
        at = dict(self.at)
        at[axis] = (at[axis] + step) % 4
        return self.mesh_id(at, self.core), at[axis]

    def across(self, axis, kind):
        at, c = dict(self.at), self.at[axis]
        at[axis] = c + 1 - 2 * (c % 2) if kind == 1 else 3 - c
        bit = ((c + 1) // 2) % 2 if kind == 1 else c // 2
        return self.mesh_id(at, self.core), bit


def greet(place, others=()):
    barrier = pltpu.get_barrier_semaphore()
    partners = [place.sibling()] + [place.along(a, s)[0] for a in "xyz" for s in (1, 2, 3)] + list(others)
    for partner in partners:
        pl.semaphore_signal(barrier, inc=1, device_id=partner, device_id_type=pl.DeviceIdType.MESH)
    pl.semaphore_wait(barrier, len(partners))


class Sum:
    def __init__(self, place, u, g, done, got, send, recv):
        self.u, self.g, self.done, self.got, self.send, self.recv = u, g, done, got, send, recv
        self.stage, self.slots, self.copies = 0, 0, []
        order, first = ROUTES[u]
        self.steps, base, rows = [], 0, D

        def halve(name, target, bit, base, rows):
            rows //= 2
            self.steps.append((name, [(target, base + (1 - bit) * rows)], base + bit * rows, rows))
            return base + bit * rows, rows

        def quarter(name, axis, base, rows):
            rows //= 4
            peers = [place.along(axis, step) for step in (1, 2, 3)]
            self.steps.append((name, [(t, base + c * rows) for t, c in peers], base + place.at[axis] * rows, rows))
            return base + place.at[axis] * rows, rows

        base, rows = halve("core", place.sibling(), place.core, base, rows)
        if first:
            base, rows = halve("near", *place.across(order[0], first), base, rows)
            base, rows = halve("far", *place.across(order[0], 4 - first), base, rows)
        else:
            base, rows = quarter("axis", order[0], base, rows)
        base, rows = quarter("second", order[1], base, rows)
        peers = [place.along(order[2], step)[0] for step in (1, 2, 3)]
        self.swap = (peers, place.at[order[2]], base, rows)
        self.last = 2 * len(self.steps) + 1

    def part(self, ref, base, rows):
        return ref.at[self.u, pl.ds(pl.multiple_of(base, rows), rows), :]

    def copy(self, src, dst, target):
        slot = self.slots
        self.slots += 1
        one = pltpu.make_async_remote_copy(
            src_ref=src, dst_ref=dst, send_sem=self.send.at[self.u, slot], recv_sem=self.recv.at[self.u, slot],
            device_id=target, device_id_type=pl.DeviceIdType.MESH,
        )
        one.start()
        self.copies.append(one)

    def landing(self, name, i):
        if name == "axis":
            return self.got[name].at[i, self.u - QKV_BLOCKS[0]]
        return self.got[name].at[i, self.u]

    def advance(self):
        n, stage = len(self.steps), self.stage
        self.stage += 1
        for one in self.copies:
            one.wait()
        self.copies = []
        if 1 <= stage <= n:
            name, targets, base, rows = self.steps[stage - 1]
            mine = self.part(self.g, base, rows)
            total = mine[...].astype(F32)
            for i in range(len(targets)):
                total = total + self.landing(name, i)[...].astype(F32)
            mine[...] = total.astype(BF16)
        if stage == n + 1:
            _, _, base, rows = self.swap
            four = [self.got["swap"][c, self.u].astype(F32) for c in range(4)]
            self.part(self.done, base, rows)[...] = ((four[0] + four[1]) + (four[2] + four[3])).astype(BF16)
        if stage < n:
            name, targets, _, rows = self.steps[stage]
            for i, (target, base) in enumerate(targets):
                self.copy(self.part(self.g, base, rows), self.landing(name, i), target)
        elif stage == n:
            targets, at, base, rows = self.swap
            mine = self.part(self.g, base, rows)
            self.got["swap"][at, self.u] = mine[...]
            for target in targets:
                self.copy(mine, self.got["swap"].at[at, self.u], target)
        elif stage <= 2 * n:
            _, targets, base, rows = self.steps[2 * n - stage]
            mine = self.part(self.done, base, rows)
            for target, _ in targets:
                self.copy(mine, mine, target)


LANDINGS = (
    ("core", (1, BLOCKS, D // 2, D)),
    ("near", (1, BLOCKS - 3, D // 4, D)),
    ("far", (1, BLOCKS - 3, D // 8, D)),
    ("axis", (3, 3, D // 8, D)),
    ("second", (3, BLOCKS, D // 32, D)),
    ("swap", (4, BLOCKS, D // 32, D)),
)


def sum_scratch():
    return [pltpu.VMEM(shape, BF16) for _, shape in LANDINGS] + [pltpu.SemaphoreType.DMA((BLOCKS, SLOTS))] * 2


def unpack_kernel(g_ref, tok_ref, out_ref, in_ref, qkv_ref, proj_ref, tok_out, half, full, lines_in, got, put, whole):
    def target(u):
        if u == PROJ_BLOCK:
            return proj_ref
        if u in OUT_BLOCKS:
            return out_ref.at[pl.ds(D * OUT_BLOCKS.index(u), D), :]
        if u in IN_BLOCKS:
            return in_ref.at[:, pl.ds(D * IN_BLOCKS.index(u), D)]
        return qkv_ref.at[:, pl.ds(D * QKV_BLOCKS.index(u), D)]

    ins = [pltpu.make_async_copy(g_ref.at[u], half.at[u], got.at[u]) for u in range(BLOCKS)]
    outs = [pltpu.make_async_copy(full.at[u], target(u), put.at[u]) for u in range(BLOCKS)]
    arrive = pltpu.make_async_copy(tok_ref, lines_in, whole.at[0])
    leave = pltpu.make_async_copy(lines_in, tok_out, whole.at[1])
    arrive.start()
    for one in ins:
        one.start()
    arrive.wait()
    leave.start()
    for u in range(BLOCKS):
        ins[u].wait()
        full[u] = half[u].astype(F32)
        outs[u].start()
    for one in outs:
        one.wait()
    leave.wait()


def unpack_call(grads, grad_tokens):
    anywhere = pl.BlockSpec(memory_space=pl.ANY)
    return pl.pallas_call(
        unpack_kernel,
        out_shape=tuple(jax.ShapeDtypeStruct(s, F32) for s in ((FFN, D), (D, FFN), (D, 3 * D), (D, D), grad_tokens.shape)),
        in_specs=[anywhere] * 2,
        out_specs=(anywhere,) * 5,
        scratch_shapes=[
            pltpu.VMEM((BLOCKS, D, D), BF16),
            pltpu.VMEM((BLOCKS, D, D), F32),
            pltpu.VMEM(grad_tokens.shape, F32),
            pltpu.SemaphoreType.DMA((BLOCKS,)),
            pltpu.SemaphoreType.DMA((BLOCKS,)),
            pltpu.SemaphoreType.DMA((2,)),
        ],
        compiler_params=pltpu.CompilerParams(vmem_limit_bytes=60 * 1024 * 1024),
        name="unpack",
    )(grads, grad_tokens)


LAT_ROWS, LON_ROWS = 64, 16
LAT_AT, LON_AT, DIAG_AT, HALO_ROWS = 0, 192, 336, 384
WINDOWS = 6
FEW = 144
TINY = 16
PIECE = 256
WIDE = 3
OWN_ROWS = 9
OWN_COLS = 30
STRIP = OWN_COLS * WLEV
EDGE = HALF_LON * WLEV
LINE = WLON * WLEV
HALO_PARTS = ((LAT_AT, LON_AT), (LON_AT, DIAG_AT), (DIAG_AT, HALO_ROWS))


def cell(row, wide):
    return ((row // WLAT) * WIDE + wide) * WIN + (row % WLAT) * LINE


def lines(v):
    return v.reshape(v.shape[0] * WLEV, D)


def cells(v):
    return v.reshape(v.shape[0] // WLEV, WLEV, D)


def padded(pieces, rows):
    have = sum(p.shape[0] for p in pieces)
    return jnp.concatenate(pieces + [jnp.zeros((rows - have, D), F32)], axis=0).astype(BF16)


def ahead_at(row):
    return DIAG_AT + row * LON_ROWS if row < HALF_LAT else LON_AT + (row - HALF_LAT) * LON_ROWS


def behind_at(row):
    return LON_AT + row * LON_ROWS if row < OWN_ROWS else DIAG_AT + (row - OWN_ROWS) * LON_ROWS


def pack_ahead(src, dst):
    for row in range(HALF_LAT):
        at = LAT_AT + row * LAT_ROWS
        dst[at : at + LAT_ROWS, :] = padded([lines(src[row, HALF_LON : HALF_LON + OWN_COLS])], LAT_ROWS)
    for row in range(HALF_LAT + OWN_ROWS):
        at = ahead_at(row)
        dst[at : at + LON_ROWS, :] = padded([lines(src[row, :HALF_LON])], LON_ROWS)


def place_strip(flat, row, strip):
    flat[cell(row, 0) : cell(row, 0) + LINE, :] = strip[:LINE]
    flat[cell(row, 1) : cell(row, 1) + LINE, :] = strip[LINE : 2 * LINE]
    flat[cell(row, 2) : cell(row, 2) + EDGE, :] = strip[2 * LINE : STRIP]


def take_strip(flat, row):
    return [
        flat[cell(row, 0) : cell(row, 0) + LINE, :],
        flat[cell(row, 1) : cell(row, 1) + LINE, :],
        flat[cell(row, 2) : cell(row, 2) + EDGE, :],
    ]


def place_own(src, flat):
    for row in range(OWN_ROWS):
        place_strip(flat, row, lines(src[row + HALF_LAT, HALF_LON : HALF_LON + OWN_COLS]))


def place_halo(got, flat):
    for row in range(HALF_LAT):
        at = LAT_AT + row * LAT_ROWS
        place_strip(flat, OWN_ROWS + row, got[at : at + LAT_ROWS, :].astype(F32))
    for row in range(OWN_ROWS + HALF_LAT):
        at, to = behind_at(row), cell(row, 2) + EDGE
        flat[to : to + EDGE, :] = got[at : at + LON_ROWS, :].astype(F32)[:EDGE]


def pack_back(flat, dst):
    for row in range(HALF_LAT):
        at = LAT_AT + row * LAT_ROWS
        dst[at : at + LAT_ROWS, :] = padded(take_strip(flat, OWN_ROWS + row), LAT_ROWS)
    for row in range(OWN_ROWS + HALF_LAT):
        at, end = behind_at(row), cell(row, 2) + EDGE
        dst[at : at + LON_ROWS, :] = padded([flat[end : end + EDGE, :]], LON_ROWS)


def return_own(flat, out):
    for row in range(OWN_ROWS):
        strip = jnp.concatenate(take_strip(flat, row), axis=0)
        out[row + HALF_LAT, HALF_LON : HALF_LON + OWN_COLS] = cells(strip)


def return_halo(got, out):
    for row in range(HALF_LAT + OWN_ROWS):
        at = ahead_at(row)
        out[row, :HALF_LON] = cells(got[at : at + LON_ROWS, :].astype(F32)[:EDGE])
    for row in range(HALF_LAT):
        at = LAT_AT + row * LAT_ROWS
        out[row, HALF_LON : HALF_LON + OWN_COLS] = cells(got[at : at + LAT_ROWS, :].astype(F32)[:STRIP])


def place_regions(region, flat):
    for row in range(HALF_LAT + OWN_ROWS):
        ids = region[row].astype(F32)
        levels = [jnp.broadcast_to(ids[l : l + 1], (128, ids.shape[1])).T for l in range(WLEV)]
        both = jnp.stack(levels[::-1], axis=1).reshape(ids.shape[1] * WLEV, 128)
        for wide in range(WIDE):
            flat[cell(row, wide) : cell(row, wide) + LINE, :] = both[LINE * wide : LINE * (wide + 1)]


AFTER_CHUNK = ((0, 1), (2, 3), (0, 1, 4, 5), (2, 3, 6, 7))
AFTER_PROJ = (8, 0, 1, 4, 5)
AFTER_WINDOW = ((2, 3, 6, 7), (8,), (0, 1, 4, 5), (2, 3, 6, 7), (8,), (0, 1, 4, 5))
AFTER_QKV = (2, 3, 6, 7, 8)
AFTER_INPUT = (9, 10, 11, 0, 1, 4, 5)
AFTER_NORM = (2, 3, 6, 7, 8)


def block_kernel(
    tokens, cotangent, region, wqkv, wproj, win, wout,
    out_ref, done_hbm,
    done_ref, cot_ref, region_ref, x_ref, c_ref, wqkv_ref, wproj_ref, win_ref, wout_ref,
    normed, packed, probs, mixed, mid, nmid, dnm, g_ref,
    pre, dact, act, dpre, cot_half, dscores,
    halo_out, halo_in, back_out, back_in, load_sem, halo_sem, done_sem, *landings_and_sems,
):
    place = Place()
    *landings, send, recv = landings_and_sems
    got = {name: ref for (name, _), ref in zip(LANDINGS, landings)}
    sums = [Sum(place, u, g_ref, done_ref, got, send, recv) for u in range(BLOCKS)]

    leaving = {u: pltpu.make_async_copy(done_ref.at[u], done_hbm.at[u], done_sem.at[u]) for u in range(BLOCKS)}

    def tick(*blocks):
        for u in blocks:
            sums[u].advance()
            if sums[u].stage == sums[u].last + 1:
                leaving[u].start()

    loads = [
        pltpu.make_async_copy(src, dst, load_sem.at[i])
        for i, (src, dst) in enumerate(
            ((tokens, out_ref), (cotangent, cot_ref), (wqkv, wqkv_ref), (wproj, wproj_ref), (win, win_ref), (wout, wout_ref))
        )
    ]
    for one in loads:
        one.start()

    lat, lon = lax.axis_index("lat"), lax.axis_index("lon")
    lats, lons = lax.axis_size("lat"), lax.axis_size("lon")
    up, down = lax.rem(lat + lats - 1, lats), lax.rem(lat + 1, lats)
    left, right = lax.rem(lon + lons - 1, lons), lax.rem(lon + 1, lons)
    ahead = ((up, lon), (lat, left), (up, left))
    back = ((down, lon), (lat, right), (down, right))
    greet(place, ahead + back)

    def exchange(src, dst, targets, at):
        copies = []
        for i, (lo, hi) in enumerate(HALO_PARTS):
            one = pltpu.make_async_remote_copy(
                src_ref=src.at[lo:hi], dst_ref=dst.at[lo:hi],
                send_sem=halo_sem.at[0, at + i], recv_sem=halo_sem.at[1, at + i],
                device_id=targets[i], device_id_type=pl.DeviceIdType.MESH,
            )
            one.start()
            copies.append(one)
        return copies

    loads[0].wait()
    pack_ahead(out_ref, halo_out.at[0])
    token_halo = exchange(halo_out.at[0], halo_in.at[0], ahead, 0)
    loads[1].wait()
    pack_ahead(cot_ref, halo_out.at[1])
    cot_halo = exchange(halo_out.at[1], halo_in.at[1], ahead, 3)
    place_own(out_ref, x_ref)
    place_regions(region, region_ref)

    rows_of = lambda w: pl.ds(pl.multiple_of(w * WIN, WIN), WIN)
    few_of = lambda i: pl.ds(pl.multiple_of(i * FEW, FEW), FEW)
    fews = WIN // FEW
    pieces = [(c, min(c + PIECE, SPREAD)) for c in range(0, SPREAD, PIECE)]

    def attention_forward(first, last):
        @pl.loop(first * fews, last * fews)
        def _(i):
            unit, _ = norm_parts(x_ref[few_of(i), :])
            normed[few_of(i), :] = unit.astype(BF16)

        if first == 0:
            loads[2].wait()
        rows = slice(first * WIN, last * WIN)
        for j in range(3):
            cols = slice(D * j, D * (j + 1))
            packed[rows, cols] = nn(normed[rows, :], wqkv_ref[:, cols]).astype(BF16)

        @pl.loop(first, last)
        def _(w):
            rows = rows_of(w)
            ids = region_ref[rows, :]
            of_key, of_query = ids[:, :1], jnp.concatenate([ids.T[:1]] * GROUP, axis=1)
            for g in range(GROUPS):
                lo = LANES * g
                q = packed[rows, lo : lo + LANES]
                k = packed[rows, D + lo : D + lo + LANES]
                v = packed[rows, 2 * D + lo : 2 * D + lo + LANES]
                q = spread_heads(q)
                for c0, c1 in pieces:
                    s = jnp.where(of_key == of_query[:, c0:c1], nt(k, q[c0:c1]), MASKED)
                    e = jnp.exp2((s - jnp.max(s, axis=0, keepdims=True)) * (SCALE * LOG2E))
                    p = e * (1.0 / jnp.sum(e, axis=0, keepdims=True))
                    probs[w * GROUPS + g, :, c0:c1] = p.astype(BF16)
                mixed[rows, lo : lo + LANES] = own_blocks(nn(v.T, probs[w * GROUPS + g])).T.astype(BF16)

    attention_forward(0, 2)
    for one in token_halo:
        one.wait()
    place_halo(halo_in.at[0], x_ref)
    attention_forward(2, WINDOWS)

    loads[3].wait()
    mid[...] = nn(mixed[...], wproj_ref[...]).astype(BF16).astype(F32)

    @pl.loop(0, WINDOWS * fews)
    def _(i):
        rows = few_of(i)
        middle = x_ref[rows, :] + mid[rows, :]
        mid[rows, :] = middle
        nmid[rows, :] = norm_parts(middle)[0].astype(BF16)

    place_own(cot_ref, c_ref)
    for one in cot_halo:
        one.wait()
    place_halo(halo_in.at[1], c_ref)
    loads[4].wait()
    loads[5].wait()

    nmid_t = nmid[...].T
    cot_half[...] = c_ref[...].astype(BF16)
    for j in range(FFN // D):
        cols = slice(D * j, D * (j + 1))
        pre[...] = nn(nmid[...], win_ref[:, cols])
        dact[...] = nt(cot_half[...], wout_ref[cols, :])

        @pl.loop(0, WINDOWS * WIN // TINY, unroll=9)
        def _(i):
            rows = pl.ds(pl.multiple_of(i * TINY, TINY), TINY)
            u = pre[rows, :]
            square = u * u
            t = jnp.tanh(u * (GELU_A + (GELU_A * GELU_B) * square))
            half = 0.5 + 0.5 * t
            act[rows, :] = (u * half).astype(BF16)
            slope = half + u * (0.5 - 0.5 * t * t) * (GELU_A + (3 * GELU_A * GELU_B) * square)
            dpre[rows, :] = (slope * dact[rows, :]).astype(BF16)

        g_ref[OUT_BLOCKS[j]] = nn(act[...].T, cot_half[...]).astype(BF16)
        g_ref[IN_BLOCKS[j]] = nn(nmid_t, dpre[...]).astype(BF16)
        part = nt(dpre[...], win_ref[:, cols])
        if j == 0:
            dnm[...] = part
        else:
            dnm[...] += part
        tick(*AFTER_CHUNK[j])

    @pl.loop(0, WINDOWS * fews)
    def _(i):
        rows = few_of(i)
        unit, r = norm_parts(mid[rows, :])
        d_mid = c_ref[rows, :] + norm_back(unit, r, dnm[rows, :])
        c_ref[rows, :] = d_mid
        nmid[rows, :] = d_mid.astype(BF16)

    g_ref[PROJ_BLOCK] = nn(mixed[...].T, nmid[...]).astype(BF16)
    tick(*AFTER_PROJ)
    mixed[...] = nt(nmid[...], wproj_ref[...]).astype(BF16)

    for w in range(WINDOWS):

        @pl.loop(w, w + 1)
        def _(w):
            rows = rows_of(w)
            for g in range(GROUPS):
                lo = LANES * g
                q = spread_heads(packed[rows, lo : lo + LANES])
                k = packed[rows, D + lo : D + lo + LANES]
                v = packed[rows, 2 * D + lo : 2 * D + lo + LANES]
                do = spread_heads(mixed[rows, lo : lo + LANES])
                p = probs[w * GROUPS + g]
                for c0, c1 in pieces:
                    dp = nt(v, do[c0:c1])
                    pf = probs[w * GROUPS + g, :, c0:c1].astype(F32)
                    total = jnp.sum(dp * pf, axis=0, keepdims=True)
                    dscores[:, c0:c1] = (pf * (dp - total) * SCALE).astype(BF16)
                ds = dscores[...]
                packed[rows, lo : lo + LANES] = own_blocks(nn(k.T, ds)).T.astype(BF16)
                packed[rows, D + lo : D + lo + LANES] = nn(ds, q).astype(BF16)
                packed[rows, 2 * D + lo : 2 * D + lo + LANES] = nn(p, do).astype(BF16)

        tick(*AFTER_WINDOW[w])

    normed_t = normed[...].T
    for j in range(3):
        g_ref[QKV_BLOCKS[j]] = nn(normed_t, packed[:, D * j : D * (j + 1)]).astype(BF16)
        tick(QKV_BLOCKS[j])
    tick(*AFTER_QKV)
    for j in range(3):
        cols = slice(D * j, D * (j + 1))
        part = nt(packed[:, cols], wqkv_ref[:, cols])
        if j == 0:
            dnm[...] = part
        else:
            dnm[...] += part
    tick(*AFTER_INPUT)

    @pl.loop(0, WINDOWS * fews)
    def _(i):
        rows = few_of(i)
        unit, r = norm_parts(x_ref[rows, :])
        c_ref[rows, :] = c_ref[rows, :] + norm_back(unit, r, dnm[rows, :])

    tick(*AFTER_NORM)
    pack_back(c_ref, back_out)
    grad_halo = exchange(back_out, back_in, back, 6)
    return_own(c_ref, out_ref)

    rounds = 0
    while any(one.stage <= one.last for one in sums):
        tick(*(u for u in (9, 10, 11, 0, 1, 2, 3, 4, 5, 6, 7, 8) if sums[u].stage <= sums[u].last))
        rounds += 1
        if rounds == 2:
            for one in grad_halo:
                one.wait()
            return_halo(back_in, out_ref)
    for one in leaving.values():
        one.wait()


def block_call(tokens, cotangent, region, w_qkv, w_proj, w_in, w_out):
    anywhere, vmem = pl.BlockSpec(memory_space=pl.ANY), pl.BlockSpec(memory_space=pltpu.VMEM)
    count = WINDOWS * WIN
    return pl.pallas_call(
        block_kernel,
        out_shape=(jax.ShapeDtypeStruct(tokens.shape, F32), jax.ShapeDtypeStruct((BLOCKS, D, D), BF16)),
        in_specs=[anywhere, anywhere, vmem] + [anywhere] * 4,
        out_specs=(vmem, anywhere),
        scratch_shapes=[
            pltpu.VMEM((BLOCKS, D, D), BF16),
            pltpu.VMEM(tokens.shape, F32),
            pltpu.VMEM((count, 128), F32),
            pltpu.VMEM((count, D), F32),
            pltpu.VMEM((count, D), F32),
            pltpu.VMEM(w_qkv.shape, BF16),
            pltpu.VMEM(w_proj.shape, BF16),
            pltpu.VMEM(w_in.shape, BF16),
            pltpu.VMEM(w_out.shape, BF16),
            pltpu.VMEM((count, D), BF16),
            pltpu.VMEM((count, 3 * D), BF16),
            pltpu.VMEM((WINDOWS * GROUPS, WIN, SPREAD), BF16),
            pltpu.VMEM((count, D), BF16),
            pltpu.VMEM((count, D), F32),
            pltpu.VMEM((count, D), BF16),
            pltpu.VMEM((count, D), F32),
            pltpu.VMEM((BLOCKS, D, D), BF16),
            pltpu.VMEM((count, D), F32),
            pltpu.VMEM((count, D), F32),
            pltpu.VMEM((count, D), BF16),
            pltpu.VMEM((count, D), BF16),
            pltpu.VMEM((count, D), BF16),
            pltpu.VMEM((WIN, SPREAD), BF16),
            pltpu.VMEM((2, HALO_ROWS, D), BF16),
            pltpu.VMEM((2, HALO_ROWS, D), BF16),
            pltpu.VMEM((HALO_ROWS, D), BF16),
            pltpu.VMEM((HALO_ROWS, D), BF16),
            pltpu.SemaphoreType.DMA((6,)),
            pltpu.SemaphoreType.DMA((2, 9)),
            pltpu.SemaphoreType.DMA((BLOCKS,)),
        ]
        + sum_scratch(),
        compiler_params=pltpu.CompilerParams(
            collective_id=0, has_side_effects=True, vmem_limit_bytes=63 * 1024 * 1024
        ),
        cost_estimate=pl.CostEstimate(flops=16 * 10**9, bytes_accessed=24 * 10**6, transcendentals=4 * 10**6),
        name="block",
    )(tokens, cotangent, region, w_qkv, w_proj, w_in, w_out)


def local(tokens, cotangent, region_ids, w_qkv, w_proj, w_in, w_out):
    grad_tokens, grads = block_call(
        tokens.transpose(1, 2, 0, 3), cotangent.transpose(1, 2, 0, 3), region_ids.transpose(1, 0, 2),
        w_qkv, w_proj, w_in, w_out,
    )
    grad_out, grad_in, grad_qkv, grad_proj, grad_tokens = unpack_call(grads, grad_tokens)
    return grad_tokens.transpose(2, 0, 1, 3), grad_qkv, grad_proj, grad_in, grad_out


def solution(mesh):
    grid = P(None, "lat", "lon", None)
    in_specs = (grid, grid, P(None, "lat", "lon"), P(), P(), P(), P())
    out_specs = (grid, P(), P(), P(), P())
    return jax.shard_map(local, mesh=mesh, in_specs=in_specs, out_specs=out_specs, check_vma=False)
```

```python
import functools

import jax
import jax.numpy as jnp
from jax import lax
from jax.experimental import pallas as pl
from jax.experimental.pallas import tpu as pltpu
from jax.sharding import PartitionSpec as P

D = 512
HEADS = 16
HEAD_DIM = D // HEADS
FFN = 2048
WLEV = 2
WLAT = 6
WLON = 12
WIN = WLEV * WLAT * WLON
GROUP = 8
LANES = GROUP * HEAD_DIM
GROUPS = HEADS // GROUP
SPREAD = GROUP * WIN
HALF_LAT = WLAT // 2
HALF_LON = WLON // 2
EPS = 1e-05
MASKED = -1e10
SCALE = HEAD_DIM ** -0.5
LOG2E = 1.4426950408889634
GELU_A = 0.7978845608028654
GELU_B = 0.044715
F32 = jnp.float32
BF16 = jnp.bfloat16


def nn(a, b):
    return lax.dot_general(a, b, (((1,), (0,)), ((), ())), preferred_element_type=F32)


def nt(a, b):
    return lax.dot_general(a, b, (((1,), (1,)), ((), ())), preferred_element_type=F32)


def norm_parts(v):
    centred = v - jnp.mean(v, axis=-1, keepdims=True)
    r = lax.rsqrt(jnp.mean(centred * centred, axis=-1, keepdims=True) + EPS)
    return centred * r, r


def norm_back(unit, r, g):
    return r * (g - jnp.mean(g, axis=-1, keepdims=True) - unit * jnp.mean(g * unit, axis=-1, keepdims=True))


def spread_heads(v):
    lane_head = lax.broadcasted_iota(jnp.int32, v.shape, 1) // HEAD_DIM
    zero = jnp.zeros_like(v)
    return jnp.concatenate([jnp.where(lane_head == h, v, zero) for h in range(GROUP)], axis=0)


def own_blocks(full):
    return jnp.concatenate(
        [full[HEAD_DIM * h : HEAD_DIM * (h + 1), WIN * h : WIN * (h + 1)] for h in range(GROUP)], axis=0
    )


BLOCKS = 12
OUT_BLOCKS = (0, 2, 4, 6)
IN_BLOCKS = (1, 3, 5, 7)
PROJ_BLOCK = 8
QKV_BLOCKS = (9, 10, 11)
UNITS = (
    (0, 2, "xyz", 1), (2, 2, "yzx", 1), (4, 2, "zxy", 1), (6, 2, "xyz", 3),
    (8, 1, "yzx", 0), (9, 1, "xyz", 0), (10, 1, "yzx", 0), (11, 1, "zxy", 0),
)
DIRECT = 8
SLOTS = 17


class Place:
    def __init__(self):
        lat, lon = lax.axis_index("lat"), lax.axis_index("lon")
        self.core = lon % 2
        self.at = {"x": (lon // 2) % 4, "y": (lon // 8) * 2 + lat % 2, "z": lat // 2}

    def mesh_id(self, at, core):
        return (at["z"] * 2 + at["y"] % 2, (at["y"] // 2) * 8 + at["x"] * 2 + core)

    def sibling(self):
        return self.mesh_id(self.at, 1 - self.core)

    def along(self, axis, step):
        at = dict(self.at)
        at[axis] = (at[axis] + step) % 4
        return self.mesh_id(at, self.core), at[axis]

    def across(self, axis, kind):
        at, c = dict(self.at), self.at[axis]
        at[axis] = c + 1 - 2 * (c % 2) if kind == 1 else 3 - c
        bit = ((c + 1) // 2) % 2 if kind == 1 else c // 2
        return self.mesh_id(at, self.core), bit


def greet(place, others=()):
    barrier = pltpu.get_barrier_semaphore()
    partners = [place.sibling()] + [place.along(a, s)[0] for a in "xyz" for s in (1, 2, 3)] + list(others)
    for partner in partners:
        pl.semaphore_signal(barrier, inc=1, device_id=partner, device_id_type=pl.DeviceIdType.MESH)
    pl.semaphore_wait(barrier, len(partners))


class Sum:
    def __init__(self, place, u, g, done, got, send, recv):
        self.first, self.count, order, first = UNITS[u]
        self.blocks = pl.ds(self.first, self.count)
        self.u, self.g, self.done, self.got, self.send, self.recv = u, g, done, got, send, recv
        self.stage, self.slots, self.copies = 0, 0, []
        self.steps, base, rows = [], 0, D

        def halve(name, target, bit, base, rows):
            rows //= 2
            self.steps.append((name, [(target, base + (1 - bit) * rows)], base + bit * rows, rows))
            return base + bit * rows, rows

        def quarter(name, axis, base, rows):
            rows //= 4
            peers = [place.along(axis, step) for step in (1, 2, 3)]
            self.steps.append((name, [(t, base + c * rows) for t, c in peers], base + place.at[axis] * rows, rows))
            return base + place.at[axis] * rows, rows

        base, rows = halve("core", place.sibling(), place.core, base, rows)
        if first:
            base, rows = halve("near", *place.across(order[0], first), base, rows)
            base, rows = halve("far", *place.across(order[0], 4 - first), base, rows)
        else:
            base, rows = quarter("axis", order[0], base, rows)
        base, rows = quarter("second", order[1], base, rows)
        peers = [place.along(order[2], step)[0] for step in (1, 2, 3)]
        self.swap = (peers, place.at[order[2]], base, rows)
        self.last = 2 * len(self.steps) + 1

    def part(self, ref, base, rows):
        return ref.at[self.blocks, pl.ds(pl.multiple_of(base, rows), rows), :]

    def copy(self, src, dst, target):
        slot = self.slots
        self.slots += 1
        one = pltpu.make_async_remote_copy(
            src_ref=src, dst_ref=dst, send_sem=self.send.at[self.u, slot], recv_sem=self.recv.at[self.u, slot],
            device_id=target, device_id_type=pl.DeviceIdType.MESH,
        )
        one.start()
        self.copies.append(one)

    def landing(self, name, i):
        if name == "axis":
            return self.got[name].at[i, pl.ds(self.first - DIRECT, self.count)]
        return self.got[name].at[i, self.blocks]

    def advance(self):
        n, stage = len(self.steps), self.stage
        self.stage += 1
        for one in self.copies:
            one.wait()
        self.copies = []
        if 1 <= stage <= n:
            name, targets, base, rows = self.steps[stage - 1]
            mine = self.part(self.g, base, rows)
            total = mine[...].astype(F32)
            for i in range(len(targets)):
                total = total + self.landing(name, i)[...].astype(F32)
            mine[...] = total.astype(BF16)
        if stage == n + 1:
            _, _, base, rows = self.swap
            four = [self.got["swap"][c, self.blocks].astype(F32) for c in range(4)]
            self.part(self.done, base, rows)[...] = ((four[0] + four[1]) + (four[2] + four[3])).astype(BF16)
        if stage < n:
            name, targets, _, rows = self.steps[stage]
            for i, (target, base) in enumerate(targets):
                self.copy(self.part(self.g, base, rows), self.landing(name, i), target)
        elif stage == n:
            targets, at, base, rows = self.swap
            mine = self.part(self.g, base, rows)
            self.got["swap"][at, self.blocks] = mine[...]
            for target in targets:
                self.copy(mine, self.got["swap"].at[at, self.blocks], target)
        elif stage <= 2 * n:
            _, targets, base, rows = self.steps[2 * n - stage]
            mine = self.part(self.done, base, rows)
            for target, _ in targets:
                self.copy(mine, mine, target)


LANDINGS = (
    ("core", (1, BLOCKS, D // 2, D)),
    ("near", (1, DIRECT, D // 4, D)),
    ("far", (1, DIRECT, D // 8, D)),
    ("axis", (3, BLOCKS - DIRECT, D // 8, D)),
    ("second", (3, BLOCKS, D // 32, D)),
    ("swap", (4, BLOCKS, D // 32, D)),
)


def sum_scratch():
    return [pltpu.VMEM(shape, BF16) for _, shape in LANDINGS] + [pltpu.SemaphoreType.DMA((len(UNITS), SLOTS))] * 2


def unpack_kernel(g_ref, tok_ref, out_ref, in_ref, qkv_ref, proj_ref, tok_out, half, full, lines_in, got, put, whole):
    def target(u):
        if u == PROJ_BLOCK:
            return proj_ref
        if u in OUT_BLOCKS:
            return out_ref.at[pl.ds(D * OUT_BLOCKS.index(u), D), :]
        if u in IN_BLOCKS:
            return in_ref.at[:, pl.ds(D * IN_BLOCKS.index(u), D)]
        return qkv_ref.at[:, pl.ds(D * QKV_BLOCKS.index(u), D)]

    ins = [pltpu.make_async_copy(g_ref.at[u], half.at[u], got.at[u]) for u in range(BLOCKS)]
    outs = [pltpu.make_async_copy(full.at[u], target(u), put.at[u]) for u in range(BLOCKS)]
    arrive = pltpu.make_async_copy(tok_ref, lines_in, whole.at[0])
    leave = pltpu.make_async_copy(lines_in, tok_out, whole.at[1])
    arrive.start()
    for one in ins:
        one.start()
    arrive.wait()
    leave.start()
    for u in range(BLOCKS):
        ins[u].wait()
        full[u] = half[u].astype(F32)
        outs[u].start()
    for one in outs:
        one.wait()
    leave.wait()


def unpack_call(grads, grad_tokens):
    anywhere = pl.BlockSpec(memory_space=pl.ANY)
    return pl.pallas_call(
        unpack_kernel,
        out_shape=tuple(jax.ShapeDtypeStruct(s, F32) for s in ((FFN, D), (D, FFN), (D, 3 * D), (D, D), grad_tokens.shape)),
        in_specs=[anywhere] * 2,
        out_specs=(anywhere,) * 5,
        scratch_shapes=[
            pltpu.VMEM((BLOCKS, D, D), BF16),
            pltpu.VMEM((BLOCKS, D, D), F32),
            pltpu.VMEM(grad_tokens.shape, F32),
            pltpu.SemaphoreType.DMA((BLOCKS,)),
            pltpu.SemaphoreType.DMA((BLOCKS,)),
            pltpu.SemaphoreType.DMA((2,)),
        ],
        compiler_params=pltpu.CompilerParams(vmem_limit_bytes=60 * 1024 * 1024),
        name="unpack",
    )(grads, grad_tokens)


LAT_ROWS, LON_ROWS = 64, 16
LAT_AT, LON_AT, DIAG_AT, HALO_ROWS = 0, 192, 336, 384
WINDOWS = 6
FEW = 144
TINY = 16
PIECE = 256
WIDE = 3
OWN_ROWS = 9
OWN_COLS = 30
STRIP = OWN_COLS * WLEV
EDGE = HALF_LON * WLEV
LINE = WLON * WLEV
HALO_PARTS = ((LAT_AT, LON_AT), (LON_AT, DIAG_AT), (DIAG_AT, HALO_ROWS))


def cell(row, wide):
    return ((row // WLAT) * WIDE + wide) * WIN + (row % WLAT) * LINE


def lines(v):
    return v.reshape(v.shape[0] * WLEV, D)


def cells(v):
    return v.reshape(v.shape[0] // WLEV, WLEV, D)


def padded(pieces, rows):
    have = sum(p.shape[0] for p in pieces)
    return jnp.concatenate(pieces + [jnp.zeros((rows - have, D), F32)], axis=0).astype(BF16)


def ahead_at(row):
    return DIAG_AT + row * LON_ROWS if row < HALF_LAT else LON_AT + (row - HALF_LAT) * LON_ROWS


def behind_at(row):
    return LON_AT + row * LON_ROWS if row < OWN_ROWS else DIAG_AT + (row - OWN_ROWS) * LON_ROWS


def pack_ahead(src, dst):
    for row in range(HALF_LAT):
        at = LAT_AT + row * LAT_ROWS
        dst[at : at + LAT_ROWS, :] = padded([lines(src[row, HALF_LON : HALF_LON + OWN_COLS])], LAT_ROWS)
    for row in range(HALF_LAT + OWN_ROWS):
        at = ahead_at(row)
        dst[at : at + LON_ROWS, :] = padded([lines(src[row, :HALF_LON])], LON_ROWS)


def place_strip(flat, row, strip):
    flat[cell(row, 0) : cell(row, 0) + LINE, :] = strip[:LINE]
    flat[cell(row, 1) : cell(row, 1) + LINE, :] = strip[LINE : 2 * LINE]
    flat[cell(row, 2) : cell(row, 2) + EDGE, :] = strip[2 * LINE : STRIP]


def take_strip(flat, row):
    return [
        flat[cell(row, 0) : cell(row, 0) + LINE, :],
        flat[cell(row, 1) : cell(row, 1) + LINE, :],
        flat[cell(row, 2) : cell(row, 2) + EDGE, :],
    ]


def place_own(src, flat):
    for row in range(OWN_ROWS):
        place_strip(flat, row, lines(src[row + HALF_LAT, HALF_LON : HALF_LON + OWN_COLS]))


def place_halo(got, flat):
    for row in range(HALF_LAT):
        at = LAT_AT + row * LAT_ROWS
        place_strip(flat, OWN_ROWS + row, got[at : at + LAT_ROWS, :].astype(F32))
    for row in range(OWN_ROWS + HALF_LAT):
        at, to = behind_at(row), cell(row, 2) + EDGE
        flat[to : to + EDGE, :] = got[at : at + LON_ROWS, :].astype(F32)[:EDGE]


def pack_back(flat, dst):
    for row in range(HALF_LAT):
        at = LAT_AT + row * LAT_ROWS
        dst[at : at + LAT_ROWS, :] = padded(take_strip(flat, OWN_ROWS + row), LAT_ROWS)
    for row in range(OWN_ROWS + HALF_LAT):
        at, end = behind_at(row), cell(row, 2) + EDGE
        dst[at : at + LON_ROWS, :] = padded([flat[end : end + EDGE, :]], LON_ROWS)


def return_own(flat, out):
    for row in range(OWN_ROWS):
        strip = jnp.concatenate(take_strip(flat, row), axis=0)
        out[row + HALF_LAT, HALF_LON : HALF_LON + OWN_COLS] = cells(strip)


def return_halo(got, out):
    for row in range(HALF_LAT + OWN_ROWS):
        at = ahead_at(row)
        out[row, :HALF_LON] = cells(got[at : at + LON_ROWS, :].astype(F32)[:EDGE])
    for row in range(HALF_LAT):
        at = LAT_AT + row * LAT_ROWS
        out[row, HALF_LON : HALF_LON + OWN_COLS] = cells(got[at : at + LAT_ROWS, :].astype(F32)[:STRIP])


def place_regions(region, flat):
    for row in range(HALF_LAT + OWN_ROWS):
        ids = region[row].astype(F32)
        levels = [jnp.broadcast_to(ids[l : l + 1], (128, ids.shape[1])).T for l in range(WLEV)]
        both = jnp.stack(levels[::-1], axis=1).reshape(ids.shape[1] * WLEV, 128)
        for wide in range(WIDE):
            flat[cell(row, wide) : cell(row, wide) + LINE, :] = both[LINE * wide : LINE * (wide + 1)]


QKV_UNITS = (5, 6, 7)
AFTER_CHUNK = ((0,), (0, 1), (1, 2), (0, 2, 3))
AFTER_PROJ = (4, 0, 1, 3)
AFTER_WINDOW = ((), (0, 1, 2, 4), (3,), (0, 1, 2), (4,), (0, 1, 2, 3))
AFTER_QKV = (4,)
AFTER_INPUT = (5, 6, 7, 0, 1, 2, 3)
AFTER_NORM = (4,)


def block_kernel(
    tokens, cotangent, region, wqkv, wproj, win, wout,
    out_ref, done_hbm,
    done_ref, cot_ref, region_ref, x_ref, c_ref, wqkv_ref, wproj_ref, win_ref, wout_ref,
    normed, packed, probs, mixed, mid, nmid, dnm, g_ref,
    pre, dact, act, dpre, cot_half, dscores,
    halo_out, halo_in, back_out, back_in, load_sem, halo_sem, done_sem, *landings_and_sems,
):
    place = Place()
    *landings, send, recv = landings_and_sems
    got = {name: ref for (name, _), ref in zip(LANDINGS, landings)}
    sums = [Sum(place, u, g_ref, done_ref, got, send, recv) for u in range(len(UNITS))]

    leaving = [
        pltpu.make_async_copy(done_ref.at[one.blocks], done_hbm.at[one.blocks], done_sem.at[one.u]) for one in sums
    ]

    def tick(*blocks):
        for u in blocks:
            sums[u].advance()
            if sums[u].stage == sums[u].last + 1:
                leaving[u].start()

    loads = [
        pltpu.make_async_copy(src, dst, load_sem.at[i])
        for i, (src, dst) in enumerate(
            ((tokens, out_ref), (cotangent, cot_ref), (wqkv, wqkv_ref), (wproj, wproj_ref), (win, win_ref), (wout, wout_ref))
        )
    ]
    for one in loads:
        one.start()

    lat, lon = lax.axis_index("lat"), lax.axis_index("lon")
    lats, lons = lax.axis_size("lat"), lax.axis_size("lon")
    up, down = lax.rem(lat + lats - 1, lats), lax.rem(lat + 1, lats)
    left, right = lax.rem(lon + lons - 1, lons), lax.rem(lon + 1, lons)
    ahead = ((up, lon), (lat, left), (up, left))
    back = ((down, lon), (lat, right), (down, right))
    greet(place, ahead + back)

    def exchange(src, dst, targets, at):
        copies = []
        for i, (lo, hi) in enumerate(HALO_PARTS):
            one = pltpu.make_async_remote_copy(
                src_ref=src.at[lo:hi], dst_ref=dst.at[lo:hi],
                send_sem=halo_sem.at[0, at + i], recv_sem=halo_sem.at[1, at + i],
                device_id=targets[i], device_id_type=pl.DeviceIdType.MESH,
            )
            one.start()
            copies.append(one)
        return copies

    loads[0].wait()
    pack_ahead(out_ref, halo_out.at[0])
    token_halo = exchange(halo_out.at[0], halo_in.at[0], ahead, 0)
    loads[1].wait()
    pack_ahead(cot_ref, halo_out.at[1])
    cot_halo = exchange(halo_out.at[1], halo_in.at[1], ahead, 3)
    place_own(out_ref, x_ref)
    place_regions(region, region_ref)

    rows_of = lambda w: pl.ds(pl.multiple_of(w * WIN, WIN), WIN)
    few_of = lambda i: pl.ds(pl.multiple_of(i * FEW, FEW), FEW)
    fews = WIN // FEW
    pieces = [(c, min(c + PIECE, SPREAD)) for c in range(0, SPREAD, PIECE)]

    def attention_forward(first, last):
        @pl.loop(first * fews, last * fews)
        def _(i):
            unit, _ = norm_parts(x_ref[few_of(i), :])
            normed[few_of(i), :] = unit.astype(BF16)

        if first == 0:
            loads[2].wait()
        rows = slice(first * WIN, last * WIN)
        for j in range(3):
            cols = slice(D * j, D * (j + 1))
            packed[rows, cols] = nn(normed[rows, :], wqkv_ref[:, cols]).astype(BF16)

        @pl.loop(first, last)
        def _(w):
            rows = rows_of(w)
            ids = region_ref[rows, :]
            of_key, of_query = ids[:, :1], jnp.concatenate([ids.T[:1]] * GROUP, axis=1)
            for g in range(GROUPS):
                lo = LANES * g
                q = packed[rows, lo : lo + LANES]
                k = packed[rows, D + lo : D + lo + LANES]
                v = packed[rows, 2 * D + lo : 2 * D + lo + LANES]
                q = spread_heads(q)
                for c0, c1 in pieces:
                    s = jnp.where(of_key == of_query[:, c0:c1], nt(k, q[c0:c1]), MASKED)
                    e = jnp.exp2((s - jnp.max(s, axis=0, keepdims=True)) * (SCALE * LOG2E))
                    p = e * (1.0 / jnp.sum(e, axis=0, keepdims=True))
                    probs[w * GROUPS + g, :, c0:c1] = p.astype(BF16)
                mixed[rows, lo : lo + LANES] = own_blocks(nn(v.T, probs[w * GROUPS + g])).T.astype(BF16)

    attention_forward(0, 2)
    for one in token_halo:
        one.wait()
    place_halo(halo_in.at[0], x_ref)
    attention_forward(2, WINDOWS)

    loads[3].wait()
    mid[...] = nn(mixed[...], wproj_ref[...]).astype(BF16).astype(F32)

    @pl.loop(0, WINDOWS * fews)
    def _(i):
        rows = few_of(i)
        middle = x_ref[rows, :] + mid[rows, :]
        mid[rows, :] = middle
        nmid[rows, :] = norm_parts(middle)[0].astype(BF16)

    place_own(cot_ref, c_ref)
    for one in cot_halo:
        one.wait()
    place_halo(halo_in.at[1], c_ref)
    loads[4].wait()
    loads[5].wait()

    nmid_t = nmid[...].T
    cot_half[...] = c_ref[...].astype(BF16)
    for j in range(FFN // D):
        cols = slice(D * j, D * (j + 1))
        pre[...] = nn(nmid[...], win_ref[:, cols])
        dact[...] = nt(cot_half[...], wout_ref[cols, :])

        @pl.loop(0, WINDOWS * WIN // TINY, unroll=9)
        def _(i):
            rows = pl.ds(pl.multiple_of(i * TINY, TINY), TINY)
            u = pre[rows, :]
            square = u * u
            t = jnp.tanh(u * (GELU_A + (GELU_A * GELU_B) * square))
            half = 0.5 + 0.5 * t
            act[rows, :] = (u * half).astype(BF16)
            slope = half + u * (0.5 - 0.5 * t * t) * (GELU_A + (3 * GELU_A * GELU_B) * square)
            dpre[rows, :] = (slope * dact[rows, :]).astype(BF16)

        g_ref[OUT_BLOCKS[j]] = nn(act[...].T, cot_half[...]).astype(BF16)
        g_ref[IN_BLOCKS[j]] = nn(nmid_t, dpre[...]).astype(BF16)
        part = nt(dpre[...], win_ref[:, cols])
        if j == 0:
            dnm[...] = part
        else:
            dnm[...] += part
        tick(*AFTER_CHUNK[j])

    @pl.loop(0, WINDOWS * fews)
    def _(i):
        rows = few_of(i)
        unit, r = norm_parts(mid[rows, :])
        d_mid = c_ref[rows, :] + norm_back(unit, r, dnm[rows, :])
        c_ref[rows, :] = d_mid
        nmid[rows, :] = d_mid.astype(BF16)

    g_ref[PROJ_BLOCK] = nn(mixed[...].T, nmid[...]).astype(BF16)
    tick(*AFTER_PROJ)
    mixed[...] = nt(nmid[...], wproj_ref[...]).astype(BF16)

    for w in range(WINDOWS):

        @pl.loop(w, w + 1)
        def _(w):
            rows = rows_of(w)
            for g in range(GROUPS):
                lo = LANES * g
                q = spread_heads(packed[rows, lo : lo + LANES])
                k = packed[rows, D + lo : D + lo + LANES]
                v = packed[rows, 2 * D + lo : 2 * D + lo + LANES]
                do = spread_heads(mixed[rows, lo : lo + LANES])
                p = probs[w * GROUPS + g]
                for c0, c1 in pieces:
                    dp = nt(v, do[c0:c1])
                    pf = probs[w * GROUPS + g, :, c0:c1].astype(F32)
                    total = jnp.sum(dp * pf, axis=0, keepdims=True)
                    dscores[:, c0:c1] = (pf * (dp - total) * SCALE).astype(BF16)
                ds = dscores[...]
                packed[rows, lo : lo + LANES] = own_blocks(nn(k.T, ds)).T.astype(BF16)
                packed[rows, D + lo : D + lo + LANES] = nn(ds, q).astype(BF16)
                packed[rows, 2 * D + lo : 2 * D + lo + LANES] = nn(p, do).astype(BF16)

        tick(*AFTER_WINDOW[w])

    normed_t = normed[...].T
    for j in range(3):
        g_ref[QKV_BLOCKS[j]] = nn(normed_t, packed[:, D * j : D * (j + 1)]).astype(BF16)
        tick(QKV_UNITS[j])
    tick(*AFTER_QKV)
    for j in range(3):
        cols = slice(D * j, D * (j + 1))
        part = nt(packed[:, cols], wqkv_ref[:, cols])
        if j == 0:
            dnm[...] = part
        else:
            dnm[...] += part
    tick(*AFTER_INPUT)

    @pl.loop(0, WINDOWS * fews)
    def _(i):
        rows = few_of(i)
        unit, r = norm_parts(x_ref[rows, :])
        c_ref[rows, :] = c_ref[rows, :] + norm_back(unit, r, dnm[rows, :])

    tick(*AFTER_NORM)
    pack_back(c_ref, back_out)
    grad_halo = exchange(back_out, back_in, back, 6)
    return_own(c_ref, out_ref)

    rounds = 0
    while any(one.stage <= one.last for one in sums):
        tick(*(u for u in (*QKV_UNITS, 0, 1, 2, 3, 4) if sums[u].stage <= sums[u].last))
        rounds += 1
        if rounds == 2:
            for one in grad_halo:
                one.wait()
            return_halo(back_in, out_ref)
    for one in leaving:
        one.wait()


def block_call(tokens, cotangent, region, w_qkv, w_proj, w_in, w_out):
    anywhere, vmem = pl.BlockSpec(memory_space=pl.ANY), pl.BlockSpec(memory_space=pltpu.VMEM)
    count = WINDOWS * WIN
    return pl.pallas_call(
        block_kernel,
        out_shape=(jax.ShapeDtypeStruct(tokens.shape, F32), jax.ShapeDtypeStruct((BLOCKS, D, D), BF16)),
        in_specs=[anywhere, anywhere, vmem] + [anywhere] * 4,
        out_specs=(vmem, anywhere),
        scratch_shapes=[
            pltpu.VMEM((BLOCKS, D, D), BF16),
            pltpu.VMEM(tokens.shape, F32),
            pltpu.VMEM((count, 128), F32),
            pltpu.VMEM((count, D), F32),
            pltpu.VMEM((count, D), F32),
            pltpu.VMEM(w_qkv.shape, BF16),
            pltpu.VMEM(w_proj.shape, BF16),
            pltpu.VMEM(w_in.shape, BF16),
            pltpu.VMEM(w_out.shape, BF16),
            pltpu.VMEM((count, D), BF16),
            pltpu.VMEM((count, 3 * D), BF16),
            pltpu.VMEM((WINDOWS * GROUPS, WIN, SPREAD), BF16),
            pltpu.VMEM((count, D), BF16),
            pltpu.VMEM((count, D), F32),
            pltpu.VMEM((count, D), BF16),
            pltpu.VMEM((count, D), F32),
            pltpu.VMEM((BLOCKS, D, D), BF16),
            pltpu.VMEM((count, D), F32),
            pltpu.VMEM((count, D), F32),
            pltpu.VMEM((count, D), BF16),
            pltpu.VMEM((count, D), BF16),
            pltpu.VMEM((count, D), BF16),
            pltpu.VMEM((WIN, SPREAD), BF16),
            pltpu.VMEM((2, HALO_ROWS, D), BF16),
            pltpu.VMEM((2, HALO_ROWS, D), BF16),
            pltpu.VMEM((HALO_ROWS, D), BF16),
            pltpu.VMEM((HALO_ROWS, D), BF16),
            pltpu.SemaphoreType.DMA((6,)),
            pltpu.SemaphoreType.DMA((2, 9)),
            pltpu.SemaphoreType.DMA((len(UNITS),)),
        ]
        + sum_scratch(),
        compiler_params=pltpu.CompilerParams(
            collective_id=0, has_side_effects=True, vmem_limit_bytes=63 * 1024 * 1024
        ),
        cost_estimate=pl.CostEstimate(flops=16 * 10**9, bytes_accessed=24 * 10**6, transcendentals=4 * 10**6),
        name="block",
    )(tokens, cotangent, region, w_qkv, w_proj, w_in, w_out)


def local(tokens, cotangent, region_ids, w_qkv, w_proj, w_in, w_out):
    grad_tokens, grads = block_call(
        tokens.transpose(1, 2, 0, 3), cotangent.transpose(1, 2, 0, 3), region_ids.transpose(1, 0, 2),
        w_qkv, w_proj, w_in, w_out,
    )
    grad_out, grad_in, grad_qkv, grad_proj, grad_tokens = unpack_call(grads, grad_tokens)
    return grad_tokens.transpose(2, 0, 1, 3), grad_qkv, grad_proj, grad_in, grad_out


def solution(mesh):
    grid = P(None, "lat", "lon", None)
    in_specs = (grid, grid, P(None, "lat", "lon"), P(), P(), P(), P())
    out_specs = (grid, P(), P(), P(), P())
    return jax.shard_map(local, mesh=mesh, in_specs=in_specs, out_specs=out_specs, check_vma=False)
```

```python
import functools

import jax
import jax.numpy as jnp
from jax import lax
from jax.experimental import pallas as pl
from jax.experimental.pallas import tpu as pltpu
from jax.sharding import PartitionSpec as P

D = 512
HEADS = 16
HEAD_DIM = D // HEADS
FFN = 2048
WLEV = 2
WLAT = 6
WLON = 12
WIN = WLEV * WLAT * WLON
GROUP = 8
LANES = GROUP * HEAD_DIM
GROUPS = HEADS // GROUP
SPREAD = GROUP * WIN
HALF_LAT = WLAT // 2
HALF_LON = WLON // 2
EPS = 1e-05
MASKED = -1e10
SCALE = HEAD_DIM ** -0.5
LOG2E = 1.4426950408889634
GELU_A = 0.7978845608028654
GELU_B = 0.044715
F32 = jnp.float32
BF16 = jnp.bfloat16


def nn(a, b):
    return lax.dot_general(a, b, (((1,), (0,)), ((), ())), preferred_element_type=F32)


def nt(a, b):
    return lax.dot_general(a, b, (((1,), (1,)), ((), ())), preferred_element_type=F32)


def norm_parts(v):
    centred = v - jnp.mean(v, axis=-1, keepdims=True)
    r = lax.rsqrt(jnp.mean(centred * centred, axis=-1, keepdims=True) + EPS)
    return centred * r, r


def norm_back(unit, r, g):
    return r * (g - jnp.mean(g, axis=-1, keepdims=True) - unit * jnp.mean(g * unit, axis=-1, keepdims=True))


def spread_heads(v):
    lane_head = lax.broadcasted_iota(jnp.int32, v.shape, 1) // HEAD_DIM
    zero = jnp.zeros_like(v)
    return jnp.concatenate([jnp.where(lane_head == h, v, zero) for h in range(GROUP)], axis=0)


def own_blocks(full):
    return jnp.concatenate(
        [full[HEAD_DIM * h : HEAD_DIM * (h + 1), WIN * h : WIN * (h + 1)] for h in range(GROUP)], axis=0
    )


BLOCKS = 12
OUT_BLOCKS = (0, 2, 4, 6)
IN_BLOCKS = (1, 3, 5, 7)
PROJ_BLOCK = 8
QKV_BLOCKS = (9, 10, 11)
ROUTES = (
    ("xyz", 1), ("yzx", 1), ("zxy", 1), ("xyz", 3), ("yzx", 3), ("zxy", 3),
    ("xyz", 1), ("yzx", 1), ("zxy", 0),
    ("xyz", 0), ("yzx", 0), ("zxy", 0),
)
SLOTS = 17


class Place:
    def __init__(self):
        lat, lon = lax.axis_index("lat"), lax.axis_index("lon")
        self.core = lon % 2
        self.at = {"x": (lon // 2) % 4, "y": (lon // 8) * 2 + lat % 2, "z": lat // 2}

    def mesh_id(self, at, core):
        return (at["z"] * 2 + at["y"] % 2, (at["y"] // 2) * 8 + at["x"] * 2 + core)

    def sibling(self):
        return self.mesh_id(self.at, 1 - self.core)

    def along(self, axis, step):
        at = dict(self.at)
        at[axis] = (at[axis] + step) % 4
        return self.mesh_id(at, self.core), at[axis]

    def across(self, axis, kind):
        at, c = dict(self.at), self.at[axis]
        at[axis] = c + 1 - 2 * (c % 2) if kind == 1 else 3 - c
        bit = ((c + 1) // 2) % 2 if kind == 1 else c // 2
        return self.mesh_id(at, self.core), bit


def greet(place, others=()):
    barrier = pltpu.get_barrier_semaphore()
    partners = [place.sibling()] + [place.along(a, s)[0] for a in "xyz" for s in (1, 2, 3)] + list(others)
    for partner in partners:
        pl.semaphore_signal(barrier, inc=1, device_id=partner, device_id_type=pl.DeviceIdType.MESH)
    pl.semaphore_wait(barrier, len(partners))


class Sum:
    def __init__(self, place, u, g, done, got, send, recv):
        self.u, self.g, self.done, self.got, self.send, self.recv = u, g, done, got, send, recv
        self.stage, self.slots, self.copies = 0, 0, []
        order, first = ROUTES[u]
        self.steps, base, rows = [], 0, D

        def halve(name, target, bit, base, rows):
            rows //= 2
            self.steps.append((name, [(target, base + (1 - bit) * rows)], base + bit * rows, rows))
            return base + bit * rows, rows

        def quarter(name, axis, base, rows):
            rows //= 4
            peers = [place.along(axis, step) for step in (1, 2, 3)]
            self.steps.append((name, [(t, base + c * rows) for t, c in peers], base + place.at[axis] * rows, rows))
            return base + place.at[axis] * rows, rows

        base, rows = halve("core", place.sibling(), place.core, base, rows)
        if first:
            base, rows = halve("near", *place.across(order[0], first), base, rows)
            base, rows = halve("far", *place.across(order[0], 4 - first), base, rows)
        else:
            base, rows = quarter("axis", order[0], base, rows)
        base, rows = quarter("second", order[1], base, rows)
        peers = [place.along(order[2], step)[0] for step in (1, 2, 3)]
        self.swap = (peers, place.at[order[2]], base, rows)
        self.last = 2 * len(self.steps) + 1

    def part(self, ref, base, rows):
        return ref.at[self.u, pl.ds(pl.multiple_of(base, rows), rows), :]

    def copy(self, src, dst, target):
        slot = self.slots
        self.slots += 1
        one = pltpu.make_async_remote_copy(
            src_ref=src, dst_ref=dst, send_sem=self.send.at[self.u, slot], recv_sem=self.recv.at[self.u, slot],
            device_id=target, device_id_type=pl.DeviceIdType.MESH,
        )
        one.start()
        self.copies.append(one)

    def landing(self, name, i):
        if name == "axis":
            return self.got[name].at[i, self.u - PROJ_BLOCK]
        return self.got[name].at[i, self.u]

    def advance(self):
        n, stage = len(self.steps), self.stage
        self.stage += 1
        for one in self.copies:
            one.wait()
        self.copies = []
        if 1 <= stage <= n:
            name, targets, base, rows = self.steps[stage - 1]
            mine = self.part(self.g, base, rows)
            total = mine[...].astype(F32)
            for i in range(len(targets)):
                total = total + self.landing(name, i)[...].astype(F32)
            mine[...] = total.astype(BF16)
        if stage == n + 1:
            _, _, base, rows = self.swap
            four = [self.got["swap"][c, self.u].astype(F32) for c in range(4)]
            self.part(self.done, base, rows)[...] = ((four[0] + four[1]) + (four[2] + four[3])).astype(BF16)
        if stage < n:
            name, targets, _, rows = self.steps[stage]
            for i, (target, base) in enumerate(targets):
                self.copy(self.part(self.g, base, rows), self.landing(name, i), target)
        elif stage == n:
            targets, at, base, rows = self.swap
            mine = self.part(self.g, base, rows)
            self.got["swap"][at, self.u] = mine[...]
            for target in targets:
                self.copy(mine, self.got["swap"].at[at, self.u], target)
        elif stage <= 2 * n:
            _, targets, base, rows = self.steps[2 * n - stage]
            mine = self.part(self.done, base, rows)
            for target, _ in targets:
                self.copy(mine, mine, target)


LANDINGS = (
    ("core", (1, BLOCKS, D // 2, D)),
    ("near", (1, BLOCKS - 3, D // 4, D)),
    ("far", (1, BLOCKS - 3, D // 8, D)),
    ("axis", (3, 4, D // 8, D)),
    ("second", (3, BLOCKS, D // 32, D)),
    ("swap", (4, BLOCKS, D // 32, D)),
)


def sum_scratch():
    return [pltpu.VMEM(shape, BF16) for _, shape in LANDINGS] + [pltpu.SemaphoreType.DMA((BLOCKS, SLOTS))] * 2


def unpack_kernel(g_ref, tok_ref, out_ref, in_ref, qkv_ref, proj_ref, tok_out, half, full, lines_in, got, put, whole):
    def target(u):
        if u == PROJ_BLOCK:
            return proj_ref
        if u in OUT_BLOCKS:
            return out_ref.at[pl.ds(D * OUT_BLOCKS.index(u), D), :]
        if u in IN_BLOCKS:
            return in_ref.at[:, pl.ds(D * IN_BLOCKS.index(u), D)]
        return qkv_ref.at[:, pl.ds(D * QKV_BLOCKS.index(u), D)]

    ins = [pltpu.make_async_copy(g_ref.at[u], half.at[u], got.at[u]) for u in range(BLOCKS)]
    outs = [pltpu.make_async_copy(full.at[u], target(u), put.at[u]) for u in range(BLOCKS)]
    arrive = pltpu.make_async_copy(tok_ref, lines_in, whole.at[0])
    leave = pltpu.make_async_copy(lines_in, tok_out, whole.at[1])
    arrive.start()
    for one in ins:
        one.start()
    arrive.wait()
    leave.start()
    for u in range(BLOCKS):
        ins[u].wait()
        full[u] = half[u].astype(F32)
        outs[u].start()
    for one in outs:
        one.wait()
    leave.wait()


def unpack_call(grads, grad_tokens):
    anywhere = pl.BlockSpec(memory_space=pl.ANY)
    return pl.pallas_call(
        unpack_kernel,
        out_shape=tuple(jax.ShapeDtypeStruct(s, F32) for s in ((FFN, D), (D, FFN), (D, 3 * D), (D, D), grad_tokens.shape)),
        in_specs=[anywhere] * 2,
        out_specs=(anywhere,) * 5,
        scratch_shapes=[
            pltpu.VMEM((BLOCKS, D, D), BF16),
            pltpu.VMEM((BLOCKS, D, D), F32),
            pltpu.VMEM(grad_tokens.shape, F32),
            pltpu.SemaphoreType.DMA((BLOCKS,)),
            pltpu.SemaphoreType.DMA((BLOCKS,)),
            pltpu.SemaphoreType.DMA((2,)),
        ],
        compiler_params=pltpu.CompilerParams(vmem_limit_bytes=60 * 1024 * 1024),
        name="unpack",
    )(grads, grad_tokens)


LAT_ROWS, LON_ROWS = 64, 16
LAT_AT, LON_AT, DIAG_AT, HALO_ROWS = 0, 192, 336, 384
WINDOWS = 6
FEW = 144
WIDE = 3
OWN_ROWS = 9
OWN_COLS = 30
STRIP = OWN_COLS * WLEV
EDGE = HALF_LON * WLEV
LINE = WLON * WLEV
HALO_PARTS = ((LAT_AT, LON_AT), (LON_AT, DIAG_AT), (DIAG_AT, HALO_ROWS))


def cell(row, wide):
    return ((row // WLAT) * WIDE + wide) * WIN + (row % WLAT) * LINE


def lines(v):
    return v.reshape(v.shape[0] * WLEV, D)


def cells(v):
    return v.reshape(v.shape[0] // WLEV, WLEV, D)


def padded(pieces, rows):
    have = sum(p.shape[0] for p in pieces)
    return jnp.concatenate(pieces + [jnp.zeros((rows - have, D), F32)], axis=0).astype(BF16)


def ahead_at(row):
    return DIAG_AT + row * LON_ROWS if row < HALF_LAT else LON_AT + (row - HALF_LAT) * LON_ROWS


def behind_at(row):
    return LON_AT + row * LON_ROWS if row < OWN_ROWS else DIAG_AT + (row - OWN_ROWS) * LON_ROWS


def pack_ahead(src, dst):
    for row in range(HALF_LAT):
        at = LAT_AT + row * LAT_ROWS
        dst[at : at + LAT_ROWS, :] = padded([lines(src[row, HALF_LON : HALF_LON + OWN_COLS])], LAT_ROWS)
    for row in range(HALF_LAT + OWN_ROWS):
        at = ahead_at(row)
        dst[at : at + LON_ROWS, :] = padded([lines(src[row, :HALF_LON])], LON_ROWS)


def place_strip(flat, row, strip):
    flat[cell(row, 0) : cell(row, 0) + LINE, :] = strip[:LINE]
    flat[cell(row, 1) : cell(row, 1) + LINE, :] = strip[LINE : 2 * LINE]
    flat[cell(row, 2) : cell(row, 2) + EDGE, :] = strip[2 * LINE : STRIP]


def take_strip(flat, row):
    return [
        flat[cell(row, 0) : cell(row, 0) + LINE, :],
        flat[cell(row, 1) : cell(row, 1) + LINE, :],
        flat[cell(row, 2) : cell(row, 2) + EDGE, :],
    ]


def place_own(src, flat):
    for row in range(OWN_ROWS):
        place_strip(flat, row, lines(src[row + HALF_LAT, HALF_LON : HALF_LON + OWN_COLS]))


def place_halo(got, flat):
    for row in range(HALF_LAT):
        at = LAT_AT + row * LAT_ROWS
        place_strip(flat, OWN_ROWS + row, got[at : at + LAT_ROWS, :].astype(F32))
    for row in range(OWN_ROWS + HALF_LAT):
        at, to = behind_at(row), cell(row, 2) + EDGE
        flat[to : to + EDGE, :] = got[at : at + LON_ROWS, :].astype(F32)[:EDGE]


def pack_back(flat, dst):
    for row in range(HALF_LAT):
        at = LAT_AT + row * LAT_ROWS
        dst[at : at + LAT_ROWS, :] = padded(take_strip(flat, OWN_ROWS + row), LAT_ROWS)
    for row in range(OWN_ROWS + HALF_LAT):
        at, end = behind_at(row), cell(row, 2) + EDGE
        dst[at : at + LON_ROWS, :] = padded([flat[end : end + EDGE, :]], LON_ROWS)


def return_own(flat, out):
    for row in range(OWN_ROWS):
        strip = jnp.concatenate(take_strip(flat, row), axis=0)
        out[row + HALF_LAT, HALF_LON : HALF_LON + OWN_COLS] = cells(strip)


def return_halo(got, out):
    for row in range(HALF_LAT + OWN_ROWS):
        at = ahead_at(row)
        out[row, :HALF_LON] = cells(got[at : at + LON_ROWS, :].astype(F32)[:EDGE])
    for row in range(HALF_LAT):
        at = LAT_AT + row * LAT_ROWS
        out[row, HALF_LON : HALF_LON + OWN_COLS] = cells(got[at : at + LAT_ROWS, :].astype(F32)[:STRIP])


def place_regions(region, flat):
    for row in range(HALF_LAT + OWN_ROWS):
        ids = region[row].astype(F32)
        levels = [jnp.broadcast_to(ids[l : l + 1], (128, ids.shape[1])).T for l in range(WLEV)]
        both = jnp.stack(levels[::-1], axis=1).reshape(ids.shape[1] * WLEV, 128)
        for wide in range(WIDE):
            flat[cell(row, wide) : cell(row, wide) + LINE, :] = both[LINE * wide : LINE * (wide + 1)]


AFTER_CHUNK = ((0, 1), (0, 1, 2, 3), (2, 3, 4, 5), (0, 1, 4, 5, 6, 7))
AFTER_PROJ = (8, 0, 1, 2, 3, 6, 7)
AFTER_WINDOW = ((4, 5), (0, 1, 2, 3, 8), (4, 5, 6, 7), (0, 1, 2, 3), (4, 5, 6, 7, 8), (0, 1, 2, 3))
AFTER_QKV = (4, 5, 6, 7, 8)
AFTER_INPUT = (9, 10, 11, 0, 1, 2, 3)
AFTER_NORM = (4, 5, 6, 7, 8)


def block_kernel(
    tokens, cotangent, region, wqkv, wproj, win, wout,
    out_ref, done_hbm,
    done_ref, cot_ref, region_ref, x_ref, c_ref, wqkv_ref, wproj_ref, win_ref, wout_ref,
    normed, packed, probs, mixed, mid, nmid, dnm, g_ref,
    halo_out, halo_in, back_out, back_in, load_sem, halo_sem, done_sem, *landings_and_sems,
):
    place = Place()
    *landings, send, recv = landings_and_sems
    got = {name: ref for (name, _), ref in zip(LANDINGS, landings)}
    sums = [Sum(place, u, g_ref, done_ref, got, send, recv) for u in range(BLOCKS)]

    leaving = {u: pltpu.make_async_copy(done_ref.at[u], done_hbm.at[u], done_sem.at[u]) for u in range(BLOCKS)}

    def tick(*blocks):
        for u in blocks:
            sums[u].advance()
            if sums[u].stage == sums[u].last + 1:
                leaving[u].start()

    loads = [
        pltpu.make_async_copy(src, dst, load_sem.at[i])
        for i, (src, dst) in enumerate(
            ((tokens, out_ref), (cotangent, cot_ref), (wqkv, wqkv_ref), (wproj, wproj_ref), (win, win_ref), (wout, wout_ref))
        )
    ]
    for one in loads:
        one.start()

    lat, lon = lax.axis_index("lat"), lax.axis_index("lon")
    lats, lons = lax.axis_size("lat"), lax.axis_size("lon")
    up, down = lax.rem(lat + lats - 1, lats), lax.rem(lat + 1, lats)
    left, right = lax.rem(lon + lons - 1, lons), lax.rem(lon + 1, lons)
    ahead = ((up, lon), (lat, left), (up, left))
    back = ((down, lon), (lat, right), (down, right))
    greet(place, ahead + back)

    def exchange(src, dst, targets, at):
        copies = []
        for i, (lo, hi) in enumerate(HALO_PARTS):
            one = pltpu.make_async_remote_copy(
                src_ref=src.at[lo:hi], dst_ref=dst.at[lo:hi],
                send_sem=halo_sem.at[0, at + i], recv_sem=halo_sem.at[1, at + i],
                device_id=targets[i], device_id_type=pl.DeviceIdType.MESH,
            )
            one.start()
            copies.append(one)
        return copies

    loads[0].wait()
    pack_ahead(out_ref, halo_out.at[0])
    token_halo = exchange(halo_out.at[0], halo_in.at[0], ahead, 0)
    place_own(out_ref, x_ref)
    place_regions(region, region_ref)

    rows_of = lambda w: pl.ds(pl.multiple_of(w * WIN, WIN), WIN)
    few_of = lambda i: pl.ds(pl.multiple_of(i * FEW, FEW), FEW)
    fews = WIN // FEW

    def attention_forward(first, last):
        @pl.loop(first * fews, last * fews)
        def _(i):
            unit, _ = norm_parts(x_ref[few_of(i), :])
            normed[few_of(i), :] = unit.astype(BF16)

        if first == 0:
            loads[2].wait()
        rows = slice(first * WIN, last * WIN)
        for j in range(3):
            cols = slice(D * j, D * (j + 1))
            packed[rows, cols] = nn(normed[rows, :], wqkv_ref[:, cols]).astype(BF16)

        @pl.loop(first, last)
        def _(w):
            rows = rows_of(w)
            ids = region_ref[rows, :]
            allowed = ids[:, :1] == jnp.concatenate([ids.T[:1]] * GROUP, axis=1)
            for g in range(GROUPS):
                lo = LANES * g
                q = packed[rows, lo : lo + LANES]
                k = packed[rows, D + lo : D + lo + LANES]
                v = packed[rows, 2 * D + lo : 2 * D + lo + LANES]
                s = jnp.where(allowed, nt(k, spread_heads(q)), MASKED)
                e = jnp.exp2((s - jnp.max(s, axis=0, keepdims=True)) * (SCALE * LOG2E))
                p = (e * (1.0 / jnp.sum(e, axis=0, keepdims=True))).astype(BF16)
                probs[w * GROUPS + g] = p
                mixed[rows, lo : lo + LANES] = own_blocks(nn(v.T, p)).T.astype(BF16)

    attention_forward(0, 2)
    loads[1].wait()
    pack_ahead(cot_ref, halo_out.at[1])
    for one in token_halo:
        one.wait()
    cot_halo = exchange(halo_out.at[1], halo_in.at[1], ahead, 3)
    place_halo(halo_in.at[0], x_ref)
    attention_forward(2, WINDOWS)

    loads[3].wait()
    mid[...] = nn(mixed[...], wproj_ref[...]).astype(BF16).astype(F32)

    @pl.loop(0, WINDOWS * fews)
    def _(i):
        rows = few_of(i)
        middle = x_ref[rows, :] + mid[rows, :]
        mid[rows, :] = middle
        nmid[rows, :] = norm_parts(middle)[0].astype(BF16)

    place_own(cot_ref, c_ref)
    for one in cot_halo:
        one.wait()
    place_halo(halo_in.at[1], c_ref)
    loads[4].wait()
    loads[5].wait()

    nmid_t = nmid[...].T
    for j in range(FFN // D):
        cols = slice(D * j, D * (j + 1))
        cot = c_ref[...].astype(BF16)
        u = nn(nmid[...], win_ref[:, cols])
        da = nt(cot, wout_ref[cols, :])
        square = u * u
        t = jnp.tanh(u * (GELU_A + (GELU_A * GELU_B) * square))
        half = 0.5 + 0.5 * t
        act = (u * half).astype(BF16)
        slope = half + u * (0.5 - 0.5 * t * t) * (GELU_A + (3 * GELU_A * GELU_B) * square)
        dpre = (slope * da).astype(BF16)
        g_ref[OUT_BLOCKS[j]] = nn(act.T, cot).astype(BF16)
        g_ref[IN_BLOCKS[j]] = nn(nmid_t, dpre).astype(BF16)
        part = nt(dpre, win_ref[:, cols])
        if j == 0:
            dnm[...] = part
        else:
            dnm[...] += part
        tick(*AFTER_CHUNK[j])

    @pl.loop(0, WINDOWS * fews)
    def _(i):
        rows = few_of(i)
        unit, r = norm_parts(mid[rows, :])
        d_mid = c_ref[rows, :] + norm_back(unit, r, dnm[rows, :])
        c_ref[rows, :] = d_mid
        nmid[rows, :] = d_mid.astype(BF16)

    g_ref[PROJ_BLOCK] = nn(mixed[...].T, nmid[...]).astype(BF16)
    tick(*AFTER_PROJ)
    mixed[...] = nt(nmid[...], wproj_ref[...]).astype(BF16)

    for w in range(WINDOWS):

        @pl.loop(w, w + 1)
        def _(w):
            rows = rows_of(w)
            for g in range(GROUPS):
                lo = LANES * g
                q = spread_heads(packed[rows, lo : lo + LANES])
                k = packed[rows, D + lo : D + lo + LANES]
                v = packed[rows, 2 * D + lo : 2 * D + lo + LANES]
                do = spread_heads(mixed[rows, lo : lo + LANES])
                p = probs[w * GROUPS + g]
                dp = nt(v, do)
                pf = p.astype(F32)
                total = jnp.sum(dp * pf, axis=0, keepdims=True)
                ds = (pf * (dp - total) * SCALE).astype(BF16)
                packed[rows, lo : lo + LANES] = own_blocks(nn(k.T, ds)).T.astype(BF16)
                packed[rows, D + lo : D + lo + LANES] = nn(ds, q).astype(BF16)
                packed[rows, 2 * D + lo : 2 * D + lo + LANES] = nn(p, do).astype(BF16)

        tick(*AFTER_WINDOW[w])

    normed_t = normed[...].T
    for j in range(3):
        g_ref[QKV_BLOCKS[j]] = nn(normed_t, packed[:, D * j : D * (j + 1)]).astype(BF16)
        tick(QKV_BLOCKS[j])
    tick(*AFTER_QKV)
    for j in range(3):
        cols = slice(D * j, D * (j + 1))
        part = nt(packed[:, cols], wqkv_ref[:, cols])
        if j == 0:
            dnm[...] = part
        else:
            dnm[...] += part
    tick(*AFTER_INPUT)

    @pl.loop(0, WINDOWS * fews)
    def _(i):
        rows = few_of(i)
        unit, r = norm_parts(x_ref[rows, :])
        c_ref[rows, :] = c_ref[rows, :] + norm_back(unit, r, dnm[rows, :])

    tick(*AFTER_NORM)
    pack_back(c_ref, back_out)
    grad_halo = exchange(back_out, back_in, back, 6)
    return_own(c_ref, out_ref)

    rounds = 0
    while any(one.stage <= one.last for one in sums):
        tick(*(u for u in (9, 10, 11, 0, 1, 2, 3, 4, 5, 6, 7, 8) if sums[u].stage <= sums[u].last))
        rounds += 1
        if rounds == 2:
            for one in grad_halo:
                one.wait()
            return_halo(back_in, out_ref)
    for one in leaving.values():
        one.wait()


def block_call(tokens, cotangent, region, w_qkv, w_proj, w_in, w_out):
    anywhere, vmem = pl.BlockSpec(memory_space=pl.ANY), pl.BlockSpec(memory_space=pltpu.VMEM)
    count = WINDOWS * WIN
    return pl.pallas_call(
        block_kernel,
        out_shape=(jax.ShapeDtypeStruct(tokens.shape, F32), jax.ShapeDtypeStruct((BLOCKS, D, D), BF16)),
        in_specs=[anywhere, anywhere, vmem] + [anywhere] * 4,
        out_specs=(vmem, anywhere),
        scratch_shapes=[
            pltpu.VMEM((BLOCKS, D, D), BF16),
            pltpu.VMEM(tokens.shape, F32),
            pltpu.VMEM((count, 128), F32),
            pltpu.VMEM((count, D), F32),
            pltpu.VMEM((count, D), F32),
            pltpu.VMEM(w_qkv.shape, BF16),
            pltpu.VMEM(w_proj.shape, BF16),
            pltpu.VMEM(w_in.shape, BF16),
            pltpu.VMEM(w_out.shape, BF16),
            pltpu.VMEM((count, D), BF16),
            pltpu.VMEM((count, 3 * D), BF16),
            pltpu.VMEM((WINDOWS * GROUPS, WIN, SPREAD), BF16),
            pltpu.VMEM((count, D), BF16),
            pltpu.VMEM((count, D), F32),
            pltpu.VMEM((count, D), BF16),
            pltpu.VMEM((count, D), F32),
            pltpu.VMEM((BLOCKS, D, D), BF16),
            pltpu.VMEM((2, HALO_ROWS, D), BF16),
            pltpu.VMEM((2, HALO_ROWS, D), BF16),
            pltpu.VMEM((HALO_ROWS, D), BF16),
            pltpu.VMEM((HALO_ROWS, D), BF16),
            pltpu.SemaphoreType.DMA((6,)),
            pltpu.SemaphoreType.DMA((2, 9)),
            pltpu.SemaphoreType.DMA((BLOCKS,)),
        ]
        + sum_scratch(),
        compiler_params=pltpu.CompilerParams(
            collective_id=0, has_side_effects=True, vmem_limit_bytes=63 * 1024 * 1024
        ),
        cost_estimate=pl.CostEstimate(flops=16 * 10**9, bytes_accessed=24 * 10**6, transcendentals=4 * 10**6),
        name="block",
    )(tokens, cotangent, region, w_qkv, w_proj, w_in, w_out)


def local(tokens, cotangent, region_ids, w_qkv, w_proj, w_in, w_out):
    grad_tokens, grads = block_call(
        tokens.transpose(1, 2, 0, 3), cotangent.transpose(1, 2, 0, 3), region_ids.transpose(1, 0, 2),
        w_qkv, w_proj, w_in, w_out,
    )
    grad_out, grad_in, grad_qkv, grad_proj, grad_tokens = unpack_call(grads, grad_tokens)
    return grad_tokens.transpose(2, 0, 1, 3), grad_qkv, grad_proj, grad_in, grad_out


def solution(mesh):
    grid = P(None, "lat", "lon", None)
    in_specs = (grid, grid, P(None, "lat", "lon"), P(), P(), P(), P())
    out_specs = (grid, P(), P(), P(), P())
    return jax.shard_map(local, mesh=mesh, in_specs=in_specs, out_specs=out_specs, check_vma=False)
```

```python
import functools

import jax
import jax.numpy as jnp
from jax import lax
from jax.experimental import pallas as pl
from jax.experimental.pallas import tpu as pltpu
from jax.sharding import PartitionSpec as P

D = 512
HEADS = 16
HEAD_DIM = D // HEADS
FFN = 2048
WLEV = 2
WLAT = 6
WLON = 12
WIN = WLEV * WLAT * WLON
GROUP = 8
LANES = GROUP * HEAD_DIM
GROUPS = HEADS // GROUP
SPREAD = GROUP * WIN
HALF_LAT = WLAT // 2
HALF_LON = WLON // 2
EPS = 1e-05
MASKED = -1e10
SCALE = HEAD_DIM ** -0.5
LOG2E = 1.4426950408889634
GELU_A = 0.7978845608028654
GELU_B = 0.044715
F32 = jnp.float32
BF16 = jnp.bfloat16


def nn(a, b):
    return lax.dot_general(a, b, (((1,), (0,)), ((), ())), preferred_element_type=F32)


def nt(a, b):
    return lax.dot_general(a, b, (((1,), (1,)), ((), ())), preferred_element_type=F32)


def norm_parts(v):
    centred = v - jnp.mean(v, axis=-1, keepdims=True)
    r = lax.rsqrt(jnp.mean(centred * centred, axis=-1, keepdims=True) + EPS)
    return centred * r, r


def norm_back(unit, r, g):
    return r * (g - jnp.mean(g, axis=-1, keepdims=True) - unit * jnp.mean(g * unit, axis=-1, keepdims=True))


def spread_heads(v):
    lane_head = lax.broadcasted_iota(jnp.int32, v.shape, 1) // HEAD_DIM
    zero = jnp.zeros_like(v)
    return jnp.concatenate([jnp.where(lane_head == h, v, zero) for h in range(GROUP)], axis=0)


def own_blocks(full):
    return jnp.concatenate(
        [full[HEAD_DIM * h : HEAD_DIM * (h + 1), WIN * h : WIN * (h + 1)] for h in range(GROUP)], axis=0
    )


BLOCKS = 12
OUT_BLOCKS = (0, 2, 4, 6)
IN_BLOCKS = (1, 3, 5, 7)
PROJ_BLOCK = 8
QKV_BLOCKS = (9, 10, 11)
UNITS = (
    (0, 0, D, "xyz", 1), (1, 0, D, "yzx", 1), (2, 0, D, "zxy", 1), (3, 0, D, "xyz", 3),
    (4, 0, D, "yzx", 3), (5, 0, D, "zxy", 3), (6, 0, D, "xyz", 1), (7, 0, D, "yzx", 1),
    (8, 0, D, "zxy", 0),
    (9, 0, LANES, "xyz", 0), (10, 0, LANES, "yzx", 0), (11, 0, LANES, "zxy", 0),
    (9, LANES, LANES, "xyz", 0), (10, LANES, LANES, "yzx", 0), (11, LANES, LANES, "zxy", 0),
)
QKV_UNITS = ((9, 10, 11), (12, 13, 14))
SLOTS = 17


class Place:
    def __init__(self):
        lat, lon = lax.axis_index("lat"), lax.axis_index("lon")
        self.core = lon % 2
        self.at = {"x": (lon // 2) % 4, "y": (lon // 8) * 2 + lat % 2, "z": lat // 2}

    def mesh_id(self, at, core):
        return (at["z"] * 2 + at["y"] % 2, (at["y"] // 2) * 8 + at["x"] * 2 + core)

    def sibling(self):
        return self.mesh_id(self.at, 1 - self.core)

    def along(self, axis, step):
        at = dict(self.at)
        at[axis] = (at[axis] + step) % 4
        return self.mesh_id(at, self.core), at[axis]

    def across(self, axis, kind):
        at, c = dict(self.at), self.at[axis]
        at[axis] = c + 1 - 2 * (c % 2) if kind == 1 else 3 - c
        bit = ((c + 1) // 2) % 2 if kind == 1 else c // 2
        return self.mesh_id(at, self.core), bit


def greet(place, others=()):
    barrier = pltpu.get_barrier_semaphore()
    partners = [place.sibling()] + [place.along(a, s)[0] for a in "xyz" for s in (1, 2, 3)] + list(others)
    for partner in partners:
        pl.semaphore_signal(barrier, inc=1, device_id=partner, device_id_type=pl.DeviceIdType.MESH)
    pl.semaphore_wait(barrier, len(partners))


class Sum:
    def __init__(self, place, u, g, done, got, send, recv):
        self.u, self.g, self.done, self.got, self.send, self.recv = u, g, done, got, send, recv
        self.stage, self.slots, self.copies = 0, 0, []
        self.block, col, width, order, first = UNITS[u]
        self.cols = pl.ds(col, width)
        self.steps, base, rows = [], 0, D

        def halve(name, target, bit, base, rows):
            rows //= 2
            self.steps.append((name, [(target, base + (1 - bit) * rows)], base + bit * rows, rows))
            return base + bit * rows, rows

        def quarter(name, axis, base, rows):
            rows //= 4
            peers = [place.along(axis, step) for step in (1, 2, 3)]
            self.steps.append((name, [(t, base + c * rows) for t, c in peers], base + place.at[axis] * rows, rows))
            return base + place.at[axis] * rows, rows

        base, rows = halve("core", place.sibling(), place.core, base, rows)
        if first:
            base, rows = halve("near", *place.across(order[0], first), base, rows)
            base, rows = halve("far", *place.across(order[0], 4 - first), base, rows)
        else:
            base, rows = quarter("axis", order[0], base, rows)
        base, rows = quarter("second", order[1], base, rows)
        peers = [place.along(order[2], step)[0] for step in (1, 2, 3)]
        self.swap = (peers, place.at[order[2]], base, rows)
        self.last = 2 * len(self.steps) + 1

    def part(self, ref, base, rows):
        return ref.at[self.block, pl.ds(pl.multiple_of(base, rows), rows), self.cols]

    def copy(self, src, dst, target):
        slot = self.slots
        self.slots += 1
        one = pltpu.make_async_remote_copy(
            src_ref=src, dst_ref=dst, send_sem=self.send.at[self.u, slot], recv_sem=self.recv.at[self.u, slot],
            device_id=target, device_id_type=pl.DeviceIdType.MESH,
        )
        one.start()
        self.copies.append(one)

    def landing(self, name, i):
        if name == "axis":
            return self.got[name].at[i, self.block - PROJ_BLOCK, :, self.cols]
        return self.got[name].at[i, self.block, :, self.cols]

    def advance(self):
        n, stage = len(self.steps), self.stage
        self.stage += 1
        for one in self.copies:
            one.wait()
        self.copies = []
        if 1 <= stage <= n:
            name, targets, base, rows = self.steps[stage - 1]
            mine = self.part(self.g, base, rows)
            total = mine[...].astype(F32)
            for i in range(len(targets)):
                total = total + self.landing(name, i)[...].astype(F32)
            mine[...] = total.astype(BF16)
        if stage == n + 1:
            _, _, base, rows = self.swap
            four = [self.got["swap"][c, self.block, :, self.cols].astype(F32) for c in range(4)]
            self.part(self.done, base, rows)[...] = ((four[0] + four[1]) + (four[2] + four[3])).astype(BF16)
        if stage < n:
            name, targets, _, rows = self.steps[stage]
            for i, (target, base) in enumerate(targets):
                self.copy(self.part(self.g, base, rows), self.landing(name, i), target)
        elif stage == n:
            targets, at, base, rows = self.swap
            mine = self.part(self.g, base, rows)
            self.got["swap"][at, self.block, :, self.cols] = mine[...]
            for target in targets:
                self.copy(mine, self.got["swap"].at[at, self.block, :, self.cols], target)
        elif stage <= 2 * n:
            _, targets, base, rows = self.steps[2 * n - stage]
            mine = self.part(self.done, base, rows)
            for target, _ in targets:
                self.copy(mine, mine, target)


LANDINGS = (
    ("core", (1, BLOCKS, D // 2, D)),
    ("near", (1, BLOCKS - 3, D // 4, D)),
    ("far", (1, BLOCKS - 3, D // 8, D)),
    ("axis", (3, 4, D // 8, D)),
    ("second", (3, BLOCKS, D // 32, D)),
    ("swap", (4, BLOCKS, D // 32, D)),
)


def sum_scratch():
    return [pltpu.VMEM(shape, BF16) for _, shape in LANDINGS] + [pltpu.SemaphoreType.DMA((len(UNITS), SLOTS))] * 2


def unpack_kernel(g_ref, tok_ref, out_ref, in_ref, qkv_ref, proj_ref, tok_out, half, full, lines_in, got, put, whole):
    def target(u):
        if u == PROJ_BLOCK:
            return proj_ref
        if u in OUT_BLOCKS:
            return out_ref.at[pl.ds(D * OUT_BLOCKS.index(u), D), :]
        if u in IN_BLOCKS:
            return in_ref.at[:, pl.ds(D * IN_BLOCKS.index(u), D)]
        return qkv_ref.at[:, pl.ds(D * QKV_BLOCKS.index(u), D)]

    ins = [pltpu.make_async_copy(g_ref.at[u], half.at[u], got.at[u]) for u in range(BLOCKS)]
    outs = [pltpu.make_async_copy(full.at[u], target(u), put.at[u]) for u in range(BLOCKS)]
    arrive = pltpu.make_async_copy(tok_ref, lines_in, whole.at[0])
    leave = pltpu.make_async_copy(lines_in, tok_out, whole.at[1])
    arrive.start()
    for one in ins:
        one.start()
    arrive.wait()
    leave.start()
    for u in range(BLOCKS):
        ins[u].wait()
        full[u] = half[u].astype(F32)
        outs[u].start()
    for one in outs:
        one.wait()
    leave.wait()


def unpack_call(grads, grad_tokens):
    anywhere = pl.BlockSpec(memory_space=pl.ANY)
    return pl.pallas_call(
        unpack_kernel,
        out_shape=tuple(jax.ShapeDtypeStruct(s, F32) for s in ((FFN, D), (D, FFN), (D, 3 * D), (D, D), grad_tokens.shape)),
        in_specs=[anywhere] * 2,
        out_specs=(anywhere,) * 5,
        scratch_shapes=[
            pltpu.VMEM((BLOCKS, D, D), BF16),
            pltpu.VMEM((BLOCKS, D, D), F32),
            pltpu.VMEM(grad_tokens.shape, F32),
            pltpu.SemaphoreType.DMA((BLOCKS,)),
            pltpu.SemaphoreType.DMA((BLOCKS,)),
            pltpu.SemaphoreType.DMA((2,)),
        ],
        compiler_params=pltpu.CompilerParams(vmem_limit_bytes=60 * 1024 * 1024),
        name="unpack",
    )(grads, grad_tokens)


LAT_ROWS, LON_ROWS = 64, 16
LAT_AT, LON_AT, DIAG_AT, HALO_ROWS = 0, 192, 336, 384
WINDOWS = 6
FEW = 144
WIDE = 3
OWN_ROWS = 9
OWN_COLS = 30
STRIP = OWN_COLS * WLEV
EDGE = HALF_LON * WLEV
LINE = WLON * WLEV
HALO_PARTS = ((LAT_AT, LON_AT), (LON_AT, DIAG_AT), (DIAG_AT, HALO_ROWS))


def cell(row, wide):
    return ((row // WLAT) * WIDE + wide) * WIN + (row % WLAT) * LINE


def lines(v):
    return v.reshape(v.shape[0] * WLEV, D)


def cells(v):
    return v.reshape(v.shape[0] // WLEV, WLEV, D)


def padded(pieces, rows):
    have = sum(p.shape[0] for p in pieces)
    return jnp.concatenate(pieces + [jnp.zeros((rows - have, D), F32)], axis=0).astype(BF16)


def ahead_at(row):
    return DIAG_AT + row * LON_ROWS if row < HALF_LAT else LON_AT + (row - HALF_LAT) * LON_ROWS


def behind_at(row):
    return LON_AT + row * LON_ROWS if row < OWN_ROWS else DIAG_AT + (row - OWN_ROWS) * LON_ROWS


def pack_ahead(src, dst):
    for row in range(HALF_LAT):
        at = LAT_AT + row * LAT_ROWS
        dst[at : at + LAT_ROWS, :] = padded([lines(src[row, HALF_LON : HALF_LON + OWN_COLS])], LAT_ROWS)
    for row in range(HALF_LAT + OWN_ROWS):
        at = ahead_at(row)
        dst[at : at + LON_ROWS, :] = padded([lines(src[row, :HALF_LON])], LON_ROWS)


def place_strip(flat, row, strip):
    flat[cell(row, 0) : cell(row, 0) + LINE, :] = strip[:LINE]
    flat[cell(row, 1) : cell(row, 1) + LINE, :] = strip[LINE : 2 * LINE]
    flat[cell(row, 2) : cell(row, 2) + EDGE, :] = strip[2 * LINE : STRIP]


def take_strip(flat, row):
    return [
        flat[cell(row, 0) : cell(row, 0) + LINE, :],
        flat[cell(row, 1) : cell(row, 1) + LINE, :],
        flat[cell(row, 2) : cell(row, 2) + EDGE, :],
    ]


def place_own(src, flat):
    for row in range(OWN_ROWS):
        place_strip(flat, row, lines(src[row + HALF_LAT, HALF_LON : HALF_LON + OWN_COLS]))


def place_halo(got, flat):
    for row in range(HALF_LAT):
        at = LAT_AT + row * LAT_ROWS
        place_strip(flat, OWN_ROWS + row, got[at : at + LAT_ROWS, :].astype(F32))
    for row in range(OWN_ROWS + HALF_LAT):
        at, to = behind_at(row), cell(row, 2) + EDGE
        flat[to : to + EDGE, :] = got[at : at + LON_ROWS, :].astype(F32)[:EDGE]


def pack_back(flat, dst):
    for row in range(HALF_LAT):
        at = LAT_AT + row * LAT_ROWS
        dst[at : at + LAT_ROWS, :] = padded(take_strip(flat, OWN_ROWS + row), LAT_ROWS)
    for row in range(OWN_ROWS + HALF_LAT):
        at, end = behind_at(row), cell(row, 2) + EDGE
        dst[at : at + LON_ROWS, :] = padded([flat[end : end + EDGE, :]], LON_ROWS)


def return_own(flat, out):
    for row in range(OWN_ROWS):
        strip = jnp.concatenate(take_strip(flat, row), axis=0)
        out[row + HALF_LAT, HALF_LON : HALF_LON + OWN_COLS] = cells(strip)


def return_halo(got, out):
    for row in range(HALF_LAT + OWN_ROWS):
        at = ahead_at(row)
        out[row, :HALF_LON] = cells(got[at : at + LON_ROWS, :].astype(F32)[:EDGE])
    for row in range(HALF_LAT):
        at = LAT_AT + row * LAT_ROWS
        out[row, HALF_LON : HALF_LON + OWN_COLS] = cells(got[at : at + LAT_ROWS, :].astype(F32)[:STRIP])


def place_regions(region, flat):
    for row in range(HALF_LAT + OWN_ROWS):
        ids = region[row].astype(F32)
        levels = [jnp.broadcast_to(ids[l : l + 1], (128, ids.shape[1])).T for l in range(WLEV)]
        both = jnp.stack(levels[::-1], axis=1).reshape(ids.shape[1] * WLEV, 128)
        for wide in range(WIDE):
            flat[cell(row, wide) : cell(row, wide) + LINE, :] = both[LINE * wide : LINE * (wide + 1)]


AFTER_CHUNK = ((0, 1), (0, 1, 2, 3), (2, 3, 4, 5), (0, 1, 4, 5, 6, 7))
AFTER_PROJ = (8, 0, 1, 2, 3, 6, 7)
AFTER_WINDOW = (
    ((), (4, 5), (), (0, 1, 2, 3, 8), (), (4, 5, 6, 7)),
    ((), (0, 1, 2, 3, 9, 10, 11), (), (4, 5, 6, 7, 8), (), (0, 1, 2, 3, 9, 10, 11)),
)
AFTER_QKV = (4, 5, 6, 7, 8)
AFTER_INPUT = (12, 13, 14, 9, 10, 11, 0, 1, 2, 3)
AFTER_NORM = (9, 10, 11, 4, 5, 6, 7, 8)


def block_kernel(
    tokens, cotangent, region, wqkv, wproj, win, wout,
    out_ref, done_hbm,
    done_ref, cot_ref, region_ref, x_ref, c_ref, wqkv_ref, wproj_ref, win_ref, wout_ref,
    normed, packed, probs, mixed, mid, nmid, dnm, g_ref,
    halo_out, halo_in, back_out, back_in, load_sem, halo_sem, done_sem, *landings_and_sems,
):
    place = Place()
    *landings, send, recv = landings_and_sems
    got = {name: ref for (name, _), ref in zip(LANDINGS, landings)}
    sums = [Sum(place, u, g_ref, done_ref, got, send, recv) for u in range(len(UNITS))]

    leaving = [
        pltpu.make_async_copy(
            done_ref.at[one.block, :, one.cols], done_hbm.at[one.block, :, one.cols], done_sem.at[one.u]
        )
        for one in sums
    ]

    def tick(*blocks):
        for u in blocks:
            sums[u].advance()
            if sums[u].stage == sums[u].last + 1:
                leaving[u].start()

    loads = [
        pltpu.make_async_copy(src, dst, load_sem.at[i])
        for i, (src, dst) in enumerate(
            ((tokens, out_ref), (cotangent, cot_ref), (wqkv, wqkv_ref), (wproj, wproj_ref), (win, win_ref), (wout, wout_ref))
        )
    ]
    for one in loads:
        one.start()

    lat, lon = lax.axis_index("lat"), lax.axis_index("lon")
    lats, lons = lax.axis_size("lat"), lax.axis_size("lon")
    up, down = lax.rem(lat + lats - 1, lats), lax.rem(lat + 1, lats)
    left, right = lax.rem(lon + lons - 1, lons), lax.rem(lon + 1, lons)
    ahead = ((up, lon), (lat, left), (up, left))
    back = ((down, lon), (lat, right), (down, right))
    greet(place, ahead + back)

    def exchange(src, dst, targets, at):
        copies = []
        for i, (lo, hi) in enumerate(HALO_PARTS):
            one = pltpu.make_async_remote_copy(
                src_ref=src.at[lo:hi], dst_ref=dst.at[lo:hi],
                send_sem=halo_sem.at[0, at + i], recv_sem=halo_sem.at[1, at + i],
                device_id=targets[i], device_id_type=pl.DeviceIdType.MESH,
            )
            one.start()
            copies.append(one)
        return copies

    loads[0].wait()
    pack_ahead(out_ref, halo_out.at[0])
    token_halo = exchange(halo_out.at[0], halo_in.at[0], ahead, 0)
    place_own(out_ref, x_ref)
    place_regions(region, region_ref)

    rows_of = lambda w: pl.ds(pl.multiple_of(w * WIN, WIN), WIN)
    few_of = lambda i: pl.ds(pl.multiple_of(i * FEW, FEW), FEW)
    fews = WIN // FEW

    def attention_forward(first, last):
        @pl.loop(first * fews, last * fews)
        def _(i):
            unit, _ = norm_parts(x_ref[few_of(i), :])
            normed[few_of(i), :] = unit.astype(BF16)

        if first == 0:
            loads[2].wait()
        rows = slice(first * WIN, last * WIN)
        for j in range(3):
            cols = slice(D * j, D * (j + 1))
            packed[rows, cols] = nn(normed[rows, :], wqkv_ref[:, cols]).astype(BF16)

        @pl.loop(first, last)
        def _(w):
            rows = rows_of(w)
            ids = region_ref[rows, :]
            allowed = ids[:, :1] == jnp.concatenate([ids.T[:1]] * GROUP, axis=1)
            for g in range(GROUPS):
                lo = LANES * g
                q = packed[rows, lo : lo + LANES]
                k = packed[rows, D + lo : D + lo + LANES]
                v = packed[rows, 2 * D + lo : 2 * D + lo + LANES]
                s = jnp.where(allowed, nt(k, spread_heads(q)), MASKED)
                e = jnp.exp2((s - jnp.max(s, axis=0, keepdims=True)) * (SCALE * LOG2E))
                p = (e * (1.0 / jnp.sum(e, axis=0, keepdims=True))).astype(BF16)
                probs[w * GROUPS + g] = p
                mixed[rows, lo : lo + LANES] = own_blocks(nn(v.T, p)).T.astype(BF16)

    attention_forward(0, 2)
    loads[1].wait()
    pack_ahead(cot_ref, halo_out.at[1])
    for one in token_halo:
        one.wait()
    cot_halo = exchange(halo_out.at[1], halo_in.at[1], ahead, 3)
    place_halo(halo_in.at[0], x_ref)
    attention_forward(2, WINDOWS)

    loads[3].wait()
    mid[...] = nn(mixed[...], wproj_ref[...]).astype(BF16).astype(F32)

    @pl.loop(0, WINDOWS * fews)
    def _(i):
        rows = few_of(i)
        middle = x_ref[rows, :] + mid[rows, :]
        mid[rows, :] = middle
        nmid[rows, :] = norm_parts(middle)[0].astype(BF16)

    place_own(cot_ref, c_ref)
    for one in cot_halo:
        one.wait()
    place_halo(halo_in.at[1], c_ref)
    loads[4].wait()
    loads[5].wait()

    nmid_t = nmid[...].T
    for j in range(FFN // D):
        cols = slice(D * j, D * (j + 1))
        cot = c_ref[...].astype(BF16)
        u = nn(nmid[...], win_ref[:, cols])
        da = nt(cot, wout_ref[cols, :])
        square = u * u
        t = jnp.tanh(u * (GELU_A + (GELU_A * GELU_B) * square))
        half = 0.5 + 0.5 * t
        act = (u * half).astype(BF16)
        slope = half + u * (0.5 - 0.5 * t * t) * (GELU_A + (3 * GELU_A * GELU_B) * square)
        dpre = (slope * da).astype(BF16)
        g_ref[OUT_BLOCKS[j]] = nn(act.T, cot).astype(BF16)
        g_ref[IN_BLOCKS[j]] = nn(nmid_t, dpre).astype(BF16)
        part = nt(dpre, win_ref[:, cols])
        if j == 0:
            dnm[...] = part
        else:
            dnm[...] += part
        tick(*AFTER_CHUNK[j])

    @pl.loop(0, WINDOWS * fews)
    def _(i):
        rows = few_of(i)
        unit, r = norm_parts(mid[rows, :])
        d_mid = c_ref[rows, :] + norm_back(unit, r, dnm[rows, :])
        c_ref[rows, :] = d_mid
        nmid[rows, :] = d_mid.astype(BF16)

    g_ref[PROJ_BLOCK] = nn(mixed[...].T, nmid[...]).astype(BF16)
    tick(*AFTER_PROJ)
    mixed[...] = nt(nmid[...], wproj_ref[...]).astype(BF16)

    normed_t = normed[...].T
    for g in range(GROUPS):
        lo = LANES * g
        for w in range(WINDOWS):

            @pl.loop(w, w + 1)
            def _(w):
                rows = rows_of(w)
                q = spread_heads(packed[rows, lo : lo + LANES])
                k = packed[rows, D + lo : D + lo + LANES]
                v = packed[rows, 2 * D + lo : 2 * D + lo + LANES]
                do = spread_heads(mixed[rows, lo : lo + LANES])
                p = probs[w * GROUPS + g]
                dp = nt(v, do)
                pf = p.astype(F32)
                total = jnp.sum(dp * pf, axis=0, keepdims=True)
                ds = (pf * (dp - total) * SCALE).astype(BF16)
                packed[rows, lo : lo + LANES] = own_blocks(nn(k.T, ds)).T.astype(BF16)
                packed[rows, D + lo : D + lo + LANES] = nn(ds, q).astype(BF16)
                packed[rows, 2 * D + lo : 2 * D + lo + LANES] = nn(p, do).astype(BF16)

            tick(*AFTER_WINDOW[g][w])
        for j in range(3):
            g_ref[QKV_BLOCKS[j], :, lo : lo + LANES] = nn(
                normed_t, packed[:, D * j + lo : D * j + lo + LANES]
            ).astype(BF16)
            tick(QKV_UNITS[g][j])
    tick(*AFTER_QKV)
    for j in range(3):
        cols = slice(D * j, D * (j + 1))
        part = nt(packed[:, cols], wqkv_ref[:, cols])
        if j == 0:
            dnm[...] = part
        else:
            dnm[...] += part
    tick(*AFTER_INPUT)

    @pl.loop(0, WINDOWS * fews)
    def _(i):
        rows = few_of(i)
        unit, r = norm_parts(x_ref[rows, :])
        c_ref[rows, :] = c_ref[rows, :] + norm_back(unit, r, dnm[rows, :])

    tick(*AFTER_NORM)
    pack_back(c_ref, back_out)
    grad_halo = exchange(back_out, back_in, back, 6)
    return_own(c_ref, out_ref)

    rounds = 0
    while any(one.stage <= one.last for one in sums):
        tick(*(u for u in (*QKV_UNITS[1], *QKV_UNITS[0], 0, 1, 2, 3, 4, 5, 6, 7, 8) if sums[u].stage <= sums[u].last))
        rounds += 1
        if rounds == 2:
            for one in grad_halo:
                one.wait()
            return_halo(back_in, out_ref)
    for one in leaving:
        one.wait()


def block_call(tokens, cotangent, region, w_qkv, w_proj, w_in, w_out):
    anywhere, vmem = pl.BlockSpec(memory_space=pl.ANY), pl.BlockSpec(memory_space=pltpu.VMEM)
    count = WINDOWS * WIN
    return pl.pallas_call(
        block_kernel,
        out_shape=(jax.ShapeDtypeStruct(tokens.shape, F32), jax.ShapeDtypeStruct((BLOCKS, D, D), BF16)),
        in_specs=[anywhere, anywhere, vmem] + [anywhere] * 4,
        out_specs=(vmem, anywhere),
        scratch_shapes=[
            pltpu.VMEM((BLOCKS, D, D), BF16),
            pltpu.VMEM(tokens.shape, F32),
            pltpu.VMEM((count, 128), F32),
            pltpu.VMEM((count, D), F32),
            pltpu.VMEM((count, D), F32),
            pltpu.VMEM(w_qkv.shape, BF16),
            pltpu.VMEM(w_proj.shape, BF16),
            pltpu.VMEM(w_in.shape, BF16),
            pltpu.VMEM(w_out.shape, BF16),
            pltpu.VMEM((count, D), BF16),
            pltpu.VMEM((count, 3 * D), BF16),
            pltpu.VMEM((WINDOWS * GROUPS, WIN, SPREAD), BF16),
            pltpu.VMEM((count, D), BF16),
            pltpu.VMEM((count, D), F32),
            pltpu.VMEM((count, D), BF16),
            pltpu.VMEM((count, D), F32),
            pltpu.VMEM((BLOCKS, D, D), BF16),
            pltpu.VMEM((2, HALO_ROWS, D), BF16),
            pltpu.VMEM((2, HALO_ROWS, D), BF16),
            pltpu.VMEM((HALO_ROWS, D), BF16),
            pltpu.VMEM((HALO_ROWS, D), BF16),
            pltpu.SemaphoreType.DMA((6,)),
            pltpu.SemaphoreType.DMA((2, 9)),
            pltpu.SemaphoreType.DMA((len(UNITS),)),
        ]
        + sum_scratch(),
        compiler_params=pltpu.CompilerParams(
            collective_id=0, has_side_effects=True, vmem_limit_bytes=63 * 1024 * 1024
        ),
        cost_estimate=pl.CostEstimate(flops=16 * 10**9, bytes_accessed=24 * 10**6, transcendentals=4 * 10**6),
        name="block",
    )(tokens, cotangent, region, w_qkv, w_proj, w_in, w_out)


def local(tokens, cotangent, region_ids, w_qkv, w_proj, w_in, w_out):
    grad_tokens, grads = block_call(
        tokens.transpose(1, 2, 0, 3), cotangent.transpose(1, 2, 0, 3), region_ids.transpose(1, 0, 2),
        w_qkv, w_proj, w_in, w_out,
    )
    grad_out, grad_in, grad_qkv, grad_proj, grad_tokens = unpack_call(grads, grad_tokens)
    return grad_tokens.transpose(2, 0, 1, 3), grad_qkv, grad_proj, grad_in, grad_out


def solution(mesh):
    grid = P(None, "lat", "lon", None)
    in_specs = (grid, grid, P(None, "lat", "lon"), P(), P(), P(), P())
    out_specs = (grid, P(), P(), P(), P())
    return jax.shard_map(local, mesh=mesh, in_specs=in_specs, out_specs=out_specs, check_vma=False)
```

```python
import functools

import jax
import jax.numpy as jnp
from jax import lax
from jax.experimental import pallas as pl
from jax.experimental.pallas import tpu as pltpu
from jax.sharding import PartitionSpec as P

D = 512
HEADS = 16
HEAD_DIM = D // HEADS
FFN = 2048
WLEV = 2
WLAT = 6
WLON = 12
WIN = WLEV * WLAT * WLON
GROUP = 8
LANES = GROUP * HEAD_DIM
GROUPS = HEADS // GROUP
SPREAD = GROUP * WIN
HALF_LAT = WLAT // 2
HALF_LON = WLON // 2
EPS = 1e-05
MASKED = -1e10
SCALE = HEAD_DIM ** -0.5
LOG2E = 1.4426950408889634
GELU_A = 0.7978845608028654
GELU_B = 0.044715
F32 = jnp.float32
BF16 = jnp.bfloat16


def nn(a, b):
    return lax.dot_general(a, b, (((1,), (0,)), ((), ())), preferred_element_type=F32)


def nt(a, b):
    return lax.dot_general(a, b, (((1,), (1,)), ((), ())), preferred_element_type=F32)


def norm_parts(v):
    centred = v - jnp.mean(v, axis=-1, keepdims=True)
    r = lax.rsqrt(jnp.mean(centred * centred, axis=-1, keepdims=True) + EPS)
    return centred * r, r


def norm_back(unit, r, g):
    return r * (g - jnp.mean(g, axis=-1, keepdims=True) - unit * jnp.mean(g * unit, axis=-1, keepdims=True))


def spread_heads(v):
    lane_head = lax.broadcasted_iota(jnp.int32, v.shape, 1) // HEAD_DIM
    zero = jnp.zeros_like(v)
    return jnp.concatenate([jnp.where(lane_head == h, v, zero) for h in range(GROUP)], axis=0)


def own_blocks(full):
    return jnp.concatenate(
        [full[HEAD_DIM * h : HEAD_DIM * (h + 1), WIN * h : WIN * (h + 1)] for h in range(GROUP)], axis=0
    )


BLOCKS = 12
OUT_BLOCKS = (0, 2, 4, 6)
IN_BLOCKS = (1, 3, 5, 7)
PROJ_BLOCK = 8
QKV_BLOCKS = (9, 10, 11)
UNITS = (
    (0, 2, "xyz"), (2, 2, "yzx"), (4, 2, "zxy"), (6, 2, "xyz"),
    (8, 1, "yzx"), (9, 1, "xyz"), (10, 1, "yzx"), (11, 1, "zxy"),
)
QKV_UNITS = (5, 6, 7)
PAIRED = 8
SLOTS = 19
SPLIT = (4, 2, D // 8, D)


class Place:
    def __init__(self):
        lat, lon = lax.axis_index("lat"), lax.axis_index("lon")
        self.core = lon % 2
        self.at = {"x": (lon // 2) % 4, "y": (lon // 8) * 2 + lat % 2, "z": lat // 2}

    def mesh_id(self, at, core):
        return (at["z"] * 2 + at["y"] % 2, (at["y"] // 2) * 8 + at["x"] * 2 + core)

    def sibling(self):
        return self.mesh_id(self.at, 1 - self.core)

    def along(self, axis, step):
        at = dict(self.at)
        at[axis] = (at[axis] + step) % 4
        return self.mesh_id(at, self.core), at[axis]

    def across(self, axis, kind):
        at, c = dict(self.at), self.at[axis]
        at[axis] = c + 1 - 2 * (c % 2) if kind == 1 else 3 - c
        bit = ((c + 1) // 2) % 2 if kind == 1 else c // 2
        return self.mesh_id(at, self.core), bit


def greet(place, others=()):
    barrier = pltpu.get_barrier_semaphore()
    partners = [place.sibling()] + [place.along(a, s)[0] for a in "xyz" for s in (1, 2, 3)] + list(others)
    for partner in partners:
        pl.semaphore_signal(barrier, inc=1, device_id=partner, device_id_type=pl.DeviceIdType.MESH)
    pl.semaphore_wait(barrier, len(partners))


class Sum:
    def __init__(self, place, u, g, done, got, send, recv):
        first, count, order = UNITS[u]
        self.u, self.g, self.done, self.send, self.recv = u, g, done, send, recv
        self.blocks = blocks = pl.ds(first, count)
        self.stage, self.slots, self.copies = 0, 0, []
        top, other = place.core * 2, (1 - place.core) * 2
        self.steps = []

        def half(pieces):
            self.steps.append((
                [(out, land, target) for out, keep, land, target in pieces],
                [(keep, [land]) for out, keep, land, target in pieces],
                [(keep, target) for out, keep, land, target in pieces],
            ))

        def quarter(axis, piece, landing):
            peers = [place.along(axis, step) for step in (1, 2, 3)]
            keep = piece(place.at[axis])
            self.steps.append((
                [(piece(c), landing[i], target) for i, (target, c) in enumerate(peers)],
                [(keep, landing)],
                [(keep, target) for target, _ in peers],
            ))

        half([(
            lambda r: r.at[blocks, pl.ds(other, 2)], lambda r: r.at[blocks, pl.ds(top, 2)],
            got["core"].at[blocks], place.sibling(),
        )])
        if count == 2:
            a, b = first, first + 1
            (one, h1), (three, h3) = place.across(order[0], 1), place.across(order[0], 3)
            near, far = got["near"], got["far"]
            half([
                (lambda r: r.at[a, top + 1 - h1], lambda r: r.at[a, top + h1], near.at[a], one),
                (lambda r: r.at[b, pl.ds(top, 2), 1 - h3], lambda r: r.at[b, pl.ds(top, 2), h3], near.at[b], three),
            ])
            half([
                (lambda r: r.at[a, top + h1, 1 - h3], lambda r: r.at[a, top + h1, h3], far.at[a], three),
                (lambda r: r.at[b, top + 1 - h1, h3], lambda r: r.at[b, top + h1, h3], far.at[b], one),
            ])
            at1, at3 = top + h1, h3
        else:
            land = [got["axis"].at[i, pl.ds(first - PAIRED, count)] for i in range(3)]
            quarter(order[0], lambda c: lambda r: r.at[blocks, top + c // 2, c % 2], land)
            c = place.at[order[0]]
            at1, at3 = top + c // 2, c % 2

        def small(c):
            return lambda r: r.at[blocks, at1, at3, pl.ds(pl.multiple_of(c * (D // 32), D // 32), D // 32)]

        quarter(order[1], small, [got["second"].at[i, blocks] for i in range(3)])
        peers = [place.along(order[2], step)[0] for step in (1, 2, 3)]
        self.swap = (peers, small(place.at[order[1]]), place.at[order[2]], got["swap"])
        self.last = 2 * len(self.steps) + 1

    def copy(self, src, dst, target):
        slot = self.slots
        self.slots += 1
        one = pltpu.make_async_remote_copy(
            src_ref=src, dst_ref=dst, send_sem=self.send.at[self.u, slot], recv_sem=self.recv.at[self.u, slot],
            device_id=target, device_id_type=pl.DeviceIdType.MESH,
        )
        one.start()
        self.copies.append(one)

    def advance(self):
        n, stage = len(self.steps), self.stage
        self.stage += 1
        for one in self.copies:
            one.wait()
        self.copies = []
        peers, piece, at, slots = self.swap
        if 1 <= stage <= n:
            for keep, landings in self.steps[stage - 1][1]:
                mine = keep(self.g)
                total = mine[...].astype(F32)
                for landing in landings:
                    total = total + landing[...].astype(F32)
                mine[...] = total.astype(BF16)
        if stage == n + 1:
            four = [slots[c, self.blocks].astype(F32) for c in range(4)]
            piece(self.done)[...] = ((four[0] + four[1]) + (four[2] + four[3])).astype(BF16)
        if stage < n:
            for out, landing, target in self.steps[stage][0]:
                self.copy(out(self.g), landing, target)
        elif stage == n:
            mine = piece(self.g)
            slots[at, self.blocks] = mine[...]
            for target in peers:
                self.copy(mine, slots.at[at, self.blocks], target)
        elif stage <= 2 * n:
            for keep, target in self.steps[2 * n - stage][2]:
                self.copy(keep(self.done), keep(self.done), target)


LANDINGS = (
    ("core", (BLOCKS, 2, 2, D // 8, D)),
    ("near", (PAIRED, 2, D // 8, D)),
    ("far", (PAIRED, D // 8, D)),
    ("axis", (3, BLOCKS - PAIRED, D // 8, D)),
    ("second", (3, BLOCKS, D // 32, D)),
    ("swap", (4, BLOCKS, D // 32, D)),
)


def sum_scratch():
    return [pltpu.VMEM(shape, BF16) for _, shape in LANDINGS] + [pltpu.SemaphoreType.DMA((len(UNITS), SLOTS))] * 2


def unpack_kernel(g_ref, tok_ref, out_ref, in_ref, qkv_ref, proj_ref, tok_out, half, full, lines_in, got, put, whole):
    def target(u):
        if u == PROJ_BLOCK:
            return proj_ref
        if u in OUT_BLOCKS:
            return out_ref.at[pl.ds(D * OUT_BLOCKS.index(u), D), :]
        if u in IN_BLOCKS:
            return in_ref.at[:, pl.ds(D * IN_BLOCKS.index(u), D)]
        return qkv_ref.at[:, pl.ds(D * QKV_BLOCKS.index(u), D)]

    ins = [pltpu.make_async_copy(g_ref.at[u], half.at[u], got.at[u]) for u in range(BLOCKS)]
    outs = [pltpu.make_async_copy(full.at[u], target(u), put.at[u]) for u in range(BLOCKS)]
    arrive = pltpu.make_async_copy(tok_ref, lines_in, whole.at[0])
    leave = pltpu.make_async_copy(lines_in, tok_out, whole.at[1])
    arrive.start()
    for one in ins:
        one.start()
    arrive.wait()
    leave.start()
    for u in range(BLOCKS):
        ins[u].wait()
        full[u] = half[u].astype(F32)
        outs[u].start()
    for one in outs:
        one.wait()
    leave.wait()


def unpack_call(grads, grad_tokens):
    anywhere = pl.BlockSpec(memory_space=pl.ANY)
    return pl.pallas_call(
        unpack_kernel,
        out_shape=tuple(jax.ShapeDtypeStruct(s, F32) for s in ((FFN, D), (D, FFN), (D, 3 * D), (D, D), grad_tokens.shape)),
        in_specs=[anywhere] * 2,
        out_specs=(anywhere,) * 5,
        scratch_shapes=[
            pltpu.VMEM((BLOCKS, D, D), BF16),
            pltpu.VMEM((BLOCKS, D, D), F32),
            pltpu.VMEM(grad_tokens.shape, F32),
            pltpu.SemaphoreType.DMA((BLOCKS,)),
            pltpu.SemaphoreType.DMA((BLOCKS,)),
            pltpu.SemaphoreType.DMA((2,)),
        ],
        compiler_params=pltpu.CompilerParams(vmem_limit_bytes=60 * 1024 * 1024),
        name="unpack",
    )(grads, grad_tokens)


LAT_ROWS, LON_ROWS = 64, 16
LAT_AT, LON_AT, DIAG_AT, HALO_ROWS = 0, 192, 336, 384
WINDOWS = 6
FEW = 144
WIDE = 3
OWN_ROWS = 9
OWN_COLS = 30
STRIP = OWN_COLS * WLEV
EDGE = HALF_LON * WLEV
LINE = WLON * WLEV
HALO_PARTS = ((LAT_AT, LON_AT), (LON_AT, DIAG_AT), (DIAG_AT, HALO_ROWS))


def cell(row, wide):
    return ((row // WLAT) * WIDE + wide) * WIN + (row % WLAT) * LINE


def lines(v):
    return v.reshape(v.shape[0] * WLEV, D)


def cells(v):
    return v.reshape(v.shape[0] // WLEV, WLEV, D)


def padded(pieces, rows):
    have = sum(p.shape[0] for p in pieces)
    return jnp.concatenate(pieces + [jnp.zeros((rows - have, D), F32)], axis=0).astype(BF16)


def ahead_at(row):
    return DIAG_AT + row * LON_ROWS if row < HALF_LAT else LON_AT + (row - HALF_LAT) * LON_ROWS


def behind_at(row):
    return LON_AT + row * LON_ROWS if row < OWN_ROWS else DIAG_AT + (row - OWN_ROWS) * LON_ROWS


def pack_ahead(src, dst):
    for row in range(HALF_LAT):
        at = LAT_AT + row * LAT_ROWS
        dst[at : at + LAT_ROWS, :] = padded([lines(src[row, HALF_LON : HALF_LON + OWN_COLS])], LAT_ROWS)
    for row in range(HALF_LAT + OWN_ROWS):
        at = ahead_at(row)
        dst[at : at + LON_ROWS, :] = padded([lines(src[row, :HALF_LON])], LON_ROWS)


def place_strip(flat, row, strip):
    flat[cell(row, 0) : cell(row, 0) + LINE, :] = strip[:LINE]
    flat[cell(row, 1) : cell(row, 1) + LINE, :] = strip[LINE : 2 * LINE]
    flat[cell(row, 2) : cell(row, 2) + EDGE, :] = strip[2 * LINE : STRIP]


def take_strip(flat, row):
    return [
        flat[cell(row, 0) : cell(row, 0) + LINE, :],
        flat[cell(row, 1) : cell(row, 1) + LINE, :],
        flat[cell(row, 2) : cell(row, 2) + EDGE, :],
    ]


def place_own(src, flat):
    for row in range(OWN_ROWS):
        place_strip(flat, row, lines(src[row + HALF_LAT, HALF_LON : HALF_LON + OWN_COLS]))


def place_halo(got, flat):
    for row in range(HALF_LAT):
        at = LAT_AT + row * LAT_ROWS
        place_strip(flat, OWN_ROWS + row, got[at : at + LAT_ROWS, :].astype(F32))
    for row in range(OWN_ROWS + HALF_LAT):
        at, to = behind_at(row), cell(row, 2) + EDGE
        flat[to : to + EDGE, :] = got[at : at + LON_ROWS, :].astype(F32)[:EDGE]


def pack_back(flat, dst):
    for row in range(HALF_LAT):
        at = LAT_AT + row * LAT_ROWS
        dst[at : at + LAT_ROWS, :] = padded(take_strip(flat, OWN_ROWS + row), LAT_ROWS)
    for row in range(OWN_ROWS + HALF_LAT):
        at, end = behind_at(row), cell(row, 2) + EDGE
        dst[at : at + LON_ROWS, :] = padded([flat[end : end + EDGE, :]], LON_ROWS)


def return_own(flat, out):
    for row in range(OWN_ROWS):
        strip = jnp.concatenate(take_strip(flat, row), axis=0)
        out[row + HALF_LAT, HALF_LON : HALF_LON + OWN_COLS] = cells(strip)


def return_halo(got, out):
    for row in range(HALF_LAT + OWN_ROWS):
        at = ahead_at(row)
        out[row, :HALF_LON] = cells(got[at : at + LON_ROWS, :].astype(F32)[:EDGE])
    for row in range(HALF_LAT):
        at = LAT_AT + row * LAT_ROWS
        out[row, HALF_LON : HALF_LON + OWN_COLS] = cells(got[at : at + LAT_ROWS, :].astype(F32)[:STRIP])


def place_regions(region, flat):
    for row in range(HALF_LAT + OWN_ROWS):
        ids = region[row].astype(F32)
        levels = [jnp.broadcast_to(ids[l : l + 1], (128, ids.shape[1])).T for l in range(WLEV)]
        both = jnp.stack(levels[::-1], axis=1).reshape(ids.shape[1] * WLEV, 128)
        for wide in range(WIDE):
            flat[cell(row, wide) : cell(row, wide) + LINE, :] = both[LINE * wide : LINE * (wide + 1)]


AFTER_CHUNK = ((0,), (1,), (0, 2), (1, 3))
AFTER_PROJ = (4, 0, 2)
AFTER_WINDOW = ((1, 3), (4,), (0, 2), (1, 3), (4,), (0, 2))
AFTER_QKV = (1, 3, 4)
AFTER_INPUT = (5, 6, 7, 0, 2)
AFTER_NORM = (1, 3, 4)


def block_kernel(
    tokens, cotangent, region, wqkv, wproj, win, wout,
    out_ref, done_hbm,
    done_ref, cot_ref, region_ref, x_ref, c_ref, wqkv_ref, wproj_ref, win_ref, wout_ref,
    normed, packed, probs, mixed, mid, nmid, dnm, g_ref,
    halo_out, halo_in, back_out, back_in, load_sem, halo_sem, done_sem, *landings_and_sems,
):
    place = Place()
    *landings, send, recv = landings_and_sems
    got = {name: ref for (name, _), ref in zip(LANDINGS, landings)}
    sums = [Sum(place, u, g_ref, done_ref, got, send, recv) for u in range(len(UNITS))]

    leaving = [
        pltpu.make_async_copy(done_ref.at[one.blocks], done_hbm.at[one.blocks], done_sem.at[one.u]) for one in sums
    ]

    def tick(*blocks):
        for u in blocks:
            sums[u].advance()
            if sums[u].stage == sums[u].last + 1:
                leaving[u].start()

    loads = [
        pltpu.make_async_copy(src, dst, load_sem.at[i])
        for i, (src, dst) in enumerate(
            ((tokens, out_ref), (cotangent, cot_ref), (wqkv, wqkv_ref), (wproj, wproj_ref), (win, win_ref), (wout, wout_ref))
        )
    ]
    for one in loads:
        one.start()

    lat, lon = lax.axis_index("lat"), lax.axis_index("lon")
    lats, lons = lax.axis_size("lat"), lax.axis_size("lon")
    up, down = lax.rem(lat + lats - 1, lats), lax.rem(lat + 1, lats)
    left, right = lax.rem(lon + lons - 1, lons), lax.rem(lon + 1, lons)
    ahead = ((up, lon), (lat, left), (up, left))
    back = ((down, lon), (lat, right), (down, right))
    greet(place, ahead + back)

    def exchange(src, dst, targets, at):
        copies = []
        for i, (lo, hi) in enumerate(HALO_PARTS):
            one = pltpu.make_async_remote_copy(
                src_ref=src.at[lo:hi], dst_ref=dst.at[lo:hi],
                send_sem=halo_sem.at[0, at + i], recv_sem=halo_sem.at[1, at + i],
                device_id=targets[i], device_id_type=pl.DeviceIdType.MESH,
            )
            one.start()
            copies.append(one)
        return copies

    loads[0].wait()
    pack_ahead(out_ref, halo_out.at[0])
    token_halo = exchange(halo_out.at[0], halo_in.at[0], ahead, 0)
    place_own(out_ref, x_ref)
    place_regions(region, region_ref)

    rows_of = lambda w: pl.ds(pl.multiple_of(w * WIN, WIN), WIN)
    few_of = lambda i: pl.ds(pl.multiple_of(i * FEW, FEW), FEW)
    fews = WIN // FEW

    def attention_forward(first, last):
        @pl.loop(first * fews, last * fews)
        def _(i):
            unit, _ = norm_parts(x_ref[few_of(i), :])
            normed[few_of(i), :] = unit.astype(BF16)

        if first == 0:
            loads[2].wait()
        rows = slice(first * WIN, last * WIN)
        for j in range(3):
            cols = slice(D * j, D * (j + 1))
            packed[rows, cols] = nn(normed[rows, :], wqkv_ref[:, cols]).astype(BF16)

        @pl.loop(first, last)
        def _(w):
            rows = rows_of(w)
            ids = region_ref[rows, :]
            allowed = ids[:, :1] == jnp.concatenate([ids.T[:1]] * GROUP, axis=1)
            for g in range(GROUPS):
                lo = LANES * g
                q = packed[rows, lo : lo + LANES]
                k = packed[rows, D + lo : D + lo + LANES]
                v = packed[rows, 2 * D + lo : 2 * D + lo + LANES]
                s = jnp.where(allowed, nt(k, spread_heads(q)), MASKED)
                e = jnp.exp2((s - jnp.max(s, axis=0, keepdims=True)) * (SCALE * LOG2E))
                p = (e * (1.0 / jnp.sum(e, axis=0, keepdims=True))).astype(BF16)
                probs[w * GROUPS + g] = p
                mixed[rows, lo : lo + LANES] = own_blocks(nn(v.T, p)).T.astype(BF16)

    attention_forward(0, 2)
    loads[1].wait()
    pack_ahead(cot_ref, halo_out.at[1])
    for one in token_halo:
        one.wait()
    cot_halo = exchange(halo_out.at[1], halo_in.at[1], ahead, 3)
    place_halo(halo_in.at[0], x_ref)
    attention_forward(2, WINDOWS)

    loads[3].wait()
    mid[...] = nn(mixed[...], wproj_ref[...]).astype(BF16).astype(F32)

    @pl.loop(0, WINDOWS * fews)
    def _(i):
        rows = few_of(i)
        middle = x_ref[rows, :] + mid[rows, :]
        mid[rows, :] = middle
        nmid[rows, :] = norm_parts(middle)[0].astype(BF16)

    place_own(cot_ref, c_ref)
    for one in cot_halo:
        one.wait()
    place_halo(halo_in.at[1], c_ref)
    loads[4].wait()
    loads[5].wait()

    nmid_t = nmid[...].T
    for j in range(FFN // D):
        cols = slice(D * j, D * (j + 1))
        cot = c_ref[...].astype(BF16)
        u = nn(nmid[...], win_ref[:, cols])
        da = nt(cot, wout_ref[cols, :])
        square = u * u
        t = jnp.tanh(u * (GELU_A + (GELU_A * GELU_B) * square))
        half = 0.5 + 0.5 * t
        act = (u * half).astype(BF16)
        slope = half + u * (0.5 - 0.5 * t * t) * (GELU_A + (3 * GELU_A * GELU_B) * square)
        dpre = (slope * da).astype(BF16)
        g_ref[OUT_BLOCKS[j]] = nn(act.T, cot).astype(BF16).reshape(SPLIT)
        g_ref[IN_BLOCKS[j]] = nn(nmid_t, dpre).astype(BF16).reshape(SPLIT)
        part = nt(dpre, win_ref[:, cols])
        if j == 0:
            dnm[...] = part
        else:
            dnm[...] += part
        tick(*AFTER_CHUNK[j])

    @pl.loop(0, WINDOWS * fews)
    def _(i):
        rows = few_of(i)
        unit, r = norm_parts(mid[rows, :])
        d_mid = c_ref[rows, :] + norm_back(unit, r, dnm[rows, :])
        c_ref[rows, :] = d_mid
        nmid[rows, :] = d_mid.astype(BF16)

    g_ref[PROJ_BLOCK] = nn(mixed[...].T, nmid[...]).astype(BF16).reshape(SPLIT)
    tick(*AFTER_PROJ)
    mixed[...] = nt(nmid[...], wproj_ref[...]).astype(BF16)

    for w in range(WINDOWS):

        @pl.loop(w, w + 1)
        def _(w):
            rows = rows_of(w)
            for g in range(GROUPS):
                lo = LANES * g
                q = spread_heads(packed[rows, lo : lo + LANES])
                k = packed[rows, D + lo : D + lo + LANES]
                v = packed[rows, 2 * D + lo : 2 * D + lo + LANES]
                do = spread_heads(mixed[rows, lo : lo + LANES])
                p = probs[w * GROUPS + g]
                dp = nt(v, do)
                pf = p.astype(F32)
                total = jnp.sum(dp * pf, axis=0, keepdims=True)
                ds = (pf * (dp - total) * SCALE).astype(BF16)
                packed[rows, lo : lo + LANES] = own_blocks(nn(k.T, ds)).T.astype(BF16)
                packed[rows, D + lo : D + lo + LANES] = nn(ds, q).astype(BF16)
                packed[rows, 2 * D + lo : 2 * D + lo + LANES] = nn(p, do).astype(BF16)

        tick(*AFTER_WINDOW[w])

    normed_t = normed[...].T
    for j in range(3):
        g_ref[QKV_BLOCKS[j]] = nn(normed_t, packed[:, D * j : D * (j + 1)]).astype(BF16).reshape(SPLIT)
        tick(QKV_UNITS[j])
    tick(*AFTER_QKV)
    for j in range(3):
        cols = slice(D * j, D * (j + 1))
        part = nt(packed[:, cols], wqkv_ref[:, cols])
        if j == 0:
            dnm[...] = part
        else:
            dnm[...] += part
    tick(*AFTER_INPUT)

    @pl.loop(0, WINDOWS * fews)
    def _(i):
        rows = few_of(i)
        unit, r = norm_parts(x_ref[rows, :])
        c_ref[rows, :] = c_ref[rows, :] + norm_back(unit, r, dnm[rows, :])

    tick(*AFTER_NORM)
    pack_back(c_ref, back_out)
    grad_halo = exchange(back_out, back_in, back, 6)
    return_own(c_ref, out_ref)

    rounds = 0
    while any(one.stage <= one.last for one in sums):
        tick(*(u for u in (*QKV_UNITS, 0, 1, 2, 3, 4) if sums[u].stage <= sums[u].last))
        rounds += 1
        if rounds == 2:
            for one in grad_halo:
                one.wait()
            return_halo(back_in, out_ref)
    for one in leaving:
        one.wait()


def block_call(tokens, cotangent, region, w_qkv, w_proj, w_in, w_out):
    anywhere, vmem = pl.BlockSpec(memory_space=pl.ANY), pl.BlockSpec(memory_space=pltpu.VMEM)
    count = WINDOWS * WIN
    return pl.pallas_call(
        block_kernel,
        out_shape=(jax.ShapeDtypeStruct(tokens.shape, F32), jax.ShapeDtypeStruct((BLOCKS, *SPLIT), BF16)),
        in_specs=[anywhere, anywhere, vmem] + [anywhere] * 4,
        out_specs=(vmem, anywhere),
        scratch_shapes=[
            pltpu.VMEM((BLOCKS, *SPLIT), BF16),
            pltpu.VMEM(tokens.shape, F32),
            pltpu.VMEM((count, 128), F32),
            pltpu.VMEM((count, D), F32),
            pltpu.VMEM((count, D), F32),
            pltpu.VMEM(w_qkv.shape, BF16),
            pltpu.VMEM(w_proj.shape, BF16),
            pltpu.VMEM(w_in.shape, BF16),
            pltpu.VMEM(w_out.shape, BF16),
            pltpu.VMEM((count, D), BF16),
            pltpu.VMEM((count, 3 * D), BF16),
            pltpu.VMEM((WINDOWS * GROUPS, WIN, SPREAD), BF16),
            pltpu.VMEM((count, D), BF16),
            pltpu.VMEM((count, D), F32),
            pltpu.VMEM((count, D), BF16),
            pltpu.VMEM((count, D), F32),
            pltpu.VMEM((BLOCKS, *SPLIT), BF16),
            pltpu.VMEM((2, HALO_ROWS, D), BF16),
            pltpu.VMEM((2, HALO_ROWS, D), BF16),
            pltpu.VMEM((HALO_ROWS, D), BF16),
            pltpu.VMEM((HALO_ROWS, D), BF16),
            pltpu.SemaphoreType.DMA((6,)),
            pltpu.SemaphoreType.DMA((2, 9)),
            pltpu.SemaphoreType.DMA((len(UNITS),)),
        ]
        + sum_scratch(),
        compiler_params=pltpu.CompilerParams(
            collective_id=0, has_side_effects=True, vmem_limit_bytes=63 * 1024 * 1024
        ),
        cost_estimate=pl.CostEstimate(flops=16 * 10**9, bytes_accessed=24 * 10**6, transcendentals=4 * 10**6),
        name="block",
    )(tokens, cotangent, region, w_qkv, w_proj, w_in, w_out)


def local(tokens, cotangent, region_ids, w_qkv, w_proj, w_in, w_out):
    grad_tokens, grads = block_call(
        tokens.transpose(1, 2, 0, 3), cotangent.transpose(1, 2, 0, 3), region_ids.transpose(1, 0, 2),
        w_qkv, w_proj, w_in, w_out,
    )
    grad_out, grad_in, grad_qkv, grad_proj, grad_tokens = unpack_call(grads.reshape(BLOCKS, D, D), grad_tokens)
    return grad_tokens.transpose(2, 0, 1, 3), grad_qkv, grad_proj, grad_in, grad_out


def solution(mesh):
    grid = P(None, "lat", "lon", None)
    in_specs = (grid, grid, P(None, "lat", "lon"), P(), P(), P(), P())
    out_specs = (grid, P(), P(), P(), P())
    return jax.shard_map(local, mesh=mesh, in_specs=in_specs, out_specs=out_specs, check_vma=False)
```

```python
import functools

import jax
import jax.numpy as jnp
from jax import lax
from jax.experimental import pallas as pl
from jax.experimental.pallas import tpu as pltpu
from jax.sharding import PartitionSpec as P

D = 512
HEADS = 16
HEAD_DIM = D // HEADS
FFN = 2048
WLEV = 2
WLAT = 6
WLON = 12
WIN = WLEV * WLAT * WLON
GROUP = 8
LANES = GROUP * HEAD_DIM
GROUPS = HEADS // GROUP
SPREAD = GROUP * WIN
HALF_LAT = WLAT // 2
HALF_LON = WLON // 2
EPS = 1e-05
MASKED = -1e10
SCALE = HEAD_DIM ** -0.5
LOG2E = 1.4426950408889634
GELU_A = 0.7978845608028654
GELU_B = 0.044715
F32 = jnp.float32
BF16 = jnp.bfloat16


def nn(a, b):
    return lax.dot_general(a, b, (((1,), (0,)), ((), ())), preferred_element_type=F32)


def nt(a, b):
    return lax.dot_general(a, b, (((1,), (1,)), ((), ())), preferred_element_type=F32)


def norm_parts(v):
    centred = v - jnp.mean(v, axis=-1, keepdims=True)
    r = lax.rsqrt(jnp.mean(centred * centred, axis=-1, keepdims=True) + EPS)
    return centred * r, r


def norm_back(unit, r, g):
    return r * (g - jnp.mean(g, axis=-1, keepdims=True) - unit * jnp.mean(g * unit, axis=-1, keepdims=True))


def spread_heads(v):
    lane_head = lax.broadcasted_iota(jnp.int32, v.shape, 1) // HEAD_DIM
    zero = jnp.zeros_like(v)
    return jnp.concatenate([jnp.where(lane_head == h, v, zero) for h in range(GROUP)], axis=0)


def own_blocks(full):
    return jnp.concatenate(
        [full[HEAD_DIM * h : HEAD_DIM * (h + 1), WIN * h : WIN * (h + 1)] for h in range(GROUP)], axis=0
    )


BLOCKS = 12
OUT_BLOCKS = (0, 2, 4, 6)
IN_BLOCKS = (1, 3, 5, 7)
PROJ_BLOCK = 8
QKV_BLOCKS = (9, 10, 11)
UNITS = (
    (0, 2, "xyz"), (2, 2, "yzx"), (4, 2, "zxy"), (6, 3, "xyz"),
    (9, 1, "xyz"), (10, 1, "yzx"), (11, 1, "zxy"),
)
QKV_UNITS = (4, 5, 6)
PAIRED = 9
SLOTS = 23
SPLIT = (4, 2, D // 8, D)


class Place:
    def __init__(self):
        lat, lon = lax.axis_index("lat"), lax.axis_index("lon")
        self.core = lon % 2
        self.at = {"x": (lon // 2) % 4, "y": (lon // 8) * 2 + lat % 2, "z": lat // 2}

    def mesh_id(self, at, core):
        return (at["z"] * 2 + at["y"] % 2, (at["y"] // 2) * 8 + at["x"] * 2 + core)

    def sibling(self):
        return self.mesh_id(self.at, 1 - self.core)

    def along(self, axis, step):
        at = dict(self.at)
        at[axis] = (at[axis] + step) % 4
        return self.mesh_id(at, self.core), at[axis]

    def across(self, axis, kind):
        at, c = dict(self.at), self.at[axis]
        at[axis] = c + 1 - 2 * (c % 2) if kind == 1 else 3 - c
        bit = ((c + 1) // 2) % 2 if kind == 1 else c // 2
        return self.mesh_id(at, self.core), bit


def greet(place, others=()):
    barrier = pltpu.get_barrier_semaphore()
    partners = [place.sibling()] + [place.along(a, s)[0] for a in "xyz" for s in (1, 2, 3)] + list(others)
    for partner in partners:
        pl.semaphore_signal(barrier, inc=1, device_id=partner, device_id_type=pl.DeviceIdType.MESH)
    pl.semaphore_wait(barrier, len(partners))


class Sum:
    def __init__(self, place, u, g, done, got, send, recv):
        first, count, order = UNITS[u]
        self.u, self.g, self.done, self.send, self.recv = u, g, done, send, recv
        self.blocks = blocks = pl.ds(first, count)
        self.stage, self.slots, self.copies = 0, 0, []
        top, other = place.core * 2, (1 - place.core) * 2
        self.steps = []

        def half(pieces):
            self.steps.append((
                [(out, land, target) for out, keep, land, target in pieces],
                [(keep, [land]) for out, keep, land, target in pieces],
                [(keep, target) for out, keep, land, target in pieces],
            ))

        def quarter(axis, piece, landing):
            peers = [place.along(axis, step) for step in (1, 2, 3)]
            keep = piece(place.at[axis])
            self.steps.append((
                [(piece(c), landing[i], target) for i, (target, c) in enumerate(peers)],
                [(keep, landing)],
                [(keep, target) for target, _ in peers],
            ))

        half([(
            lambda r: r.at[blocks, pl.ds(other, 2)], lambda r: r.at[blocks, pl.ds(top, 2)],
            got["core"].at[blocks], place.sibling(),
        )])
        if count > 1:
            (one, h1), (three, h3) = place.across(order[0], 1), place.across(order[0], 3)
            near, far = got["near"], got["far"]

            def near_one(u):
                return lambda r: r.at[u, top + 1 - h1], lambda r: r.at[u, top + h1], near.at[u], one

            def near_three(u):
                return lambda r: r.at[u, pl.ds(top, 2), 1 - h3], lambda r: r.at[u, pl.ds(top, 2), h3], near.at[u], three

            def far_three(u):
                return lambda r: r.at[u, top + h1, 1 - h3], lambda r: r.at[u, top + h1, h3], far.at[u], three

            def far_one(u):
                return lambda r: r.at[u, top + 1 - h1, h3], lambda r: r.at[u, top + h1, h3], far.at[u], one

            half([(near_three if i == 1 else near_one)(first + i) for i in range(count)])
            half([(far_one if i == 1 else far_three)(first + i) for i in range(count)])
            at1, at3 = top + h1, h3
        else:
            land = [got["axis"].at[i, pl.ds(first - PAIRED, count)] for i in range(3)]
            quarter(order[0], lambda c: lambda r: r.at[blocks, top + c // 2, c % 2], land)
            c = place.at[order[0]]
            at1, at3 = top + c // 2, c % 2

        def small(c):
            return lambda r: r.at[blocks, at1, at3, pl.ds(pl.multiple_of(c * (D // 32), D // 32), D // 32)]

        quarter(order[1], small, [got["second"].at[i, blocks] for i in range(3)])
        peers = [place.along(order[2], step)[0] for step in (1, 2, 3)]
        self.swap = (peers, small(place.at[order[1]]), place.at[order[2]], got["swap"])
        self.last = 2 * len(self.steps) + 1

    def copy(self, src, dst, target):
        slot = self.slots
        self.slots += 1
        one = pltpu.make_async_remote_copy(
            src_ref=src, dst_ref=dst, send_sem=self.send.at[self.u, slot], recv_sem=self.recv.at[self.u, slot],
            device_id=target, device_id_type=pl.DeviceIdType.MESH,
        )
        one.start()
        self.copies.append(one)

    def advance(self):
        n, stage = len(self.steps), self.stage
        self.stage += 1
        for one in self.copies:
            one.wait()
        self.copies = []
        peers, piece, at, slots = self.swap
        if 1 <= stage <= n:
            for keep, landings in self.steps[stage - 1][1]:
                mine = keep(self.g)
                total = mine[...].astype(F32)
                for landing in landings:
                    total = total + landing[...].astype(F32)
                mine[...] = total.astype(BF16)
        if stage == n + 1:
            four = [slots[c, self.blocks].astype(F32) for c in range(4)]
            piece(self.done)[...] = ((four[0] + four[1]) + (four[2] + four[3])).astype(BF16)
        if stage < n:
            for out, landing, target in self.steps[stage][0]:
                self.copy(out(self.g), landing, target)
        elif stage == n:
            mine = piece(self.g)
            slots[at, self.blocks] = mine[...]
            for target in peers:
                self.copy(mine, slots.at[at, self.blocks], target)
        elif stage <= 2 * n:
            for keep, target in self.steps[2 * n - stage][2]:
                self.copy(keep(self.done), keep(self.done), target)


LANDINGS = (
    ("core", (BLOCKS, 2, 2, D // 8, D)),
    ("near", (PAIRED, 2, D // 8, D)),
    ("far", (PAIRED, D // 8, D)),
    ("axis", (3, BLOCKS - PAIRED, D // 8, D)),
    ("second", (3, BLOCKS, D // 32, D)),
    ("swap", (4, BLOCKS, D // 32, D)),
)


def sum_scratch():
    return [pltpu.VMEM(shape, BF16) for _, shape in LANDINGS] + [pltpu.SemaphoreType.DMA((len(UNITS), SLOTS))] * 2


def unpack_kernel(g_ref, tok_ref, out_ref, in_ref, qkv_ref, proj_ref, tok_out, half, full, lines_in, got, put, whole):
    def target(u):
        if u == PROJ_BLOCK:
            return proj_ref
        if u in OUT_BLOCKS:
            return out_ref.at[pl.ds(D * OUT_BLOCKS.index(u), D), :]
        if u in IN_BLOCKS:
            return in_ref.at[:, pl.ds(D * IN_BLOCKS.index(u), D)]
        return qkv_ref.at[:, pl.ds(D * QKV_BLOCKS.index(u), D)]

    ins = [pltpu.make_async_copy(g_ref.at[u], half.at[u], got.at[u]) for u in range(BLOCKS)]
    outs = [pltpu.make_async_copy(full.at[u], target(u), put.at[u]) for u in range(BLOCKS)]
    arrive = pltpu.make_async_copy(tok_ref, lines_in, whole.at[0])
    leave = pltpu.make_async_copy(lines_in, tok_out, whole.at[1])
    arrive.start()
    for one in ins:
        one.start()
    arrive.wait()
    leave.start()
    for u in range(BLOCKS):
        ins[u].wait()
        full[u] = half[u].astype(F32)
        outs[u].start()
    for one in outs:
        one.wait()
    leave.wait()


def unpack_call(grads, grad_tokens):
    anywhere = pl.BlockSpec(memory_space=pl.ANY)
    return pl.pallas_call(
        unpack_kernel,
        out_shape=tuple(jax.ShapeDtypeStruct(s, F32) for s in ((FFN, D), (D, FFN), (D, 3 * D), (D, D), grad_tokens.shape)),
        in_specs=[anywhere] * 2,
        out_specs=(anywhere,) * 5,
        scratch_shapes=[
            pltpu.VMEM((BLOCKS, D, D), BF16),
            pltpu.VMEM((BLOCKS, D, D), F32),
            pltpu.VMEM(grad_tokens.shape, F32),
            pltpu.SemaphoreType.DMA((BLOCKS,)),
            pltpu.SemaphoreType.DMA((BLOCKS,)),
            pltpu.SemaphoreType.DMA((2,)),
        ],
        compiler_params=pltpu.CompilerParams(vmem_limit_bytes=60 * 1024 * 1024),
        name="unpack",
    )(grads, grad_tokens)


LAT_ROWS, LON_ROWS = 64, 16
LAT_AT, LON_AT, DIAG_AT, HALO_ROWS = 0, 192, 336, 384
WINDOWS = 6
FEW = 144
WIDE = 3
OWN_ROWS = 9
OWN_COLS = 30
STRIP = OWN_COLS * WLEV
EDGE = HALF_LON * WLEV
LINE = WLON * WLEV
HALO_PARTS = ((LAT_AT, LON_AT), (LON_AT, DIAG_AT), (DIAG_AT, HALO_ROWS))


def cell(row, wide):
    return ((row // WLAT) * WIDE + wide) * WIN + (row % WLAT) * LINE


def lines(v):
    return v.reshape(v.shape[0] * WLEV, D)


def cells(v):
    return v.reshape(v.shape[0] // WLEV, WLEV, D)


def padded(pieces, rows):
    have = sum(p.shape[0] for p in pieces)
    return jnp.concatenate(pieces + [jnp.zeros((rows - have, D), F32)], axis=0).astype(BF16)


def ahead_at(row):
    return DIAG_AT + row * LON_ROWS if row < HALF_LAT else LON_AT + (row - HALF_LAT) * LON_ROWS


def behind_at(row):
    return LON_AT + row * LON_ROWS if row < OWN_ROWS else DIAG_AT + (row - OWN_ROWS) * LON_ROWS


def pack_ahead(src, dst):
    for row in range(HALF_LAT):
        at = LAT_AT + row * LAT_ROWS
        dst[at : at + LAT_ROWS, :] = padded([lines(src[row, HALF_LON : HALF_LON + OWN_COLS])], LAT_ROWS)
    for row in range(HALF_LAT + OWN_ROWS):
        at = ahead_at(row)
        dst[at : at + LON_ROWS, :] = padded([lines(src[row, :HALF_LON])], LON_ROWS)


def place_strip(flat, row, strip):
    flat[cell(row, 0) : cell(row, 0) + LINE, :] = strip[:LINE]
    flat[cell(row, 1) : cell(row, 1) + LINE, :] = strip[LINE : 2 * LINE]
    flat[cell(row, 2) : cell(row, 2) + EDGE, :] = strip[2 * LINE : STRIP]


def take_strip(flat, row):
    return [
        flat[cell(row, 0) : cell(row, 0) + LINE, :],
        flat[cell(row, 1) : cell(row, 1) + LINE, :],
        flat[cell(row, 2) : cell(row, 2) + EDGE, :],
    ]


def place_own(src, flat):
    for row in range(OWN_ROWS):
        place_strip(flat, row, lines(src[row + HALF_LAT, HALF_LON : HALF_LON + OWN_COLS]))


def place_halo(got, flat):
    for row in range(HALF_LAT):
        at = LAT_AT + row * LAT_ROWS
        place_strip(flat, OWN_ROWS + row, got[at : at + LAT_ROWS, :].astype(F32))
    for row in range(OWN_ROWS + HALF_LAT):
        at, to = behind_at(row), cell(row, 2) + EDGE
        flat[to : to + EDGE, :] = got[at : at + LON_ROWS, :].astype(F32)[:EDGE]


def pack_back(flat, dst):
    for row in range(HALF_LAT):
        at = LAT_AT + row * LAT_ROWS
        dst[at : at + LAT_ROWS, :] = padded(take_strip(flat, OWN_ROWS + row), LAT_ROWS)
    for row in range(OWN_ROWS + HALF_LAT):
        at, end = behind_at(row), cell(row, 2) + EDGE
        dst[at : at + LON_ROWS, :] = padded([flat[end : end + EDGE, :]], LON_ROWS)


def return_own(flat, out):
    for row in range(OWN_ROWS):
        strip = jnp.concatenate(take_strip(flat, row), axis=0)
        out[row + HALF_LAT, HALF_LON : HALF_LON + OWN_COLS] = cells(strip)


def return_halo(got, out):
    for row in range(HALF_LAT + OWN_ROWS):
        at = ahead_at(row)
        out[row, :HALF_LON] = cells(got[at : at + LON_ROWS, :].astype(F32)[:EDGE])
    for row in range(HALF_LAT):
        at = LAT_AT + row * LAT_ROWS
        out[row, HALF_LON : HALF_LON + OWN_COLS] = cells(got[at : at + LAT_ROWS, :].astype(F32)[:STRIP])


def place_regions(region, flat):
    for row in range(HALF_LAT + OWN_ROWS):
        ids = region[row].astype(F32)
        levels = [jnp.broadcast_to(ids[l : l + 1], (128, ids.shape[1])).T for l in range(WLEV)]
        both = jnp.stack(levels[::-1], axis=1).reshape(ids.shape[1] * WLEV, 128)
        for wide in range(WIDE):
            flat[cell(row, wide) : cell(row, wide) + LINE, :] = both[LINE * wide : LINE * (wide + 1)]


AFTER_CHUNK = ((0,), (1,), (0, 2), (1,))
AFTER_PROJ = (3, 0, 2)
AFTER_WINDOW = ((1,), (3,), (0, 2), (1,), (3,), (0, 2))
AFTER_QKV = (1, 3)
AFTER_INPUT = (4, 5, 6, 0, 2)
AFTER_NORM = (1, 3)


def block_kernel(
    tokens, cotangent, region, wqkv, wproj, win, wout,
    out_ref, done_hbm,
    done_ref, cot_ref, region_ref, x_ref, c_ref, wqkv_ref, wproj_ref, win_ref, wout_ref,
    normed, packed, probs, mixed, mid, nmid, dnm, g_ref,
    halo_out, halo_in, back_out, back_in, load_sem, halo_sem, done_sem, *landings_and_sems,
):
    place = Place()
    *landings, send, recv = landings_and_sems
    got = {name: ref for (name, _), ref in zip(LANDINGS, landings)}
    sums = [Sum(place, u, g_ref, done_ref, got, send, recv) for u in range(len(UNITS))]

    leaving = [
        pltpu.make_async_copy(done_ref.at[one.blocks], done_hbm.at[one.blocks], done_sem.at[one.u]) for one in sums
    ]

    def tick(*blocks):
        for u in blocks:
            sums[u].advance()
            if sums[u].stage == sums[u].last + 1:
                leaving[u].start()

    loads = [
        pltpu.make_async_copy(src, dst, load_sem.at[i])
        for i, (src, dst) in enumerate(
            ((tokens, out_ref), (cotangent, cot_ref), (wqkv, wqkv_ref), (wproj, wproj_ref), (win, win_ref), (wout, wout_ref))
        )
    ]
    for one in loads:
        one.start()

    lat, lon = lax.axis_index("lat"), lax.axis_index("lon")
    lats, lons = lax.axis_size("lat"), lax.axis_size("lon")
    up, down = lax.rem(lat + lats - 1, lats), lax.rem(lat + 1, lats)
    left, right = lax.rem(lon + lons - 1, lons), lax.rem(lon + 1, lons)
    ahead = ((up, lon), (lat, left), (up, left))
    back = ((down, lon), (lat, right), (down, right))
    greet(place, ahead + back)

    def exchange(src, dst, targets, at):
        copies = []
        for i, (lo, hi) in enumerate(HALO_PARTS):
            one = pltpu.make_async_remote_copy(
                src_ref=src.at[lo:hi], dst_ref=dst.at[lo:hi],
                send_sem=halo_sem.at[0, at + i], recv_sem=halo_sem.at[1, at + i],
                device_id=targets[i], device_id_type=pl.DeviceIdType.MESH,
            )
            one.start()
            copies.append(one)
        return copies

    loads[0].wait()
    pack_ahead(out_ref, halo_out.at[0])
    token_halo = exchange(halo_out.at[0], halo_in.at[0], ahead, 0)
    place_own(out_ref, x_ref)
    place_regions(region, region_ref)

    rows_of = lambda w: pl.ds(pl.multiple_of(w * WIN, WIN), WIN)
    few_of = lambda i: pl.ds(pl.multiple_of(i * FEW, FEW), FEW)
    fews = WIN // FEW

    def attention_forward(first, last):
        @pl.loop(first * fews, last * fews)
        def _(i):
            unit, _ = norm_parts(x_ref[few_of(i), :])
            normed[few_of(i), :] = unit.astype(BF16)

        if first == 0:
            loads[2].wait()
        rows = slice(first * WIN, last * WIN)
        for j in range(3):
            cols = slice(D * j, D * (j + 1))
            packed[rows, cols] = nn(normed[rows, :], wqkv_ref[:, cols]).astype(BF16)

        @pl.loop(first, last)
        def _(w):
            rows = rows_of(w)
            ids = region_ref[rows, :]
            allowed = ids[:, :1] == jnp.concatenate([ids.T[:1]] * GROUP, axis=1)
            for g in range(GROUPS):
                lo = LANES * g
                q = packed[rows, lo : lo + LANES]
                k = packed[rows, D + lo : D + lo + LANES]
                v = packed[rows, 2 * D + lo : 2 * D + lo + LANES]
                s = jnp.where(allowed, nt(k, spread_heads(q)), MASKED)
                e = jnp.exp2((s - jnp.max(s, axis=0, keepdims=True)) * (SCALE * LOG2E))
                p = (e * (1.0 / jnp.sum(e, axis=0, keepdims=True))).astype(BF16)
                probs[w * GROUPS + g] = p
                mixed[rows, lo : lo + LANES] = own_blocks(nn(v.T, p)).T.astype(BF16)

    attention_forward(0, 2)
    loads[1].wait()
    pack_ahead(cot_ref, halo_out.at[1])
    for one in token_halo:
        one.wait()
    cot_halo = exchange(halo_out.at[1], halo_in.at[1], ahead, 3)
    place_halo(halo_in.at[0], x_ref)
    attention_forward(2, WINDOWS)

    loads[3].wait()
    mid[...] = nn(mixed[...], wproj_ref[...]).astype(BF16).astype(F32)

    @pl.loop(0, WINDOWS * fews)
    def _(i):
        rows = few_of(i)
        middle = x_ref[rows, :] + mid[rows, :]
        mid[rows, :] = middle
        nmid[rows, :] = norm_parts(middle)[0].astype(BF16)

    place_own(cot_ref, c_ref)
    for one in cot_halo:
        one.wait()
    place_halo(halo_in.at[1], c_ref)
    loads[4].wait()
    loads[5].wait()

    nmid_t = nmid[...].T
    for j in range(FFN // D):
        cols = slice(D * j, D * (j + 1))
        cot = c_ref[...].astype(BF16)
        u = nn(nmid[...], win_ref[:, cols])
        da = nt(cot, wout_ref[cols, :])
        square = u * u
        t = jnp.tanh(u * (GELU_A + (GELU_A * GELU_B) * square))
        half = 0.5 + 0.5 * t
        act = (u * half).astype(BF16)
        slope = half + u * (0.5 - 0.5 * t * t) * (GELU_A + (3 * GELU_A * GELU_B) * square)
        dpre = (slope * da).astype(BF16)
        g_ref[OUT_BLOCKS[j]] = nn(act.T, cot).astype(BF16).reshape(SPLIT)
        g_ref[IN_BLOCKS[j]] = nn(nmid_t, dpre).astype(BF16).reshape(SPLIT)
        part = nt(dpre, win_ref[:, cols])
        if j == 0:
            dnm[...] = part
        else:
            dnm[...] += part
        tick(*AFTER_CHUNK[j])

    @pl.loop(0, WINDOWS * fews)
    def _(i):
        rows = few_of(i)
        unit, r = norm_parts(mid[rows, :])
        d_mid = c_ref[rows, :] + norm_back(unit, r, dnm[rows, :])
        c_ref[rows, :] = d_mid
        nmid[rows, :] = d_mid.astype(BF16)

    g_ref[PROJ_BLOCK] = nn(mixed[...].T, nmid[...]).astype(BF16).reshape(SPLIT)
    tick(*AFTER_PROJ)
    mixed[...] = nt(nmid[...], wproj_ref[...]).astype(BF16)

    for w in range(WINDOWS):

        @pl.loop(w, w + 1)
        def _(w):
            rows = rows_of(w)
            for g in range(GROUPS):
                lo = LANES * g
                q = spread_heads(packed[rows, lo : lo + LANES])
                k = packed[rows, D + lo : D + lo + LANES]
                v = packed[rows, 2 * D + lo : 2 * D + lo + LANES]
                do = spread_heads(mixed[rows, lo : lo + LANES])
                p = probs[w * GROUPS + g]
                dp = nt(v, do)
                pf = p.astype(F32)
                total = jnp.sum(dp * pf, axis=0, keepdims=True)
                ds = (pf * (dp - total) * SCALE).astype(BF16)
                packed[rows, lo : lo + LANES] = own_blocks(nn(k.T, ds)).T.astype(BF16)
                packed[rows, D + lo : D + lo + LANES] = nn(ds, q).astype(BF16)
                packed[rows, 2 * D + lo : 2 * D + lo + LANES] = nn(p, do).astype(BF16)

        tick(*AFTER_WINDOW[w])

    normed_t = normed[...].T
    for j in range(3):
        g_ref[QKV_BLOCKS[j]] = nn(normed_t, packed[:, D * j : D * (j + 1)]).astype(BF16).reshape(SPLIT)
        tick(QKV_UNITS[j])
    tick(*AFTER_QKV)
    for j in range(3):
        cols = slice(D * j, D * (j + 1))
        part = nt(packed[:, cols], wqkv_ref[:, cols])
        if j == 0:
            dnm[...] = part
        else:
            dnm[...] += part
    tick(*AFTER_INPUT)

    @pl.loop(0, WINDOWS * fews)
    def _(i):
        rows = few_of(i)
        unit, r = norm_parts(x_ref[rows, :])
        c_ref[rows, :] = c_ref[rows, :] + norm_back(unit, r, dnm[rows, :])

    tick(*AFTER_NORM)
    pack_back(c_ref, back_out)
    grad_halo = exchange(back_out, back_in, back, 6)
    return_own(c_ref, out_ref)

    rounds = 0
    while any(one.stage <= one.last for one in sums):
        tick(*(u for u in (*QKV_UNITS, 0, 1, 2, 3) if sums[u].stage <= sums[u].last))
        rounds += 1
        if rounds == 2:
            for one in grad_halo:
                one.wait()
            return_halo(back_in, out_ref)
    for one in leaving:
        one.wait()


def block_call(tokens, cotangent, region, w_qkv, w_proj, w_in, w_out):
    anywhere, vmem = pl.BlockSpec(memory_space=pl.ANY), pl.BlockSpec(memory_space=pltpu.VMEM)
    count = WINDOWS * WIN
    return pl.pallas_call(
        block_kernel,
        out_shape=(jax.ShapeDtypeStruct(tokens.shape, F32), jax.ShapeDtypeStruct((BLOCKS, *SPLIT), BF16)),
        in_specs=[anywhere, anywhere, vmem] + [anywhere] * 4,
        out_specs=(vmem, anywhere),
        scratch_shapes=[
            pltpu.VMEM((BLOCKS, *SPLIT), BF16),
            pltpu.VMEM(tokens.shape, F32),
            pltpu.VMEM((count, 128), F32),
            pltpu.VMEM((count, D), F32),
            pltpu.VMEM((count, D), F32),
            pltpu.VMEM(w_qkv.shape, BF16),
            pltpu.VMEM(w_proj.shape, BF16),
            pltpu.VMEM(w_in.shape, BF16),
            pltpu.VMEM(w_out.shape, BF16),
            pltpu.VMEM((count, D), BF16),
            pltpu.VMEM((count, 3 * D), BF16),
            pltpu.VMEM((WINDOWS * GROUPS, WIN, SPREAD), BF16),
            pltpu.VMEM((count, D), BF16),
            pltpu.VMEM((count, D), F32),
            pltpu.VMEM((count, D), BF16),
            pltpu.VMEM((count, D), F32),
            pltpu.VMEM((BLOCKS, *SPLIT), BF16),
            pltpu.VMEM((2, HALO_ROWS, D), BF16),
            pltpu.VMEM((2, HALO_ROWS, D), BF16),
            pltpu.VMEM((HALO_ROWS, D), BF16),
            pltpu.VMEM((HALO_ROWS, D), BF16),
            pltpu.SemaphoreType.DMA((6,)),
            pltpu.SemaphoreType.DMA((2, 9)),
            pltpu.SemaphoreType.DMA((len(UNITS),)),
        ]
        + sum_scratch(),
        compiler_params=pltpu.CompilerParams(
            collective_id=0, has_side_effects=True, vmem_limit_bytes=63 * 1024 * 1024
        ),
        cost_estimate=pl.CostEstimate(flops=16 * 10**9, bytes_accessed=24 * 10**6, transcendentals=4 * 10**6),
        name="block",
    )(tokens, cotangent, region, w_qkv, w_proj, w_in, w_out)


def local(tokens, cotangent, region_ids, w_qkv, w_proj, w_in, w_out):
    grad_tokens, grads = block_call(
        tokens.transpose(1, 2, 0, 3), cotangent.transpose(1, 2, 0, 3), region_ids.transpose(1, 0, 2),
        w_qkv, w_proj, w_in, w_out,
    )
    grad_out, grad_in, grad_qkv, grad_proj, grad_tokens = unpack_call(grads.reshape(BLOCKS, D, D), grad_tokens)
    return grad_tokens.transpose(2, 0, 1, 3), grad_qkv, grad_proj, grad_in, grad_out


def solution(mesh):
    grid = P(None, "lat", "lon", None)
    in_specs = (grid, grid, P(None, "lat", "lon"), P(), P(), P(), P())
    out_specs = (grid, P(), P(), P(), P())
    return jax.shard_map(local, mesh=mesh, in_specs=in_specs, out_specs=out_specs, check_vma=False)
```
